256 devices in a mesh: modes: 8 (over z_lo, y), space: 32 (over z_hi, x, core).
Axes of the slice: x: 4, y: 4, z: 8 (z_hi: 4, z_lo: 2; z = z_hi * 2 + z_lo), core: 2. Of those that a mesh axis runs over, the one named last changes fastest.
Arguments:
- pressure: float32 [120, 64, 32, 128], P('modes', 'space'), may hold values from -6 to 6
- source: float32 [120, 64, 32, 128], P('modes', 'space'), may hold values from -12 to 12
- perm_modes: float32 [8, 64, 32, 128], P(None, 'space'), may hold values from -3.4 to 3.4, as said below
- triples: int32 [3, 2880], replicated, may hold values from 0 to 119, as said below
- coeffs: float32 [2880], replicated, may hold values from -0.6 to 2, as said below
Outputs:
- applied: float32 [120, 64, 32, 128], P('modes', 'space')
- relaxed: float32 [120, 64, 32, 128], P('modes', 'space')
The draws below stay inside these ranges and needn't reach their ends.
Inputs may be any that keep to these rules, and one draw needn't show every extreme that they name: `triples`: for each mode i and each k < 8 there are 3 entries with that i and k, in random order; exactly one entry per i has j equal to i, and it has k = 0; k is below 8. `coeffs`: the entry with j equal to i has a coefficient of 0.5 or more. `perm_modes`: the first field is 0.3 or more in every cell.
All inputs are finite; a program needn't handle non-finite values.
Results may differ from the reference program's by a relative error of at most 0.00011.
Values sent between devices are 32-bit elements; how exact they have to be, the bound alone decides.
A program may use at most 128 MiB of HBM per device.

```python
import jax
import jax.numpy as jnp
from jax import lax

P_SIZE = 120
KA = 8
NNZ = 3
NY = 32
NW = 128
NX = 64
NT = 2880


def table_layout(key):
    base = jax.random.fold_in(key, 11)
    key_offset, key_order = jax.random.split(base)
    mode_i = jnp.broadcast_to(jnp.arange(P_SIZE, dtype=jnp.int32)[:, None, None], (P_SIZE, KA, NNZ))
    mode_k = jnp.broadcast_to(jnp.arange(KA, dtype=jnp.int32)[None, :, None], (P_SIZE, KA, NNZ))
    slot_ids = jnp.broadcast_to(jnp.arange(NNZ, dtype=jnp.int32)[None, None, :], (P_SIZE, KA, NNZ))
    offsets = jax.random.randint(key_offset, (P_SIZE, KA, NNZ), 1, P_SIZE)
    mode_j = (mode_i + offsets) % P_SIZE
    on_diag = (mode_k == 0) & (slot_ids == 0)
    mode_j = jnp.where(on_diag, mode_i, mode_j)
    order = jax.random.permutation(key_order, NT)
    return (mode_i.reshape(-1)[order], mode_j.reshape(-1)[order], mode_k.reshape(-1)[order], on_diag.reshape(-1)[order])


def draw_triples(key, part):
    mode_i, mode_j, mode_k, on_diag = table_layout(key)
    return jnp.stack([mode_i, mode_j, mode_k]).astype(jnp.int32)


def draw_coeffs(key, part):
    mode_i, mode_j, mode_k, on_diag = table_layout(key)
    key = jax.random.fold_in(key, 5)
    key_diag, key_off = jax.random.split(key, 2)
    diag_part = 0.5 * 4.0 ** jax.random.uniform(key_diag, (NT,), jnp.float32)
    off_part = jax.random.uniform(key_off, (NT,), jnp.float32, -0.5, 0.5)
    return jnp.where(on_diag, diag_part, off_part).astype(jnp.float32)


def draw_perm_modes(key, part):
    key = jax.random.fold_in(key, 3)
    key_mean, key_rest = jax.random.split(key)
    mean_field = jnp.exp(jax.random.uniform(key_mean, (NX, NY, NW), jnp.float32, -1.2, 1.2))
    rest = mean_field[None] * 0.3 * jnp.clip(jax.random.normal(key_rest, (KA - 1, NX, NY, NW), jnp.float32), -3.0, 3.0)
    return jnp.concatenate([mean_field[None], rest], axis=0).astype(jnp.float32)


def shard_levels(rng, extent, shards, least, largest):
    gain, own = 1.0, jax.random.fold_in(rng, 6)
    for axis_at, parts in shards:
        steps = jnp.exp(jax.random.uniform(jax.random.fold_in(own, axis_at), (parts,), jnp.float32, least / len(shards), largest / len(shards)))
        gain = gain * jnp.repeat(steps, extent[axis_at] // parts).reshape([-1 if axis == axis_at else 1 for axis in range(len(extent))])
    return gain


def bell_draw(key, extent, deviation, most, pieces=(), held_as=jnp.bfloat16):
    entries = jax.random.normal(key, extent, jnp.float32) * deviation
    if len(pieces) > 0:
        entries = shard_levels(key, extent, pieces, -0.22, 0.18) * entries
    return jnp.clip(entries, min=-most, max=most).astype(held_as)


def setup_inputs(seed: int = 0) -> dict:
    seeds = jax.random.split(jax.random.key(seed), 6)
    return {
        "pressure": bell_draw(seeds[0], (P_SIZE, NX, NY, NW), 1.0, 6.0, ((0, 8), (1, 32)), jnp.float32),
        "source": bell_draw(seeds[1], (P_SIZE, NX, NY, NW), 2.0, 12.0, ((0, 8), (1, 32)), jnp.float32),
        "perm_modes": draw_perm_modes(jax.random.fold_in(seeds[5], 71), 0),
        "triples": draw_triples(jax.random.fold_in(seeds[5], 71), 0),
        "coeffs": draw_coeffs(jax.random.fold_in(seeds[5], 71), 0),
    }


relax_weight = 0.8


def coupling_table(triples, coeffs):
    mode_ids = jnp.arange(P_SIZE, dtype=jnp.int32)
    pair_ids = jnp.arange(P_SIZE * KA, dtype=jnp.int32)
    pair_col = triples[1] * KA + triples[2]
    left_hot = (triples[0][:, None] == mode_ids[None, :]).astype(jnp.float32)
    right_hot = (pair_col[:, None] == pair_ids[None, :]).astype(jnp.float32) * coeffs[:, None]
    return jnp.dot(left_hot.T, right_hot, precision=lax.Precision.HIGHEST)


def neighbours(padded):
    middle = padded[..., 1:-1, 1:-1, 1:-1]
    sides = [padded[..., 2:, 1:-1, 1:-1], padded[..., :-2, 1:-1, 1:-1],
             padded[..., 1:-1, 2:, 1:-1], padded[..., 1:-1, :-2, 1:-1],
             padded[..., 1:-1, 1:-1, 2:], padded[..., 1:-1, 1:-1, :-2]]
    return middle, sides


def apply_fields(perm_ext, field_ext):
    perm_mid, perm_sides = neighbours(perm_ext)
    field_mid, field_sides = neighbours(field_ext)
    running = 0.0
    for perm_side, field_side in zip(perm_sides, field_sides):
        running = running + 0.5 * (perm_mid + perm_side) * (field_mid - field_side)
    return running


def diag_fields(perm_ext):
    perm_mid, perm_sides = neighbours(perm_ext)
    running = 0.0
    for perm_side in perm_sides:
        running = running + 0.5 * (perm_mid + perm_side)
    return running


def pad_all(field):
    return jnp.pad(field, ((0, 0), (1, 1), (1, 1), (1, 1)))


def reference(pressure, source, perm_modes, triples, coeffs):
    coupling_full = coupling_table(triples, coeffs).reshape(P_SIZE, P_SIZE, KA)
    perm_ext = pad_all(perm_modes)
    flat_field = pressure.reshape(P_SIZE, -1)

    def mode_apply(mode_row):
        coupled = jnp.dot(mode_row.T, flat_field, precision=lax.Precision.HIGHEST)
        coupled = coupled.reshape(KA, NX, NY, NW)
        return jnp.sum(apply_fields(perm_ext, pad_all(coupled)), axis=0)

    applied = lax.map(mode_apply, coupling_full)
    mode_ids = jnp.arange(P_SIZE, dtype=jnp.int32)
    diag_rows = coupling_full[mode_ids, mode_ids]
    diag_field = diag_fields(perm_ext).reshape(KA, -1)
    scale = jnp.dot(diag_rows, diag_field, precision=lax.Precision.HIGHEST).reshape(P_SIZE, NX, NY, NW)
    relaxed = pressure + relax_weight * (source - applied) / scale
    return applied, relaxed
```

```python
import functools

import jax
import jax.numpy as jnp
from jax import lax
from jax.experimental import pallas as pl
from jax.experimental.pallas import tpu as pltpu
from jax.sharding import PartitionSpec as P

KA = 8
GROUPS = 8
LOCAL = 15
PAD = 16
LAYERS = 2
ROWS = 32
LANES = 128
OWN = ROWS // GROUPS
ENTRIES = 2880
WIDE = GROUPS * PAD
relax_weight = 0.8

MESH = pl.DeviceIdType.MESH
F32 = jnp.float32
BF16 = jnp.bfloat16


def kernel(
    space_count,
    p_hbm,
    s_hbm,
    a_hbm,
    tri_hbm,
    cf_hbm,
    out_a_hbm,
    out_r_hbm,
    p_v,
    s_v,
    a_v,
    tri_v,
    cf_v,
    t,
    q,
    r_out,
    ret,
    w_mat,
    a_hot,
    m_buf,
    w_f,
    dg,
    cdb,
    inv_v,
    base_v,
    oa_v,
    or_v,
    in_sem,
    out_sem,
    a2a_send,
    a2a_recv,
    low_send,
    low_recv,
    high_send,
    high_recv,
    perm_send,
    perm_recv,
    ret_send,
    ret_recv,
):
    m = lax.axis_index("modes")
    s = lax.axis_index("space")
    s_up = lax.rem(s + 1, space_count)
    s_dn = lax.rem(s + space_count - 1, space_count)

    def peer_to(d):
        return lax.rem(m + d, GROUPS)

    def peer_from(d):
        return lax.rem(m + GROUPS - d, GROUPS)

    def mode_rows(g):
        return pl.ds(pl.multiple_of(g * PAD, PAD), PAD)

    barrier = pltpu.get_barrier_semaphore()
    for d in range(1, GROUPS):
        pl.semaphore_signal(barrier, inc=1, device_id=(peer_to(d), s), device_id_type=MESH)
    for side in (s_up, s_dn):
        pl.semaphore_signal(barrier, inc=1, device_id=(m, side), device_id_type=MESH)

    load_p = pltpu.make_async_copy(p_hbm, p_v.at[0 : LOCAL * 64], in_sem.at[0])
    load_a = pltpu.make_async_copy(a_hbm, a_v.at[:, 1:3], in_sem.at[1])
    load_t = pltpu.make_async_copy(tri_hbm, tri_v, in_sem.at[2])
    load_c = pltpu.make_async_copy(cf_hbm, cf_v, in_sem.at[3])
    load_s = pltpu.make_async_copy(s_hbm, s_v, in_sem.at[4])
    for load in (load_p, load_a, load_t, load_c, load_s):
        load.start()

    p_v[LOCAL * 64 :, :] = jnp.zeros((64, LANES), F32)
    t[:, 0] = jnp.zeros((LAYERS, PAD, LANES), F32)
    t[:, ROWS + 1] = jnp.zeros((LAYERS, PAD, LANES), F32)
    r_out[...] = jnp.zeros(r_out.shape, F32)
    load_p.wait()

    def stage(row, carry):
        for layer in range(LAYERS):
            for half in range(2):
                start = half * 8 * 64 + layer * ROWS + row
                t[layer, row + 1, half * 8 : half * 8 + 8, :] = p_v[pl.ds(start, 8, stride=64), :]
        return carry

    lax.fori_loop(0, ROWS, stage, 0)
    q[1:3, :, mode_rows(m), :] = t[:, pl.ds(m * OWN, OWN + 2), :, :]

    def send_block(d):
        g = peer_to(d)
        return pltpu.make_async_remote_copy(
            src_ref=t.at[:, pl.ds(g * OWN, OWN + 2)],
            dst_ref=q.at[1:3, :, mode_rows(m), :],
            send_sem=a2a_send.at[d],
            recv_sem=a2a_recv.at[d],
            device_id=(g, s),
            device_id_type=MESH,
        )

    def halo(d, up):
        rows = mode_rows(peer_from(d))
        sems = (high_send, high_recv) if up else (low_send, low_recv)
        return pltpu.make_async_remote_copy(
            src_ref=q.at[2 if up else 1, 1 : OWN + 1, rows, :],
            dst_ref=q.at[0 if up else 3, 1 : OWN + 1, rows, :],
            send_sem=sems[0].at[d],
            recv_sem=sems[1].at[d],
            device_id=(m, s_up if up else s_dn),
            device_id_type=MESH,
        )

    def perm_halo(up):
        return pltpu.make_async_remote_copy(
            src_ref=a_v.at[:, 2 if up else 1],
            dst_ref=a_v.at[:, 0 if up else 3],
            send_sem=perm_send.at[1 if up else 0],
            recv_sem=perm_recv.at[1 if up else 0],
            device_id=(m, s_up if up else s_dn),
            device_id_type=MESH,
        )

    def send_back(d):
        g = peer_to(d)
        return pltpu.make_async_remote_copy(
            src_ref=r_out.at[g],
            dst_ref=ret.at[:, pl.ds(pl.multiple_of(m * OWN * PAD, OWN * PAD), OWN * PAD), :],
            send_sem=ret_send.at[d],
            recv_sem=ret_recv.at[d],
            device_id=(g, s),
            device_id_type=MESH,
        )

    pl.semaphore_wait(barrier, GROUPS - 1 + 2)
    for d in range(1, GROUPS):
        send_block(d).start()
    load_a.wait()
    perm_halo(True).start()
    perm_halo(False).start()
    halo(0, True).start()
    halo(0, False).start()

    load_t.wait()
    load_c.wait()
    mode_i = tri_v[0:1, :]
    mode_j = tri_v[1:2, :]
    mode_k = tri_v[2:3, :]
    row_i = mode_i + ((mode_i * 274) >> 12)
    col_jk = mode_j + 113 * ((mode_j * 274) >> 12) + PAD * mode_k
    cf = cf_v[...].reshape(1, ENTRIES)
    cf_hi = cf.astype(BF16).astype(F32)
    cf_lo = cf - cf_hi
    is_row = lax.broadcasted_iota(jnp.int32, (WIDE, ENTRIES), 0) == row_i
    a_hot[0:WIDE, :] = jnp.where(is_row, cf_hi, 0.0).astype(BF16)
    a_hot[WIDE:, :] = jnp.where(is_row, cf_lo, 0.0).astype(BF16)

    def table(c, carry):
        cols = lax.broadcasted_iota(jnp.int32, (2 * WIDE, ENTRIES), 0) + c * (2 * WIDE)
        b_hot = jnp.where(cols == col_jk, 1.0, 0.0).astype(BF16)
        both = lax.dot_general(
            a_hot[...], b_hot, (((1,), (1,)), ((), ())), preferred_element_type=F32
        )
        coupled = both[:WIDE] + both[WIDE:]
        for part in range(2):
            one = coupled[:, part * WIDE : (part + 1) * WIDE]
            hi = one.astype(BF16)
            lo = (one - hi.astype(F32)).astype(BF16)
            for side in range(2):
                w_mat[2 * c + part, 0:WIDE, side * WIDE : (side + 1) * WIDE] = hi
                w_mat[2 * c + part, WIDE:, side * WIDE : (side + 1) * WIDE] = lo
        return carry

    lax.fori_loop(0, GROUPS // 2, table, 0)

    perm_halo(True).wait_recv()
    perm_halo(False).wait_recv()
    has_dn = (s > 0).astype(F32)
    has_up = (s < space_count - 1).astype(F32)
    row_ids = lax.broadcasted_iota(jnp.int32, (ROWS, LANES), 0)
    lane_ids = lax.broadcasted_iota(jnp.int32, (ROWS, LANES), 1)

    def weights(k, carry):
        for layer in range(LAYERS):
            a = a_v[k, layer + 1]
            low = a_v[k, layer]
            high = a_v[k, layer + 2]
            if layer == 0:
                low = low * has_dn
            else:
                high = high * has_up
            sides = (
                low,
                high,
                jnp.where(row_ids > 0, pltpu.roll(a, 1, 0), 0.0),
                jnp.where(row_ids < ROWS - 1, pltpu.roll(a, ROWS - 1, 0), 0.0),
                jnp.where(lane_ids > 0, pltpu.roll(a, 1, 1), 0.0),
                jnp.where(lane_ids < LANES - 1, pltpu.roll(a, LANES - 1, 1), 0.0),
            )
            total = jnp.zeros((ROWS, LANES), F32)
            for f, side in enumerate(sides):
                w = 0.5 * (a + side)
                w_f[f, k, layer] = w
                total = total + w
            dg[k, layer] = total
        return carry

    lax.fori_loop(0, KA, weights, 0)

    def chunk(d):
        g = peer_from(d)
        rows = mode_rows(g)
        lanes = lax.broadcasted_iota(jnp.int32, (PAD, LANES), 1)
        for layer in range(LAYERS):
            for r in range(OWN):
                p = q[layer + 1, r + 1, rows, :]
                low = q[layer, r + 1, rows, :]
                high = q[layer + 2, r + 1, rows, :]
                if layer == 0:
                    low = low * has_dn
                else:
                    high = high * has_up
                diffs = (
                    p - low,
                    p - high,
                    p - q[layer + 1, r, rows, :],
                    p - q[layer + 1, r + 2, rows, :],
                    p - jnp.where(lanes > 0, pltpu.roll(p, 1, 1), 0.0),
                    p - jnp.where(lanes < LANES - 1, pltpu.roll(p, LANES - 1, 1), 0.0),
                )
                at = (layer * OWN + r) * LANES
                for k in range(KA):
                    total = None
                    for f in range(6):
                        term = w_f[f, k, layer, pl.ds(m * OWN + r, 1), :] * diffs[f]
                        total = term if total is None else total + term
                    hi = total.astype(BF16)
                    lo = (total - hi.astype(F32)).astype(BF16)
                    m_buf[k * PAD : (k + 1) * PAD, at : at + LANES] = hi
                    m_buf[WIDE + k * PAD : WIDE + (k + 1) * PAD, at : at + LANES] = lo
            for n in range(OWN // 2):
                at = (layer * OWN + 2 * n) * LANES
                prod = jnp.dot(
                    w_mat[g], m_buf[:, at : at + 2 * LANES], preferred_element_type=F32
                )
                prod = prod[:WIDE] + prod[WIDE:]
                for part in range(2):
                    r = 2 * n + part
                    for go in range(GROUPS):
                        r_out[go, layer, r * PAD : (r + 1) * PAD, :] += prod[
                            go * PAD : (go + 1) * PAD, part * LANES : (part + 1) * LANES
                        ]

    def step(d, carry):
        @pl.when(d < GROUPS)
        def _():
            send_block(d).wait_recv()
            halo(d, True).start()
            halo(d, False).start()

        halo(d - 1, True).wait_recv()
        halo(d - 1, False).wait_recv()
        chunk(d - 1)
        return carry

    lax.fori_loop(1, GROUPS + 1, step, 0)

    for d in range(1, GROUPS):
        send_back(d).start()
    ret[:, pl.ds(pl.multiple_of(m * OWN * PAD, OWN * PAD), OWN * PAD), :] = r_out[m]

    own_rows = w_mat[m, mode_rows(m), 0:WIDE].astype(F32) + w_mat[
        m, pl.ds(pl.multiple_of(WIDE + m * PAD, PAD), PAD), 0:WIDE
    ].astype(F32)
    sub = lax.broadcasted_iota(jnp.int32, (PAD, LANES), 0)
    lane = lax.broadcasted_iota(jnp.int32, (PAD, LANES), 1)
    for k in range(KA):
        picked = jnp.where(lane == sub + k * PAD, own_rows, 0.0)
        cdb[k] = jnp.broadcast_to(jnp.sum(picked, axis=1, keepdims=True), (PAD, LANES))

    load_s.wait()

    def scales(j, carry):
        for layer in range(LAYERS):
            scale = jnp.zeros((ROWS, LANES), F32)
            for k in range(KA):
                scale = scale + cdb[k, pl.ds(j, 1), :] * dg[k, layer]
            at = pl.ds(pl.multiple_of(j * 64 + layer * ROWS, ROWS), ROWS)
            inv = relax_weight / scale
            inv_v[at, :] = inv
            base_v[at, :] = p_v[at, :] + s_v[at, :] * inv
        return carry

    lax.fori_loop(0, LOCAL, scales, 0)

    for d in range(1, GROUPS):
        send_back(d).wait_recv()

    def finish(j, carry):
        for layer in range(LAYERS):
            for r8 in range(ROWS // 8):
                got = ret[layer, pl.ds(r8 * 8 * PAD + j, 8, stride=PAD), :]
                at = pl.ds(pl.multiple_of(j * 64 + layer * ROWS + r8 * 8, 8), 8)
                oa_v[at, :] = got
                or_v[at, :] = base_v[at, :] - got * inv_v[at, :]
        return carry

    lax.fori_loop(0, LOCAL, finish, 0)
    out_a = pltpu.make_async_copy(oa_v, out_a_hbm, out_sem.at[0])
    out_r = pltpu.make_async_copy(or_v, out_r_hbm, out_sem.at[1])
    out_a.start()
    out_r.start()

    for d in range(1, GROUPS):
        send_block(d).wait_send()
        send_back(d).wait_send()
    for d in range(GROUPS):
        halo(d, True).wait_send()
        halo(d, False).wait_send()
    perm_halo(True).wait_send()
    perm_halo(False).wait_send()
    out_a.wait()
    out_r.wait()


def solution(mesh):
    space_count = mesh.shape["space"]
    cells = (LOCAL * LAYERS * ROWS, LANES)

    def on_device(pressure, source, perm_modes, triples, coeffs):
        applied, relaxed = pl.pallas_call(
            functools.partial(kernel, space_count),
            out_shape=[jax.ShapeDtypeStruct(cells, F32)] * 2,
            in_specs=[pl.BlockSpec(memory_space=pl.ANY)] * 5,
            out_specs=[pl.BlockSpec(memory_space=pl.ANY)] * 2,
            scratch_shapes=[
                pltpu.VMEM((PAD * LAYERS * ROWS, LANES), F32),
                pltpu.VMEM(cells, F32),
                pltpu.VMEM((KA, LAYERS + 2, ROWS, LANES), F32),
                pltpu.VMEM((3, ENTRIES), jnp.int32),
                pltpu.VMEM((ENTRIES,), F32),
                pltpu.VMEM((LAYERS, ROWS + 2, PAD, LANES), F32),
                pltpu.VMEM((LAYERS + 2, OWN + 2, WIDE, LANES), F32),
                pltpu.VMEM((GROUPS, LAYERS, OWN * PAD, LANES), F32),
                pltpu.VMEM((LAYERS, ROWS * PAD, LANES), F32),
                pltpu.VMEM((GROUPS, 2 * WIDE, 2 * WIDE), BF16),
                pltpu.VMEM((2 * WIDE, ENTRIES), BF16),
                pltpu.VMEM((2 * WIDE, LAYERS * OWN * LANES), BF16),
                pltpu.VMEM((6, KA, LAYERS, ROWS, LANES), F32),
                pltpu.VMEM((KA, LAYERS, ROWS, LANES), F32),
                pltpu.VMEM((KA, PAD, LANES), F32),
                pltpu.VMEM(cells, F32),
                pltpu.VMEM(cells, F32),
                pltpu.VMEM(cells, F32),
                pltpu.VMEM(cells, F32),
                pltpu.SemaphoreType.DMA((5,)),
                pltpu.SemaphoreType.DMA((2,)),
            ]
            + [pltpu.SemaphoreType.DMA((GROUPS,))] * 6
            + [pltpu.SemaphoreType.DMA((2,))] * 2
            + [pltpu.SemaphoreType.DMA((GROUPS,))] * 2,
            compiler_params=pltpu.CompilerParams(
                collective_id=0, has_side_effects=True, vmem_limit_bytes=48 * 1024 * 1024
            ),
        )(
            pressure.reshape(cells),
            source.reshape(cells),
            perm_modes,
            triples,
            coeffs,
        )
        return applied.reshape(pressure.shape), relaxed.reshape(pressure.shape)

    return jax.shard_map(
        on_device,
        mesh=mesh,
        in_specs=(
            P("modes", "space", None, None),
            P("modes", "space", None, None),
            P(None, "space", None, None),
            P(),
            P(),
        ),
        out_specs=(P("modes", "space", None, None), P("modes", "space", None, None)),
        check_vma=False,
    )
```

```python
import functools

import jax
import jax.numpy as jnp
from jax import lax
from jax.experimental import pallas as pl
from jax.experimental.pallas import tpu as pltpu
from jax.sharding import PartitionSpec as P

KA = 8
GROUPS = 8
LOCAL = 15
PAD = 16
LAYERS = 2
ROWS = 32
LANES = 128
OWN = ROWS // GROUPS
ENTRIES = 2880
LAG = 4
WIDE = GROUPS * PAD
relax_weight = 0.8

MESH = pl.DeviceIdType.MESH
F32 = jnp.float32
BF16 = jnp.bfloat16


def kernel(
    space_count,
    p_hbm,
    s_hbm,
    a_hbm,
    tri_hbm,
    cf_hbm,
    out_a_hbm,
    out_r_hbm,
    p_v,
    s_v,
    a_v,
    tri_v,
    cf_v,
    t,
    q,
    r_out,
    ret,
    w_mat,
    a_hot,
    m_buf,
    w_f,
    dg,
    cdb,
    inv_v,
    base_v,
    oa_v,
    or_v,
    in_sem,
    out_sem,
    a2a_send,
    a2a_recv,
    low_send,
    low_recv,
    high_send,
    high_recv,
    perm_send,
    perm_recv,
    ret_send,
    ret_recv,
):
    m = lax.axis_index("modes")
    s = lax.axis_index("space")
    has_dn = s > 0
    has_up = s < space_count - 1

    def peer_to(d):
        return lax.rem(m + d, GROUPS)

    def peer_from(d):
        return lax.rem(m + GROUPS - d, GROUPS)

    def mode_rows(g):
        return pl.ds(pl.multiple_of(g * PAD, PAD), PAD)

    barrier = pltpu.get_barrier_semaphore()
    for d in range(1, GROUPS):
        pl.semaphore_signal(barrier, inc=1, device_id=(peer_to(d), s), device_id_type=MESH)

    @pl.when(has_dn)
    def _():
        pl.semaphore_signal(barrier, inc=1, device_id=(m, s - 1), device_id_type=MESH)

    @pl.when(has_up)
    def _():
        pl.semaphore_signal(barrier, inc=1, device_id=(m, s + 1), device_id_type=MESH)

    load_p = pltpu.make_async_copy(p_hbm, p_v.at[0 : LOCAL * 64], in_sem.at[0])
    load_a = pltpu.make_async_copy(a_hbm, a_v.at[:, 1:3], in_sem.at[1])
    load_t = pltpu.make_async_copy(tri_hbm, tri_v, in_sem.at[2])
    load_c = pltpu.make_async_copy(cf_hbm, cf_v, in_sem.at[3])
    load_s = pltpu.make_async_copy(s_hbm, s_v, in_sem.at[4])
    for load in (load_p, load_a, load_t, load_c, load_s):
        load.start()

    p_v[LOCAL * 64 :, :] = jnp.zeros((64, LANES), F32)
    t[:, 0] = jnp.zeros((LAYERS, PAD, LANES), F32)
    t[:, ROWS + 1] = jnp.zeros((LAYERS, PAD, LANES), F32)
    load_p.wait()

    def stage(row, carry):
        for layer in range(LAYERS):
            for half in range(2):
                start = half * 8 * 64 + layer * ROWS + row
                t[layer, row + 1, half * 8 : half * 8 + 8, :] = p_v[pl.ds(start, 8, stride=64), :]
        return carry

    lax.fori_loop(0, ROWS, stage, 0)
    q[1:3, :, mode_rows(m), :] = t[:, pl.ds(m * OWN, OWN + 2), :, :]

    def send_block(d):
        g = peer_to(d)
        return pltpu.make_async_remote_copy(
            src_ref=t.at[:, pl.ds(g * OWN, OWN + 2)],
            dst_ref=q.at[1:3, :, mode_rows(m), :],
            send_sem=a2a_send.at[d],
            recv_sem=a2a_recv.at[d],
            device_id=(g, s),
            device_id_type=MESH,
        )

    def halo(d, up):
        rows = mode_rows(peer_from(d))
        sems = (high_send, high_recv) if up else (low_send, low_recv)
        return pltpu.make_async_remote_copy(
            src_ref=q.at[2 if up else 1, 1 : OWN + 1, rows, :],
            dst_ref=q.at[0 if up else 3, 1 : OWN + 1, rows, :],
            send_sem=sems[0].at[d],
            recv_sem=sems[1].at[d],
            device_id=(m, s + 1 if up else s - 1),
            device_id_type=MESH,
        )

    def perm_halo(up):
        return pltpu.make_async_remote_copy(
            src_ref=a_v.at[:, 2 if up else 1],
            dst_ref=a_v.at[:, 0 if up else 3],
            send_sem=perm_send.at[1 if up else 0],
            recv_sem=perm_recv.at[1 if up else 0],
            device_id=(m, s + 1 if up else s - 1),
            device_id_type=MESH,
        )

    def send_back(d, layer):
        g = peer_to(d)
        return pltpu.make_async_remote_copy(
            src_ref=r_out.at[g, layer],
            dst_ref=ret.at[layer, pl.ds(pl.multiple_of(m * OWN * PAD, OWN * PAD), OWN * PAD), :],
            send_sem=ret_send.at[d, layer],
            recv_sem=ret_recv.at[d, layer],
            device_id=(g, s),
            device_id_type=MESH,
        )

    def both_ways(make, act):
        @pl.when(has_up)
        def _():
            getattr(make(True), act)()

        @pl.when(has_dn)
        def _():
            getattr(make(False), act)()

    def arrived(make):
        @pl.when(has_dn)
        def _():
            make(True).wait_recv()

        @pl.when(has_up)
        def _():
            make(False).wait_recv()

    neighbours = GROUPS - 1 + has_dn.astype(jnp.int32) + has_up.astype(jnp.int32)
    pl.semaphore_wait(barrier, neighbours)
    for d in range(1, GROUPS):
        send_block(d).start()
    load_a.wait()
    both_ways(perm_halo, "start")
    both_ways(functools.partial(halo, 0), "start")

    @pl.when(jnp.logical_not(has_dn))
    def _():
        q[0] = jnp.zeros(q.shape[1:], F32)
        a_v[:, 0] = jnp.zeros((KA, ROWS, LANES), F32)

    @pl.when(jnp.logical_not(has_up))
    def _():
        q[3] = jnp.zeros(q.shape[1:], F32)
        a_v[:, 3] = jnp.zeros((KA, ROWS, LANES), F32)

    load_t.wait()
    load_c.wait()
    mode_i = tri_v[0:1, :]
    mode_j = tri_v[1:2, :]
    mode_k = tri_v[2:3, :]
    row_i = mode_i + ((mode_i * 274) >> 12)
    col_jk = mode_j + 113 * ((mode_j * 274) >> 12) + PAD * mode_k
    cf = cf_v[...].reshape(1, ENTRIES)
    cf_hi = cf.astype(BF16).astype(F32)
    cf_lo = cf - cf_hi
    is_row = lax.broadcasted_iota(jnp.int32, (WIDE, ENTRIES), 0) == row_i
    a_hot[0:WIDE, :] = jnp.where(is_row, cf_hi, 0.0).astype(BF16)
    a_hot[WIDE:, :] = jnp.where(is_row, cf_lo, 0.0).astype(BF16)

    def table(c, carry):
        cols = lax.broadcasted_iota(jnp.int32, (2 * WIDE, ENTRIES), 0) + c * (2 * WIDE)
        b_hot = jnp.where(cols == col_jk, 1.0, 0.0).astype(BF16)
        both = lax.dot_general(
            a_hot[...], b_hot, (((1,), (1,)), ((), ())), preferred_element_type=F32
        )
        coupled = both[:WIDE] + both[WIDE:]
        for part in range(2):
            one = coupled[:, part * WIDE : (part + 1) * WIDE]
            hi = one.astype(BF16)
            lo = (one - hi.astype(F32)).astype(BF16)
            for side in range(2):
                at = pl.multiple_of(c * 4 * WIDE + (2 * part + side) * WIDE, WIDE)
                w_mat[0:WIDE, pl.ds(at, WIDE)] = hi
                w_mat[WIDE:, pl.ds(at, WIDE)] = lo
        return carry

    lax.fori_loop(0, GROUPS // 2, table, 0)

    arrived(perm_halo)
    row_ids = lax.broadcasted_iota(jnp.int32, (ROWS, LANES), 0)
    lane_ids = lax.broadcasted_iota(jnp.int32, (ROWS, LANES), 1)

    def weights(k, carry):
        for layer in range(LAYERS):
            a = a_v[k, layer + 1]
            low = a_v[k, layer]
            high = a_v[k, layer + 2]
            sides = (
                low,
                high,
                jnp.where(row_ids > 0, pltpu.roll(a, 1, 0), 0.0),
                jnp.where(row_ids < ROWS - 1, pltpu.roll(a, ROWS - 1, 0), 0.0),
                jnp.where(lane_ids > 0, pltpu.roll(a, 1, 1), 0.0),
                jnp.where(lane_ids < LANES - 1, pltpu.roll(a, LANES - 1, 1), 0.0),
            )
            total = jnp.zeros((ROWS, LANES), F32)
            for f, side in enumerate(sides):
                w = 0.5 * (a + side)
                w_f[f, k, layer] = w
                total = total + w
            dg[k, layer] = total
        return carry

    lax.fori_loop(0, KA, weights, 0)

    def chunk(d):
        g = peer_from(d)
        rows = mode_rows(g)
        lanes = lax.broadcasted_iota(jnp.int32, (PAD, LANES), 1)
        for layer in range(LAYERS):
            for r in range(OWN):
                p = q[layer + 1, r + 1, rows, :]
                diffs = (
                    p - q[layer, r + 1, rows, :],
                    p - q[layer + 2, r + 1, rows, :],
                    p - q[layer + 1, r, rows, :],
                    p - q[layer + 1, r + 2, rows, :],
                    p - jnp.where(lanes > 0, pltpu.roll(p, 1, 1), 0.0),
                    p - jnp.where(lanes < LANES - 1, pltpu.roll(p, LANES - 1, 1), 0.0),
                )
                at = (layer * OWN + r) * LANES
                for k in range(KA):
                    total = None
                    for f in range(6):
                        term = w_f[f, k, layer, pl.ds(m * OWN + r, 1), :] * diffs[f]
                        total = term if total is None else total + term
                    hi = total.astype(BF16)
                    lo = (total - hi.astype(F32)).astype(BF16)
                    for part, piece in enumerate((hi, lo)):
                        to = pl.multiple_of((2 * g + part) * WIDE + k * PAD, PAD)
                        m_buf[pl.ds(to, PAD), at : at + LANES] = piece

    def step(d, carry):
        @pl.when(d < GROUPS)
        def _():
            send_block(d).wait_recv()
            both_ways(functools.partial(halo, d), "start")

        @pl.when(d >= LAG)
        def _():
            arrived(functools.partial(halo, d - LAG))
            chunk(d - LAG)

        return carry

    lax.fori_loop(1, GROUPS + LAG, step, 0)

    for layer in range(LAYERS):
        half = OWN * LANES
        prod = jnp.dot(
            w_mat[...],
            m_buf[:, layer * half : (layer + 1) * half],
            preferred_element_type=F32,
        )
        prod = prod[:WIDE] + prod[WIDE:]
        for r in range(OWN):
            for go in range(GROUPS):
                r_out[go, layer, r * PAD : (r + 1) * PAD, :] = prod[
                    go * PAD : (go + 1) * PAD, r * LANES : (r + 1) * LANES
                ]
        for d in range(1, GROUPS):
            send_back(d, layer).start()
    ret[:, pl.ds(pl.multiple_of(m * OWN * PAD, OWN * PAD), OWN * PAD), :] = r_out[m]

    own_cols = pl.ds(pl.multiple_of(2 * WIDE * m, 2 * WIDE), WIDE)
    own_rows = w_mat[mode_rows(m), own_cols].astype(F32) + w_mat[
        pl.ds(pl.multiple_of(WIDE + m * PAD, PAD), PAD), own_cols
    ].astype(F32)
    sub = lax.broadcasted_iota(jnp.int32, (PAD, LANES), 0)
    lane = lax.broadcasted_iota(jnp.int32, (PAD, LANES), 1)
    for k in range(KA):
        picked = jnp.where(lane == sub + k * PAD, own_rows, 0.0)
        cdb[k] = jnp.broadcast_to(jnp.sum(picked, axis=1, keepdims=True), (PAD, LANES))

    load_s.wait()

    def scales(j, carry):
        for layer in range(LAYERS):
            scale = jnp.zeros((ROWS, LANES), F32)
            for k in range(KA):
                scale = scale + cdb[k, pl.ds(j, 1), :] * dg[k, layer]
            at = pl.ds(pl.multiple_of(j * 64 + layer * ROWS, ROWS), ROWS)
            inv = relax_weight / scale
            inv_v[at, :] = inv
            base_v[at, :] = p_v[at, :] + s_v[at, :] * inv
        return carry

    lax.fori_loop(0, LOCAL, scales, 0)

    def finish(layer, j, carry):
        for r8 in range(ROWS // 8):
            got = ret[layer, pl.ds(r8 * 8 * PAD + j, 8, stride=PAD), :]
            at = pl.ds(pl.multiple_of(j * 64 + layer * ROWS + r8 * 8, 8), 8)
            oa_v[at, :] = got
            or_v[at, :] = base_v[at, :] - got * inv_v[at, :]
        return carry

    for layer in range(LAYERS):
        for d in range(1, GROUPS):
            send_back(d, layer).wait_recv()
        lax.fori_loop(0, LOCAL, functools.partial(finish, layer), 0)
    out_a = pltpu.make_async_copy(oa_v, out_a_hbm, out_sem.at[0])
    out_r = pltpu.make_async_copy(or_v, out_r_hbm, out_sem.at[1])
    out_a.start()
    out_r.start()

    for d in range(1, GROUPS):
        send_block(d).wait_send()
        for layer in range(LAYERS):
            send_back(d, layer).wait_send()
    for d in range(GROUPS):
        both_ways(functools.partial(halo, d), "wait_send")
    both_ways(perm_halo, "wait_send")
    out_a.wait()
    out_r.wait()


def solution(mesh):
    space_count = mesh.shape["space"]
    cells = (LOCAL * LAYERS * ROWS, LANES)

    def on_device(pressure, source, perm_modes, triples, coeffs):
        applied, relaxed = pl.pallas_call(
            functools.partial(kernel, space_count),
            out_shape=[jax.ShapeDtypeStruct(cells, F32)] * 2,
            in_specs=[pl.BlockSpec(memory_space=pltpu.HBM)] * 5,
            out_specs=[pl.BlockSpec(memory_space=pl.ANY)] * 2,
            scratch_shapes=[
                pltpu.VMEM((PAD * LAYERS * ROWS, LANES), F32),
                pltpu.VMEM(cells, F32),
                pltpu.VMEM((KA, LAYERS + 2, ROWS, LANES), F32),
                pltpu.VMEM((3, ENTRIES), jnp.int32),
                pltpu.VMEM((ENTRIES,), F32),
                pltpu.VMEM((LAYERS, ROWS + 2, PAD, LANES), F32),
                pltpu.VMEM((LAYERS + 2, OWN + 2, WIDE, LANES), F32),
                pltpu.VMEM((GROUPS, LAYERS, OWN * PAD, LANES), F32),
                pltpu.VMEM((LAYERS, ROWS * PAD, LANES), F32),
                pltpu.VMEM((2 * WIDE, GROUPS * 2 * WIDE), BF16),
                pltpu.VMEM((2 * WIDE, ENTRIES), BF16),
                pltpu.VMEM((GROUPS * 2 * WIDE, LAYERS * OWN * LANES), BF16),
                pltpu.VMEM((6, KA, LAYERS, ROWS, LANES), F32),
                pltpu.VMEM((KA, LAYERS, ROWS, LANES), F32),
                pltpu.VMEM((KA, PAD, LANES), F32),
                pltpu.VMEM(cells, F32),
                pltpu.VMEM(cells, F32),
                pltpu.VMEM(cells, F32),
                pltpu.VMEM(cells, F32),
                pltpu.SemaphoreType.DMA((5,)),
                pltpu.SemaphoreType.DMA((2,)),
            ]
            + [pltpu.SemaphoreType.DMA((GROUPS,))] * 6
            + [pltpu.SemaphoreType.DMA((2,))] * 2
            + [pltpu.SemaphoreType.DMA((GROUPS, LAYERS))] * 2,
            compiler_params=pltpu.CompilerParams(
                collective_id=0, has_side_effects=True, vmem_limit_bytes=60 * 1024 * 1024
            ),
        )(
            pressure.reshape(cells),
            source.reshape(cells),
            perm_modes,
            triples,
            coeffs,
        )
        return applied.reshape(pressure.shape), relaxed.reshape(pressure.shape)

    return jax.shard_map(
        on_device,
        mesh=mesh,
        in_specs=(
            P("modes", "space", None, None),
            P("modes", "space", None, None),
            P(None, "space", None, None),
            P(),
            P(),
        ),
        out_specs=(P("modes", "space", None, None), P("modes", "space", None, None)),
        check_vma=False,
    )
```

```python
import functools

import jax
import jax.numpy as jnp
from jax import lax
from jax.experimental import pallas as pl
from jax.experimental.pallas import tpu as pltpu
from jax.sharding import PartitionSpec as P

KA = 8
GROUPS = 8
LOCAL = 15
PAD = 16
LAYERS = 2
ROWS = 32
LANES = 128
OWN = ROWS // GROUPS
ENTRIES = 2880
LAG = 4
EDGE = 8
DATA = slice(EDGE, EDGE + ROWS)
WIDE = GROUPS * PAD
relax_weight = 0.8

MESH = pl.DeviceIdType.MESH
F32 = jnp.float32
BF16 = jnp.bfloat16


def kernel(
    space_count,
    p_hbm,
    s_hbm,
    a_hbm,
    tri_hbm,
    cf_hbm,
    out_a_hbm,
    out_b_hbm,
    out_i_hbm,
    p_v,
    s_v,
    a_v,
    tri_v,
    cf_v,
    t,
    q,
    r_out,
    ret,
    w_mat,
    a_hot,
    m_buf,
    w_f,
    a_str,
    a_y,
    dg,
    cdb,
    inv_v,
    base_v,
    oa_v,
    in_sem,
    out_sem,
    a2a_send,
    a2a_recv,
    low_send,
    low_recv,
    high_send,
    high_recv,
    perm_send,
    perm_recv,
    str_send,
    str_recv,
    ret_send,
    ret_recv,
):
    m = lax.axis_index("modes")
    s = lax.axis_index("space")
    has_dn = s > 0
    has_up = s < space_count - 1

    def peer_to(d):
        return lax.rem(m + d, GROUPS)

    def peer_from(d):
        return lax.rem(m + GROUPS - d, GROUPS)

    def mode_rows(g):
        return pl.ds(pl.multiple_of(g * PAD, PAD), PAD)

    barrier = pltpu.get_barrier_semaphore()
    for d in range(1, GROUPS):
        pl.semaphore_signal(barrier, inc=1, device_id=(peer_to(d), s), device_id_type=MESH)

    @pl.when(has_dn)
    def _():
        pl.semaphore_signal(barrier, inc=1, device_id=(m, s - 1), device_id_type=MESH)

    @pl.when(has_up)
    def _():
        pl.semaphore_signal(barrier, inc=1, device_id=(m, s + 1), device_id_type=MESH)

    load_p = pltpu.make_async_copy(p_hbm, p_v.at[0 : LOCAL * 64], in_sem.at[0])
    load_a = pltpu.make_async_copy(a_hbm, a_v.at[:, 1:3, DATA], in_sem.at[1])
    load_t = pltpu.make_async_copy(tri_hbm, tri_v, in_sem.at[2])
    load_c = pltpu.make_async_copy(cf_hbm, cf_v, in_sem.at[3])
    load_s = pltpu.make_async_copy(s_hbm, s_v, in_sem.at[4])
    for load in (load_p, load_a, load_t, load_c, load_s):
        load.start()

    p_v[LOCAL * 64 :, :] = jnp.zeros((64, LANES), F32)
    t[:, 0] = jnp.zeros((LAYERS, PAD, LANES), F32)
    t[:, ROWS + 1] = jnp.zeros((LAYERS, PAD, LANES), F32)
    load_p.wait()

    def stage(row, carry):
        for layer in range(LAYERS):
            for half in range(2):
                start = half * 8 * 64 + layer * ROWS + row
                t[layer, row + 1, half * 8 : half * 8 + 8, :] = p_v[pl.ds(start, 8, stride=64), :]
        return carry

    lax.fori_loop(0, ROWS, stage, 0)
    q[1:3, :, mode_rows(m), :] = t[:, pl.ds(m * OWN, OWN + 2), :, :]

    def send_block(d):
        g = peer_to(d)
        return pltpu.make_async_remote_copy(
            src_ref=t.at[:, pl.ds(g * OWN, OWN + 2)],
            dst_ref=q.at[1:3, :, mode_rows(m), :],
            send_sem=a2a_send.at[d],
            recv_sem=a2a_recv.at[d],
            device_id=(g, s),
            device_id_type=MESH,
        )

    def halo(d, up):
        rows = mode_rows(peer_from(d))
        sems = (high_send, high_recv) if up else (low_send, low_recv)
        return pltpu.make_async_remote_copy(
            src_ref=q.at[2 if up else 1, 1 : OWN + 1, rows, :],
            dst_ref=q.at[0 if up else 3, 1 : OWN + 1, rows, :],
            send_sem=sems[0].at[d],
            recv_sem=sems[1].at[d],
            device_id=(m, s + 1 if up else s - 1),
            device_id_type=MESH,
        )

    def perm_halo(up):
        return pltpu.make_async_remote_copy(
            src_ref=a_v.at[:, 2 if up else 1, DATA],
            dst_ref=a_v.at[:, 0 if up else 3, DATA],
            send_sem=perm_send.at[1 if up else 0],
            recv_sem=perm_recv.at[1 if up else 0],
            device_id=(m, s + 1 if up else s - 1),
            device_id_type=MESH,
        )

    def strip(up):
        return pltpu.make_async_remote_copy(
            src_ref=a_str.at[2 if up else 1],
            dst_ref=a_str.at[0 if up else 3],
            send_sem=str_send.at[1 if up else 0],
            recv_sem=str_recv.at[1 if up else 0],
            device_id=(m, s + 1 if up else s - 1),
            device_id_type=MESH,
        )

    def send_back(d, layer):
        g = peer_to(d)
        return pltpu.make_async_remote_copy(
            src_ref=r_out.at[g, layer],
            dst_ref=ret.at[layer, pl.ds(pl.multiple_of(m * OWN * PAD, OWN * PAD), OWN * PAD), :],
            send_sem=ret_send.at[d, layer],
            recv_sem=ret_recv.at[d, layer],
            device_id=(g, s),
            device_id_type=MESH,
        )

    def both_ways(make, act):
        @pl.when(has_up)
        def _():
            getattr(make(True), act)()

        @pl.when(has_dn)
        def _():
            getattr(make(False), act)()

    def arrived(make):
        @pl.when(has_dn)
        def _():
            make(True).wait_recv()

        @pl.when(has_up)
        def _():
            make(False).wait_recv()

    load_a.wait()
    for layer in range(LAYERS):
        a_v[:, layer + 1, 0:EDGE] = jnp.zeros((KA, EDGE, LANES), F32)
        a_v[:, layer + 1, EDGE + ROWS :] = jnp.zeros((KA, EDGE, LANES), F32)
        for k in range(KA):
            to = slice(k * OWN, (k + 1) * OWN)
            a_str[layer + 1, to, :] = a_v[k, layer + 1, pl.ds(EDGE + m * OWN, OWN), :]
            a_y[0, layer, to, :] = a_v[k, layer + 1, pl.ds(EDGE + m * OWN - 1, OWN), :]
            a_y[1, layer, to, :] = a_v[k, layer + 1, pl.ds(EDGE + m * OWN + 1, OWN), :]

    neighbours = GROUPS - 1 + has_dn.astype(jnp.int32) + has_up.astype(jnp.int32)
    pl.semaphore_wait(barrier, neighbours)
    both_ways(strip, "start")
    for d in range(1, GROUPS):
        send_block(d).start()
    both_ways(functools.partial(halo, 0), "start")

    @pl.when(jnp.logical_not(has_dn))
    def _():
        q[0] = jnp.zeros(q.shape[1:], F32)
        a_v[:, 0, DATA] = jnp.zeros((KA, ROWS, LANES), F32)
        a_str[0] = jnp.zeros((KA * OWN, LANES), F32)

    @pl.when(jnp.logical_not(has_up))
    def _():
        q[3] = jnp.zeros(q.shape[1:], F32)
        a_v[:, 3, DATA] = jnp.zeros((KA, ROWS, LANES), F32)
        a_str[3] = jnp.zeros((KA * OWN, LANES), F32)

    load_t.wait()
    load_c.wait()
    mode_i = tri_v[0:1, :]
    mode_j = tri_v[1:2, :]
    mode_k = tri_v[2:3, :]
    row_i = mode_i + ((mode_i * 274) >> 12)
    col_jk = mode_j + 113 * ((mode_j * 274) >> 12) + PAD * mode_k
    cf = cf_v[...].reshape(1, ENTRIES)
    cf_hi = cf.astype(BF16).astype(F32)
    cf_lo = cf - cf_hi
    is_row = lax.broadcasted_iota(jnp.int32, (WIDE, ENTRIES), 0) == row_i
    a_hot[0:WIDE, :] = jnp.where(is_row, cf_hi, 0.0).astype(BF16)
    a_hot[WIDE:, :] = jnp.where(is_row, cf_lo, 0.0).astype(BF16)

    def table(c, carry):
        cols = lax.broadcasted_iota(jnp.int32, (2 * WIDE, ENTRIES), 0) + c * (2 * WIDE)
        b_hot = jnp.where(cols == col_jk, 1.0, 0.0).astype(BF16)
        both = lax.dot_general(
            a_hot[...], b_hot, (((1,), (1,)), ((), ())), preferred_element_type=F32
        )
        coupled = both[:WIDE] + both[WIDE:]
        for part in range(2):
            one = coupled[:, part * WIDE : (part + 1) * WIDE]
            hi = one.astype(BF16)
            lo = (one - hi.astype(F32)).astype(BF16)
            for side in range(2):
                at = pl.multiple_of(c * 4 * WIDE + (2 * part + side) * WIDE, WIDE)
                w_mat[0:WIDE, pl.ds(at, WIDE)] = hi
                w_mat[WIDE:, pl.ds(at, WIDE)] = lo
        return carry

    lax.fori_loop(0, GROUPS // 2, table, 0)

    arrived(strip)
    lane_ids = lax.broadcasted_iota(jnp.int32, (ROWS, LANES), 1)

    def beside(a):
        return (
            jnp.where(lane_ids > 0, pltpu.roll(a, 1, 1), 0.0),
            jnp.where(lane_ids < LANES - 1, pltpu.roll(a, LANES - 1, 1), 0.0),
        )

    for layer in range(LAYERS):
        a = a_str[layer + 1]
        sides = (a_str[layer], a_str[layer + 2], a_y[0, layer], a_y[1, layer]) + beside(a)
        for f, side in enumerate(sides):
            w_f[f, layer] = a + side

    def chunk(d):
        g = peer_from(d)
        rows = mode_rows(g)
        lanes = lax.broadcasted_iota(jnp.int32, (PAD, LANES), 1)
        for layer in range(LAYERS):
            for r in range(OWN):
                p = q[layer + 1, r + 1, rows, :]
                diffs = (
                    p - q[layer, r + 1, rows, :],
                    p - q[layer + 2, r + 1, rows, :],
                    p - q[layer + 1, r, rows, :],
                    p - q[layer + 1, r + 2, rows, :],
                    p - jnp.where(lanes > 0, pltpu.roll(p, 1, 1), 0.0),
                    p - jnp.where(lanes < LANES - 1, pltpu.roll(p, LANES - 1, 1), 0.0),
                )
                at = (layer * OWN + r) * LANES
                for k in range(KA):
                    total = None
                    for f in range(6):
                        term = w_f[f, layer, k * OWN + r : k * OWN + r + 1, :] * diffs[f]
                        total = term if total is None else total + term
                    hi = total.astype(BF16)
                    lo = (total - hi.astype(F32)).astype(BF16)
                    for part, piece in enumerate((hi, lo)):
                        to = pl.multiple_of((2 * g + part) * WIDE + k * PAD, PAD)
                        m_buf[pl.ds(to, PAD), at : at + LANES] = piece

    def step(d, carry):
        @pl.when(d < GROUPS)
        def _():
            send_block(d).wait_recv()
            both_ways(functools.partial(halo, d), "start")

        @pl.when(d == GROUPS)
        def _():
            both_ways(perm_halo, "start")

        @pl.when(d >= LAG)
        def _():
            arrived(functools.partial(halo, d - LAG))
            chunk(d - LAG)

        return carry

    lax.fori_loop(1, GROUPS + LAG, step, 0)

    for layer in range(LAYERS):
        half = OWN * LANES
        prod = jnp.dot(
            w_mat[...],
            m_buf[:, layer * half : (layer + 1) * half],
            preferred_element_type=F32,
        )
        prod = prod[:WIDE] + prod[WIDE:]
        for r in range(OWN):
            for go in range(GROUPS):
                r_out[go, layer, r * PAD : (r + 1) * PAD, :] = prod[
                    go * PAD : (go + 1) * PAD, r * LANES : (r + 1) * LANES
                ]
        for d in range(1, GROUPS):
            send_back(d, layer).start()
    ret[:, pl.ds(pl.multiple_of(m * OWN * PAD, OWN * PAD), OWN * PAD), :] = r_out[m]

    own_cols = pl.ds(pl.multiple_of(2 * WIDE * m, 2 * WIDE), WIDE)
    own_rows = w_mat[mode_rows(m), own_cols].astype(F32) + w_mat[
        pl.ds(pl.multiple_of(WIDE + m * PAD, PAD), PAD), own_cols
    ].astype(F32)
    sub = lax.broadcasted_iota(jnp.int32, (PAD, LANES), 0)
    lane = lax.broadcasted_iota(jnp.int32, (PAD, LANES), 1)
    for k in range(KA):
        picked = jnp.where(lane == sub + k * PAD, own_rows, 0.0)
        cdb[k] = jnp.broadcast_to(jnp.sum(picked, axis=1, keepdims=True), (PAD, LANES))

    arrived(perm_halo)

    def diagonal(k, carry):
        for layer in range(LAYERS):
            a = a_v[k, layer + 1, DATA]
            sides = (
                a_v[k, layer, DATA],
                a_v[k, layer + 2, DATA],
                a_v[k, layer + 1, EDGE - 1 : EDGE - 1 + ROWS],
                a_v[k, layer + 1, EDGE + 1 : EDGE + 1 + ROWS],
            ) + beside(a)
            total = 6.0 * a
            for side in sides:
                total = total + side
            dg[k, layer] = 0.5 * total
        return carry

    lax.fori_loop(0, KA, diagonal, 0)
    load_s.wait()

    def scales(j, carry):
        for layer in range(LAYERS):
            scale = jnp.zeros((ROWS, LANES), F32)
            for k in range(KA):
                scale = scale + cdb[k, pl.ds(j, 1), :] * dg[k, layer]
            at = pl.ds(pl.multiple_of(j * 64 + layer * ROWS, ROWS), ROWS)
            inv = relax_weight / scale
            inv_v[at, :] = inv
            base_v[at, :] = p_v[at, :] + s_v[at, :] * inv
        return carry

    lax.fori_loop(0, LOCAL, scales, 0)

    def finish(layer, j, carry):
        for r8 in range(ROWS // 8):
            got = ret[layer, pl.ds(r8 * 8 * PAD + j, 8, stride=PAD), :]
            at = pl.ds(pl.multiple_of(j * 64 + layer * ROWS + r8 * 8, 8), 8)
            oa_v[at, :] = got
        return carry

    out_b = pltpu.make_async_copy(base_v, out_b_hbm, out_sem.at[0])
    out_i = pltpu.make_async_copy(inv_v, out_i_hbm, out_sem.at[1])
    out_b.start()
    out_i.start()

    for layer in range(LAYERS):
        for d in range(1, GROUPS):
            send_back(d, layer).wait_recv()
        lax.fori_loop(0, LOCAL, functools.partial(finish, layer), 0)
    out_a = pltpu.make_async_copy(oa_v, out_a_hbm, out_sem.at[2])
    out_a.start()

    for d in range(1, GROUPS):
        send_block(d).wait_send()
        for layer in range(LAYERS):
            send_back(d, layer).wait_send()
    for d in range(GROUPS):
        both_ways(functools.partial(halo, d), "wait_send")
    both_ways(perm_halo, "wait_send")
    both_ways(strip, "wait_send")
    out_b.wait()
    out_i.wait()
    out_a.wait()


def solution(mesh):
    space_count = mesh.shape["space"]
    cells = (LOCAL * LAYERS * ROWS, LANES)

    def on_device(pressure, source, perm_modes, triples, coeffs):
        doubled, base, inv = pl.pallas_call(
            functools.partial(kernel, space_count),
            out_shape=[jax.ShapeDtypeStruct(cells, F32)] * 3,
            in_specs=[pl.BlockSpec(memory_space=pltpu.HBM)] * 5,
            out_specs=[pl.BlockSpec(memory_space=pl.ANY)] * 3,
            scratch_shapes=[
                pltpu.VMEM((PAD * LAYERS * ROWS, LANES), F32),
                pltpu.VMEM(cells, F32),
                pltpu.VMEM((KA, LAYERS + 2, ROWS + 2 * EDGE, LANES), F32),
                pltpu.VMEM((3, ENTRIES), jnp.int32),
                pltpu.VMEM((ENTRIES,), F32),
                pltpu.VMEM((LAYERS, ROWS + 2, PAD, LANES), F32),
                pltpu.VMEM((LAYERS + 2, OWN + 2, WIDE, LANES), F32),
                pltpu.VMEM((GROUPS, LAYERS, OWN * PAD, LANES), F32),
                pltpu.VMEM((LAYERS, ROWS * PAD, LANES), F32),
                pltpu.VMEM((2 * WIDE, GROUPS * 2 * WIDE), BF16),
                pltpu.VMEM((2 * WIDE, ENTRIES), BF16),
                pltpu.VMEM((GROUPS * 2 * WIDE, LAYERS * OWN * LANES), BF16),
                pltpu.VMEM((6, LAYERS, KA * OWN, LANES), F32),
                pltpu.VMEM((LAYERS + 2, KA * OWN, LANES), F32),
                pltpu.VMEM((2, LAYERS, KA * OWN, LANES), F32),
                pltpu.VMEM((KA, LAYERS, ROWS, LANES), F32),
                pltpu.VMEM((KA, PAD, LANES), F32),
                pltpu.VMEM(cells, F32),
                pltpu.VMEM(cells, F32),
                pltpu.VMEM(cells, F32),
                pltpu.SemaphoreType.DMA((5,)),
                pltpu.SemaphoreType.DMA((3,)),
            ]
            + [pltpu.SemaphoreType.DMA((GROUPS,))] * 6
            + [pltpu.SemaphoreType.DMA((2,))] * 4
            + [pltpu.SemaphoreType.DMA((GROUPS, LAYERS))] * 2,
            compiler_params=pltpu.CompilerParams(
                collective_id=0, has_side_effects=True, vmem_limit_bytes=60 * 1024 * 1024
            ),
        )(
            pressure.reshape(cells),
            source.reshape(cells),
            perm_modes,
            triples,
            coeffs,
        )
        applied = 0.5 * doubled
        relaxed = base - applied * inv
        return applied.reshape(pressure.shape), relaxed.reshape(pressure.shape)

    return jax.shard_map(
        on_device,
        mesh=mesh,
        in_specs=(
            P("modes", "space", None, None),
            P("modes", "space", None, None),
            P(None, "space", None, None),
            P(),
            P(),
        ),
        out_specs=(P("modes", "space", None, None), P("modes", "space", None, None)),
        check_vma=False,
    )
```

```python
import functools

import jax
import jax.numpy as jnp
from jax import lax
from jax.experimental import pallas as pl
from jax.experimental.pallas import tpu as pltpu
from jax.sharding import PartitionSpec as P

KA = 8
GROUPS = 8
LOCAL = 15
PAD = 16
LAYERS = 2
ROWS = 32
LANES = 128
OWN = ROWS // GROUPS
ENTRIES = 2880
LAG = 4
WAVES = 2
STEP = OWN // WAVES
COMES = ((0, 4), (4, 6))
HANDED = ((1, 4), (4, 5))
EDGE = 8
DATA = slice(EDGE, EDGE + ROWS)
WIDE = GROUPS * PAD
relax_weight = 0.8

MESH = pl.DeviceIdType.MESH
F32 = jnp.float32
BF16 = jnp.bfloat16


def kernel(
    space_count,
    p_hbm,
    s_hbm,
    a_hbm,
    tri_hbm,
    cf_hbm,
    out_a_hbm,
    out_b_hbm,
    out_i_hbm,
    p_v,
    s_v,
    a_v,
    tri_v,
    cf_v,
    t,
    q,
    r_out,
    ret,
    w_mat,
    a_hot,
    m_buf,
    w_f,
    a_str,
    a_y,
    dg,
    cdb,
    inv_v,
    base_v,
    oa_v,
    in_sem,
    out_sem,
    a2a_send,
    a2a_recv,
    low_send,
    low_recv,
    high_send,
    high_recv,
    perm_send,
    perm_recv,
    str_send,
    str_recv,
    ret_send,
    ret_recv,
):
    m = lax.axis_index("modes")
    s = lax.axis_index("space")
    has_dn = s > 0
    has_up = s < space_count - 1

    def peer_to(d):
        return lax.rem(m + d, GROUPS)

    def peer_from(d):
        return lax.rem(m + GROUPS - d, GROUPS)

    def mode_rows(g):
        return pl.ds(pl.multiple_of(g * PAD, PAD), PAD)

    barrier = pltpu.get_barrier_semaphore()
    for d in range(1, GROUPS):
        pl.semaphore_signal(barrier, inc=1, device_id=(peer_to(d), s), device_id_type=MESH)

    @pl.when(has_dn)
    def _():
        pl.semaphore_signal(barrier, inc=1, device_id=(m, s - 1), device_id_type=MESH)

    @pl.when(has_up)
    def _():
        pl.semaphore_signal(barrier, inc=1, device_id=(m, s + 1), device_id_type=MESH)

    load_p = pltpu.make_async_copy(p_hbm, p_v.at[0 : LOCAL * 64], in_sem.at[0])
    load_a = pltpu.make_async_copy(a_hbm, a_v.at[:, 1:3, DATA], in_sem.at[1])
    load_t = pltpu.make_async_copy(tri_hbm, tri_v, in_sem.at[2])
    load_c = pltpu.make_async_copy(cf_hbm, cf_v, in_sem.at[3])
    load_s = pltpu.make_async_copy(s_hbm, s_v, in_sem.at[4])
    for load in (load_p, load_a, load_t, load_c, load_s):
        load.start()

    p_v[LOCAL * 64 :, :] = jnp.zeros((64, LANES), F32)
    t[:, 0] = jnp.zeros((LAYERS, PAD, LANES), F32)
    t[:, ROWS + 1] = jnp.zeros((LAYERS, PAD, LANES), F32)
    load_p.wait()

    def stage(row, carry):
        for layer in range(LAYERS):
            for half in range(2):
                start = half * 8 * 64 + layer * ROWS + row
                t[layer, row + 1, half * 8 : half * 8 + 8, :] = p_v[pl.ds(start, 8, stride=64), :]
        return carry

    lax.fori_loop(0, ROWS, stage, 0)
    q[1:3, :, mode_rows(m), :] = t[:, pl.ds(m * OWN, OWN + 2), :, :]

    def send_block(wave, d):
        g = peer_to(d)
        first, last = COMES[wave]
        return pltpu.make_async_remote_copy(
            src_ref=t.at[:, pl.ds(g * OWN + first, last - first)],
            dst_ref=q.at[1:3, first:last, mode_rows(m), :],
            send_sem=a2a_send.at[wave, d],
            recv_sem=a2a_recv.at[wave, d],
            device_id=(g, s),
            device_id_type=MESH,
        )

    def halo(wave, d, up):
        rows = mode_rows(peer_from(d))
        first, last = HANDED[wave]
        sems = (high_send, high_recv) if up else (low_send, low_recv)
        return pltpu.make_async_remote_copy(
            src_ref=q.at[2 if up else 1, first:last, rows, :],
            dst_ref=q.at[0 if up else 3, first:last, rows, :],
            send_sem=sems[0].at[wave, d],
            recv_sem=sems[1].at[wave, d],
            device_id=(m, s + 1 if up else s - 1),
            device_id_type=MESH,
        )

    def perm_halo(up):
        return pltpu.make_async_remote_copy(
            src_ref=a_v.at[:, 2 if up else 1, DATA],
            dst_ref=a_v.at[:, 0 if up else 3, DATA],
            send_sem=perm_send.at[1 if up else 0],
            recv_sem=perm_recv.at[1 if up else 0],
            device_id=(m, s + 1 if up else s - 1),
            device_id_type=MESH,
        )

    def strip(up):
        return pltpu.make_async_remote_copy(
            src_ref=a_str.at[2 if up else 1],
            dst_ref=a_str.at[0 if up else 3],
            send_sem=str_send.at[1 if up else 0],
            recv_sem=str_recv.at[1 if up else 0],
            device_id=(m, s + 1 if up else s - 1),
            device_id_type=MESH,
        )

    def ret_rows(wave):
        return pl.ds(pl.multiple_of((m * OWN + wave * STEP) * PAD, STEP * PAD), STEP * PAD)

    def send_back(wave, d):
        g = peer_to(d)
        return pltpu.make_async_remote_copy(
            src_ref=r_out.at[g, wave],
            dst_ref=ret.at[:, ret_rows(wave), :],
            send_sem=ret_send.at[wave, d],
            recv_sem=ret_recv.at[wave, d],
            device_id=(g, s),
            device_id_type=MESH,
        )

    def both_ways(make, act):
        @pl.when(has_up)
        def _():
            getattr(make(True), act)()

        @pl.when(has_dn)
        def _():
            getattr(make(False), act)()

    def arrived(make):
        @pl.when(has_dn)
        def _():
            make(True).wait_recv()

        @pl.when(has_up)
        def _():
            make(False).wait_recv()

    load_a.wait()
    for layer in range(LAYERS):
        a_v[:, layer + 1, 0:EDGE] = jnp.zeros((KA, EDGE, LANES), F32)
        a_v[:, layer + 1, EDGE + ROWS :] = jnp.zeros((KA, EDGE, LANES), F32)
        for k in range(KA):
            to = slice(k * OWN, (k + 1) * OWN)
            a_str[layer + 1, to, :] = a_v[k, layer + 1, pl.ds(EDGE + m * OWN, OWN), :]
            a_y[0, layer, to, :] = a_v[k, layer + 1, pl.ds(EDGE + m * OWN - 1, OWN), :]
            a_y[1, layer, to, :] = a_v[k, layer + 1, pl.ds(EDGE + m * OWN + 1, OWN), :]

    neighbours = GROUPS - 1 + has_dn.astype(jnp.int32) + has_up.astype(jnp.int32)
    pl.semaphore_wait(barrier, neighbours)
    both_ways(strip, "start")
    for wave in range(WAVES):
        for d in range(1, GROUPS):
            send_block(wave, d).start()
    for wave in range(WAVES):
        both_ways(functools.partial(halo, wave, 0), "start")

    @pl.when(jnp.logical_not(has_dn))
    def _():
        q[0] = jnp.zeros(q.shape[1:], F32)
        a_v[:, 0, DATA] = jnp.zeros((KA, ROWS, LANES), F32)
        a_str[0] = jnp.zeros((KA * OWN, LANES), F32)

    @pl.when(jnp.logical_not(has_up))
    def _():
        q[3] = jnp.zeros(q.shape[1:], F32)
        a_v[:, 3, DATA] = jnp.zeros((KA, ROWS, LANES), F32)
        a_str[3] = jnp.zeros((KA * OWN, LANES), F32)

    load_t.wait()
    load_c.wait()
    mode_i = tri_v[0:1, :]
    mode_j = tri_v[1:2, :]
    mode_k = tri_v[2:3, :]
    row_i = mode_i + ((mode_i * 274) >> 12)
    col_jk = mode_j + 113 * ((mode_j * 274) >> 12) + PAD * mode_k
    cf = cf_v[...].reshape(1, ENTRIES)
    cf_hi = cf.astype(BF16).astype(F32)
    cf_lo = cf - cf_hi
    is_row = lax.broadcasted_iota(jnp.int32, (WIDE, ENTRIES), 0) == row_i
    a_hot[0:WIDE, :] = jnp.where(is_row, cf_hi, 0.0).astype(BF16)
    a_hot[WIDE:, :] = jnp.where(is_row, cf_lo, 0.0).astype(BF16)

    def table(c, carry):
        cols = lax.broadcasted_iota(jnp.int32, (2 * WIDE, ENTRIES), 0) + c * (2 * WIDE)
        b_hot = jnp.where(cols == col_jk, 1.0, 0.0).astype(BF16)
        both = lax.dot_general(
            a_hot[...], b_hot, (((1,), (1,)), ((), ())), preferred_element_type=F32
        )
        coupled = both[:WIDE] + both[WIDE:]
        for part in range(2):
            one = coupled[:, part * WIDE : (part + 1) * WIDE]
            hi = one.astype(BF16)
            lo = (one - hi.astype(F32)).astype(BF16)
            for side in range(2):
                at = pl.multiple_of(c * 4 * WIDE + (2 * part + side) * WIDE, WIDE)
                w_mat[0:WIDE, pl.ds(at, WIDE)] = hi
                w_mat[WIDE:, pl.ds(at, WIDE)] = lo
        return carry

    lax.fori_loop(0, GROUPS // 2, table, 0)

    arrived(strip)
    lane_ids = lax.broadcasted_iota(jnp.int32, (ROWS, LANES), 1)

    def beside(a):
        return (
            jnp.where(lane_ids > 0, pltpu.roll(a, 1, 1), 0.0),
            jnp.where(lane_ids < LANES - 1, pltpu.roll(a, LANES - 1, 1), 0.0),
        )

    for layer in range(LAYERS):
        a = a_str[layer + 1]
        sides = (a_str[layer], a_str[layer + 2], a_y[0, layer], a_y[1, layer]) + beside(a)
        for f, side in enumerate(sides):
            w_f[f, layer] = a + side

    def chunk(wave, d):
        g = peer_from(d)
        rows = mode_rows(g)
        lanes = lax.broadcasted_iota(jnp.int32, (PAD, LANES), 1)
        for layer in range(LAYERS):
            for r in range(wave * STEP, (wave + 1) * STEP):
                p = q[layer + 1, r + 1, rows, :]
                diffs = (
                    p - q[layer, r + 1, rows, :],
                    p - q[layer + 2, r + 1, rows, :],
                    p - q[layer + 1, r, rows, :],
                    p - q[layer + 1, r + 2, rows, :],
                    p - jnp.where(lanes > 0, pltpu.roll(p, 1, 1), 0.0),
                    p - jnp.where(lanes < LANES - 1, pltpu.roll(p, LANES - 1, 1), 0.0),
                )
                at = (wave * LAYERS * STEP + layer * STEP + r - wave * STEP) * LANES
                for k in range(KA):
                    total = None
                    for f in range(6):
                        term = w_f[f, layer, k * OWN + r : k * OWN + r + 1, :] * diffs[f]
                        total = term if total is None else total + term
                    hi = total.astype(BF16)
                    lo = (total - hi.astype(F32)).astype(BF16)
                    for part, piece in enumerate((hi, lo)):
                        to = pl.multiple_of((2 * g + part) * WIDE + k * PAD, PAD)
                        m_buf[pl.ds(to, PAD), at : at + LANES] = piece

    def step(wave, d, carry):
        @pl.when(d < GROUPS)
        def _():
            send_block(wave, d).wait_recv()
            both_ways(functools.partial(halo, wave, d), "start")

        @pl.when(d >= LAG)
        def _():
            arrived(functools.partial(halo, wave, d - LAG))
            chunk(wave, d - LAG)

        return carry

    for wave in range(WAVES):
        lax.fori_loop(1, GROUPS + LAG, functools.partial(step, wave), 0)
        if wave == WAVES - 1:
            both_ways(perm_halo, "start")
        part = LAYERS * STEP * LANES
        prod = jnp.dot(
            w_mat[...],
            m_buf[:, wave * part : (wave + 1) * part],
            preferred_element_type=F32,
        )
        prod = prod[:WIDE] + prod[WIDE:]
        for layer in range(LAYERS):
            for r in range(STEP):
                at = (layer * STEP + r) * LANES
                for go in range(GROUPS):
                    r_out[go, wave, layer, r * PAD : (r + 1) * PAD, :] = prod[
                        go * PAD : (go + 1) * PAD, at : at + LANES
                    ]
        for d in range(1, GROUPS):
            send_back(wave, d).start()
        ret[:, ret_rows(wave), :] = r_out[m, wave]

    own_cols = pl.ds(pl.multiple_of(2 * WIDE * m, 2 * WIDE), WIDE)
    own_rows = w_mat[mode_rows(m), own_cols].astype(F32) + w_mat[
        pl.ds(pl.multiple_of(WIDE + m * PAD, PAD), PAD), own_cols
    ].astype(F32)
    sub = lax.broadcasted_iota(jnp.int32, (PAD, LANES), 0)
    lane = lax.broadcasted_iota(jnp.int32, (PAD, LANES), 1)
    for k in range(KA):
        picked = jnp.where(lane == sub + k * PAD, own_rows, 0.0)
        cdb[k] = jnp.broadcast_to(jnp.sum(picked, axis=1, keepdims=True), (PAD, LANES))

    arrived(perm_halo)

    def diagonal(k, carry):
        for layer in range(LAYERS):
            a = a_v[k, layer + 1, DATA]
            sides = (
                a_v[k, layer, DATA],
                a_v[k, layer + 2, DATA],
                a_v[k, layer + 1, EDGE - 1 : EDGE - 1 + ROWS],
                a_v[k, layer + 1, EDGE + 1 : EDGE + 1 + ROWS],
            ) + beside(a)
            total = 6.0 * a
            for side in sides:
                total = total + side
            dg[k, layer] = 0.5 * total
        return carry

    lax.fori_loop(0, KA, diagonal, 0)
    load_s.wait()

    def scales(j, carry):
        for layer in range(LAYERS):
            scale = jnp.zeros((ROWS, LANES), F32)
            for k in range(KA):
                scale = scale + cdb[k, pl.ds(j, 1), :] * dg[k, layer]
            at = pl.ds(pl.multiple_of(j * 64 + layer * ROWS, ROWS), ROWS)
            inv = relax_weight / scale
            inv_v[at, :] = inv
            base_v[at, :] = p_v[at, :] + s_v[at, :] * inv
        return carry

    lax.fori_loop(0, LOCAL, scales, 0)

    def finish(layer, j, carry):
        for r8 in range(ROWS // 8):
            got = ret[layer, pl.ds(r8 * 8 * PAD + j, 8, stride=PAD), :]
            at = pl.ds(pl.multiple_of(j * 64 + layer * ROWS + r8 * 8, 8), 8)
            oa_v[at, :] = got
        return carry

    out_b = pltpu.make_async_copy(base_v, out_b_hbm, out_sem.at[0])
    out_i = pltpu.make_async_copy(inv_v, out_i_hbm, out_sem.at[1])
    out_b.start()
    out_i.start()

    for wave in range(WAVES):
        for d in range(1, GROUPS):
            send_back(wave, d).wait_recv()
    for layer in range(LAYERS):
        lax.fori_loop(0, LOCAL, functools.partial(finish, layer), 0)
    out_a = pltpu.make_async_copy(oa_v, out_a_hbm, out_sem.at[2])
    out_a.start()

    for wave in range(WAVES):
        for d in range(1, GROUPS):
            send_block(wave, d).wait_send()
            send_back(wave, d).wait_send()
        for d in range(GROUPS):
            both_ways(functools.partial(halo, wave, d), "wait_send")
    both_ways(perm_halo, "wait_send")
    both_ways(strip, "wait_send")
    out_b.wait()
    out_i.wait()
    out_a.wait()


def solution(mesh):
    space_count = mesh.shape["space"]
    cells = (LOCAL * LAYERS * ROWS, LANES)

    def on_device(pressure, source, perm_modes, triples, coeffs):
        doubled, base, inv = pl.pallas_call(
            functools.partial(kernel, space_count),
            out_shape=[jax.ShapeDtypeStruct(cells, F32)] * 3,
            in_specs=[pl.BlockSpec(memory_space=pltpu.HBM)] * 5,
            out_specs=[pl.BlockSpec(memory_space=pl.ANY)] * 3,
            scratch_shapes=[
                pltpu.VMEM((PAD * LAYERS * ROWS, LANES), F32),
                pltpu.VMEM(cells, F32),
                pltpu.VMEM((KA, LAYERS + 2, ROWS + 2 * EDGE, LANES), F32),
                pltpu.VMEM((3, ENTRIES), jnp.int32),
                pltpu.VMEM((ENTRIES,), F32),
                pltpu.VMEM((LAYERS, ROWS + 2, PAD, LANES), F32),
                pltpu.VMEM((LAYERS + 2, OWN + 2, WIDE, LANES), F32),
                pltpu.VMEM((GROUPS, WAVES, LAYERS, STEP * PAD, LANES), F32),
                pltpu.VMEM((LAYERS, ROWS * PAD, LANES), F32),
                pltpu.VMEM((2 * WIDE, GROUPS * 2 * WIDE), BF16),
                pltpu.VMEM((2 * WIDE, ENTRIES), BF16),
                pltpu.VMEM((GROUPS * 2 * WIDE, LAYERS * OWN * LANES), BF16),
                pltpu.VMEM((6, LAYERS, KA * OWN, LANES), F32),
                pltpu.VMEM((LAYERS + 2, KA * OWN, LANES), F32),
                pltpu.VMEM((2, LAYERS, KA * OWN, LANES), F32),
                pltpu.VMEM((KA, LAYERS, ROWS, LANES), F32),
                pltpu.VMEM((KA, PAD, LANES), F32),
                pltpu.VMEM(cells, F32),
                pltpu.VMEM(cells, F32),
                pltpu.VMEM(cells, F32),
                pltpu.SemaphoreType.DMA((5,)),
                pltpu.SemaphoreType.DMA((3,)),
            ]
            + [pltpu.SemaphoreType.DMA((WAVES, GROUPS))] * 6
            + [pltpu.SemaphoreType.DMA((2,))] * 4
            + [pltpu.SemaphoreType.DMA((WAVES, GROUPS))] * 2,
            compiler_params=pltpu.CompilerParams(
                collective_id=0, has_side_effects=True, vmem_limit_bytes=60 * 1024 * 1024
            ),
        )(
            pressure.reshape(cells),
            source.reshape(cells),
            perm_modes,
            triples,
            coeffs,
        )
        applied = 0.5 * doubled
        relaxed = base - applied * inv
        return applied.reshape(pressure.shape), relaxed.reshape(pressure.shape)

    return jax.shard_map(
        on_device,
        mesh=mesh,
        in_specs=(
            P("modes", "space", None, None),
            P("modes", "space", None, None),
            P(None, "space", None, None),
            P(),
            P(),
        ),
        out_specs=(P("modes", "space", None, None), P("modes", "space", None, None)),
        check_vma=False,
    )
```

```python
import functools

import jax
import jax.numpy as jnp
from jax import lax
from jax.experimental import pallas as pl
from jax.experimental.pallas import tpu as pltpu
from jax.sharding import PartitionSpec as P

KA = 8
GROUPS = 8
LOCAL = 15
PAD = 16
LAYERS = 2
ROWS = 32
LANES = 128
OWN = ROWS // GROUPS
ENTRIES = 2880
HALVES = 2
QUAD = GROUPS // HALVES
EDGE = 8
DATA = slice(EDGE, EDGE + ROWS)
WIDE = GROUPS * PAD
relax_weight = 0.8

MESH = pl.DeviceIdType.MESH
F32 = jnp.float32
BF16 = jnp.bfloat16


def kernel(
    space_count,
    p_hbm,
    s_hbm,
    a_hbm,
    tri_hbm,
    cf_hbm,
    out_a_hbm,
    out_b_hbm,
    out_i_hbm,
    p_v,
    s_v,
    a_v,
    tri_v,
    cf_v,
    t,
    q,
    r_out,
    ret,
    w_mat,
    a_hot,
    m_buf,
    w_f,
    a_str,
    a_y,
    dg,
    cdb,
    inv_v,
    base_v,
    oa_v,
    in_sem,
    out_sem,
    a2a_send,
    a2a_recv,
    low_send,
    low_recv,
    high_send,
    high_recv,
    perm_send,
    perm_recv,
    str_send,
    str_recv,
    ret_send,
    ret_recv,
):
    m = lax.axis_index("modes")
    s = lax.axis_index("space")
    has_dn = s > 0
    has_up = s < space_count - 1

    half_of = m // QUAD

    def peer_to(d):
        return lax.rem(half_of + d // QUAD, HALVES) * QUAD + lax.rem(m + d, QUAD)

    def peer_from(d):
        return lax.rem(half_of + d // QUAD, HALVES) * QUAD + lax.rem(m + GROUPS - d, QUAD)

    def mode_rows(g):
        return pl.ds(pl.multiple_of(g * PAD, PAD), PAD)

    barrier = pltpu.get_barrier_semaphore()
    for d in range(1, GROUPS):
        pl.semaphore_signal(barrier, inc=1, device_id=(peer_to(d), s), device_id_type=MESH)

    @pl.when(has_dn)
    def _():
        pl.semaphore_signal(barrier, inc=1, device_id=(m, s - 1), device_id_type=MESH)

    @pl.when(has_up)
    def _():
        pl.semaphore_signal(barrier, inc=1, device_id=(m, s + 1), device_id_type=MESH)

    load_p = pltpu.make_async_copy(p_hbm, p_v.at[0 : LOCAL * 64], in_sem.at[0])
    load_a = pltpu.make_async_copy(a_hbm, a_v.at[:, 1:3, DATA], in_sem.at[1])
    load_t = pltpu.make_async_copy(tri_hbm, tri_v, in_sem.at[2])
    load_c = pltpu.make_async_copy(cf_hbm, cf_v, in_sem.at[3])
    load_s = pltpu.make_async_copy(s_hbm, s_v, in_sem.at[4])
    for load in (load_p, load_a, load_t, load_c, load_s):
        load.start()

    p_v[LOCAL * 64 :, :] = jnp.zeros((64, LANES), F32)
    t[:, 0] = jnp.zeros((LAYERS, PAD, LANES), F32)
    t[:, ROWS + 1] = jnp.zeros((LAYERS, PAD, LANES), F32)
    load_p.wait()

    def stage(row, carry):
        for layer in range(LAYERS):
            for half in range(2):
                start = half * 8 * 64 + layer * ROWS + row
                t[layer, row + 1, half * 8 : half * 8 + 8, :] = p_v[pl.ds(start, 8, stride=64), :]
        return carry

    lax.fori_loop(0, ROWS, stage, 0)
    q[1:3, :, mode_rows(m), :] = t[:, pl.ds(m * OWN, OWN + 2), :, :]

    def send_block(d):
        g = peer_to(d)
        return pltpu.make_async_remote_copy(
            src_ref=t.at[:, pl.ds(g * OWN, OWN + 2)],
            dst_ref=q.at[1:3, :, mode_rows(m), :],
            send_sem=a2a_send.at[d],
            recv_sem=a2a_recv.at[d],
            device_id=(g, s),
            device_id_type=MESH,
        )

    def halo(part, up):
        first = lax.rem(half_of + part, HALVES) * QUAD * PAD
        rows = pl.ds(pl.multiple_of(first, QUAD * PAD), QUAD * PAD)
        sems = (high_send, high_recv) if up else (low_send, low_recv)
        return pltpu.make_async_remote_copy(
            src_ref=q.at[2 if up else 1, 1 : OWN + 1, rows, :],
            dst_ref=q.at[0 if up else 3, 1 : OWN + 1, rows, :],
            send_sem=sems[0].at[part],
            recv_sem=sems[1].at[part],
            device_id=(m, s + 1 if up else s - 1),
            device_id_type=MESH,
        )

    def perm_halo(up):
        return pltpu.make_async_remote_copy(
            src_ref=a_v.at[:, 2 if up else 1, DATA],
            dst_ref=a_v.at[:, 0 if up else 3, DATA],
            send_sem=perm_send.at[1 if up else 0],
            recv_sem=perm_recv.at[1 if up else 0],
            device_id=(m, s + 1 if up else s - 1),
            device_id_type=MESH,
        )

    def strip(up):
        return pltpu.make_async_remote_copy(
            src_ref=a_str.at[2 if up else 1],
            dst_ref=a_str.at[0 if up else 3],
            send_sem=str_send.at[1 if up else 0],
            recv_sem=str_recv.at[1 if up else 0],
            device_id=(m, s + 1 if up else s - 1),
            device_id_type=MESH,
        )

    def send_back(d):
        g = peer_to(d)
        return pltpu.make_async_remote_copy(
            src_ref=r_out.at[g],
            dst_ref=ret.at[:, pl.ds(pl.multiple_of(m * OWN * PAD, OWN * PAD), OWN * PAD), :],
            send_sem=ret_send.at[d],
            recv_sem=ret_recv.at[d],
            device_id=(g, s),
            device_id_type=MESH,
        )

    def both_ways(make, act):
        @pl.when(has_up)
        def _():
            getattr(make(True), act)()

        @pl.when(has_dn)
        def _():
            getattr(make(False), act)()

    def arrived(make):
        @pl.when(has_dn)
        def _():
            make(True).wait_recv()

        @pl.when(has_up)
        def _():
            make(False).wait_recv()

    load_a.wait()
    for layer in range(LAYERS):
        a_v[:, layer + 1, 0:EDGE] = jnp.zeros((KA, EDGE, LANES), F32)
        a_v[:, layer + 1, EDGE + ROWS :] = jnp.zeros((KA, EDGE, LANES), F32)
        for k in range(KA):
            to = slice(k * OWN, (k + 1) * OWN)
            a_str[layer + 1, to, :] = a_v[k, layer + 1, pl.ds(EDGE + m * OWN, OWN), :]
            a_y[0, layer, to, :] = a_v[k, layer + 1, pl.ds(EDGE + m * OWN - 1, OWN), :]
            a_y[1, layer, to, :] = a_v[k, layer + 1, pl.ds(EDGE + m * OWN + 1, OWN), :]

    neighbours = GROUPS - 1 + has_dn.astype(jnp.int32) + has_up.astype(jnp.int32)
    pl.semaphore_wait(barrier, neighbours)
    both_ways(strip, "start")
    for d in range(1, GROUPS):
        send_block(d).start()

    @pl.when(jnp.logical_not(has_dn))
    def _():
        q[0] = jnp.zeros(q.shape[1:], F32)
        a_v[:, 0, DATA] = jnp.zeros((KA, ROWS, LANES), F32)
        a_str[0] = jnp.zeros((KA * OWN, LANES), F32)

    @pl.when(jnp.logical_not(has_up))
    def _():
        q[3] = jnp.zeros(q.shape[1:], F32)
        a_v[:, 3, DATA] = jnp.zeros((KA, ROWS, LANES), F32)
        a_str[3] = jnp.zeros((KA * OWN, LANES), F32)

    load_t.wait()
    load_c.wait()
    mode_i = tri_v[0:1, :]
    mode_j = tri_v[1:2, :]
    mode_k = tri_v[2:3, :]
    row_i = mode_i + ((mode_i * 274) >> 12)
    col_jk = mode_j + 113 * ((mode_j * 274) >> 12) + PAD * mode_k
    cf = cf_v[...].reshape(1, ENTRIES)
    cf_hi = cf.astype(BF16).astype(F32)
    cf_lo = cf - cf_hi
    is_row = lax.broadcasted_iota(jnp.int32, (WIDE, ENTRIES), 0) == row_i
    a_hot[0:WIDE, :] = jnp.where(is_row, cf_hi, 0.0).astype(BF16)
    a_hot[WIDE:, :] = jnp.where(is_row, cf_lo, 0.0).astype(BF16)

    def table(c, carry):
        cols = lax.broadcasted_iota(jnp.int32, (2 * WIDE, ENTRIES), 0) + c * (2 * WIDE)
        b_hot = jnp.where(cols == col_jk, 1.0, 0.0).astype(BF16)
        both = lax.dot_general(
            a_hot[...], b_hot, (((1,), (1,)), ((), ())), preferred_element_type=F32
        )
        coupled = both[:WIDE] + both[WIDE:]
        for part in range(2):
            one = coupled[:, part * WIDE : (part + 1) * WIDE]
            hi = one.astype(BF16)
            lo = (one - hi.astype(F32)).astype(BF16)
            for side in range(2):
                at = pl.multiple_of(c * 4 * WIDE + (2 * part + side) * WIDE, WIDE)
                w_mat[0:WIDE, pl.ds(at, WIDE)] = hi
                w_mat[WIDE:, pl.ds(at, WIDE)] = lo
        return carry

    def hand_on(part):
        for d in range(max(part * QUAD, 1), (part + 1) * QUAD):
            send_block(d).wait_recv()
        both_ways(functools.partial(halo, part), "start")

    lax.fori_loop(0, GROUPS // 4, table, 0)
    hand_on(0)
    lax.fori_loop(GROUPS // 4, GROUPS // 2, table, 0)
    arrived(strip)
    lane_ids = lax.broadcasted_iota(jnp.int32, (ROWS, LANES), 1)

    def beside(a):
        return (
            jnp.where(lane_ids > 0, pltpu.roll(a, 1, 1), 0.0),
            jnp.where(lane_ids < LANES - 1, pltpu.roll(a, LANES - 1, 1), 0.0),
        )

    for layer in range(LAYERS):
        a = a_str[layer + 1]
        sides = (a_str[layer], a_str[layer + 2], a_y[0, layer], a_y[1, layer]) + beside(a)
        for f, side in enumerate(sides):
            w_f[f, layer] = a + side
    hand_on(1)
    both_ways(perm_halo, "start")

    def chunk(d):
        g = peer_from(d)
        rows = mode_rows(g)
        lanes = lax.broadcasted_iota(jnp.int32, (PAD, LANES), 1)
        for layer in range(LAYERS):
            for r in range(OWN):
                p = q[layer + 1, r + 1, rows, :]
                diffs = (
                    p - q[layer, r + 1, rows, :],
                    p - q[layer + 2, r + 1, rows, :],
                    p - q[layer + 1, r, rows, :],
                    p - q[layer + 1, r + 2, rows, :],
                    p - jnp.where(lanes > 0, pltpu.roll(p, 1, 1), 0.0),
                    p - jnp.where(lanes < LANES - 1, pltpu.roll(p, LANES - 1, 1), 0.0),
                )
                at = (layer * OWN + r) * LANES
                for k in range(KA):
                    total = None
                    for f in range(6):
                        term = w_f[f, layer, k * OWN + r : k * OWN + r + 1, :] * diffs[f]
                        total = term if total is None else total + term
                    hi = total.astype(BF16)
                    lo = (total - hi.astype(F32)).astype(BF16)
                    for part, piece in enumerate((hi, lo)):
                        to = pl.multiple_of((2 * g + part) * WIDE + k * PAD, PAD)
                        m_buf[pl.ds(to, PAD), at : at + LANES] = piece

    def step(d, carry):
        chunk(d)
        return carry

    for part in range(HALVES):
        arrived(functools.partial(halo, part))
        lax.fori_loop(part * QUAD, (part + 1) * QUAD, step, 0)

    for layer in range(LAYERS):
        half = OWN * LANES
        prod = jnp.dot(
            w_mat[...],
            m_buf[:, layer * half : (layer + 1) * half],
            preferred_element_type=F32,
        )
        prod = prod[:WIDE] + prod[WIDE:]
        for r in range(OWN):
            for go in range(GROUPS):
                r_out[go, layer, r * PAD : (r + 1) * PAD, :] = prod[
                    go * PAD : (go + 1) * PAD, r * LANES : (r + 1) * LANES
                ]
    for d in range(1, GROUPS):
        send_back(d).start()
    ret[:, pl.ds(pl.multiple_of(m * OWN * PAD, OWN * PAD), OWN * PAD), :] = r_out[m]

    own_cols = pl.ds(pl.multiple_of(2 * WIDE * m, 2 * WIDE), WIDE)
    own_rows = w_mat[mode_rows(m), own_cols].astype(F32) + w_mat[
        pl.ds(pl.multiple_of(WIDE + m * PAD, PAD), PAD), own_cols
    ].astype(F32)
    sub = lax.broadcasted_iota(jnp.int32, (PAD, LANES), 0)
    lane = lax.broadcasted_iota(jnp.int32, (PAD, LANES), 1)
    for k in range(KA):
        picked = jnp.where(lane == sub + k * PAD, own_rows, 0.0)
        cdb[k] = jnp.broadcast_to(jnp.sum(picked, axis=1, keepdims=True), (PAD, LANES))

    arrived(perm_halo)

    def diagonal(k, carry):
        for layer in range(LAYERS):
            a = a_v[k, layer + 1, DATA]
            sides = (
                a_v[k, layer, DATA],
                a_v[k, layer + 2, DATA],
                a_v[k, layer + 1, EDGE - 1 : EDGE - 1 + ROWS],
                a_v[k, layer + 1, EDGE + 1 : EDGE + 1 + ROWS],
            ) + beside(a)
            total = 6.0 * a
            for side in sides:
                total = total + side
            dg[k, layer] = 0.5 * total
        return carry

    lax.fori_loop(0, KA, diagonal, 0)
    load_s.wait()

    def scales(j, carry):
        for layer in range(LAYERS):
            scale = jnp.zeros((ROWS, LANES), F32)
            for k in range(KA):
                scale = scale + cdb[k, pl.ds(j, 1), :] * dg[k, layer]
            at = pl.ds(pl.multiple_of(j * 64 + layer * ROWS, ROWS), ROWS)
            inv = relax_weight / scale
            inv_v[at, :] = inv
            base_v[at, :] = p_v[at, :] + s_v[at, :] * inv
        return carry

    lax.fori_loop(0, LOCAL, scales, 0)

    def finish(layer, j, carry):
        for r8 in range(ROWS // 8):
            got = ret[layer, pl.ds(r8 * 8 * PAD + j, 8, stride=PAD), :]
            at = pl.ds(pl.multiple_of(j * 64 + layer * ROWS + r8 * 8, 8), 8)
            oa_v[at, :] = got
        return carry

    out_b = pltpu.make_async_copy(base_v, out_b_hbm, out_sem.at[0])
    out_i = pltpu.make_async_copy(inv_v, out_i_hbm, out_sem.at[1])
    out_b.start()
    out_i.start()

    for d in range(1, GROUPS):
        send_back(d).wait_recv()
    for layer in range(LAYERS):
        lax.fori_loop(0, LOCAL, functools.partial(finish, layer), 0)
    out_a = pltpu.make_async_copy(oa_v, out_a_hbm, out_sem.at[2])
    out_a.start()

    for d in range(1, GROUPS):
        send_block(d).wait_send()
        send_back(d).wait_send()
    for part in range(HALVES):
        both_ways(functools.partial(halo, part), "wait_send")
    both_ways(perm_halo, "wait_send")
    both_ways(strip, "wait_send")
    out_b.wait()
    out_i.wait()
    out_a.wait()


def solution(mesh):
    space_count = mesh.shape["space"]
    cells = (LOCAL * LAYERS * ROWS, LANES)

    def on_device(pressure, source, perm_modes, triples, coeffs):
        doubled, base, inv = pl.pallas_call(
            functools.partial(kernel, space_count),
            out_shape=[jax.ShapeDtypeStruct(cells, F32)] * 3,
            in_specs=[pl.BlockSpec(memory_space=pltpu.HBM)] * 5,
            out_specs=[pl.BlockSpec(memory_space=pl.ANY)] * 3,
            scratch_shapes=[
                pltpu.VMEM((PAD * LAYERS * ROWS, LANES), F32),
                pltpu.VMEM(cells, F32),
                pltpu.VMEM((KA, LAYERS + 2, ROWS + 2 * EDGE, LANES), F32),
                pltpu.VMEM((3, ENTRIES), jnp.int32),
                pltpu.VMEM((ENTRIES,), F32),
                pltpu.VMEM((LAYERS, ROWS + 2, PAD, LANES), F32),
                pltpu.VMEM((LAYERS + 2, OWN + 2, WIDE, LANES), F32),
                pltpu.VMEM((GROUPS, LAYERS, OWN * PAD, LANES), F32),
                pltpu.VMEM((LAYERS, ROWS * PAD, LANES), F32),
                pltpu.VMEM((2 * WIDE, GROUPS * 2 * WIDE), BF16),
                pltpu.VMEM((2 * WIDE, ENTRIES), BF16),
                pltpu.VMEM((GROUPS * 2 * WIDE, LAYERS * OWN * LANES), BF16),
                pltpu.VMEM((6, LAYERS, KA * OWN, LANES), F32),
                pltpu.VMEM((LAYERS + 2, KA * OWN, LANES), F32),
                pltpu.VMEM((2, LAYERS, KA * OWN, LANES), F32),
                pltpu.VMEM((KA, LAYERS, ROWS, LANES), F32),
                pltpu.VMEM((KA, PAD, LANES), F32),
                pltpu.VMEM(cells, F32),
                pltpu.VMEM(cells, F32),
                pltpu.VMEM(cells, F32),
                pltpu.SemaphoreType.DMA((5,)),
                pltpu.SemaphoreType.DMA((3,)),
            ]
            + [pltpu.SemaphoreType.DMA((GROUPS,))] * 2
            + [pltpu.SemaphoreType.DMA((HALVES,))] * 4
            + [pltpu.SemaphoreType.DMA((2,))] * 4
            + [pltpu.SemaphoreType.DMA((GROUPS,))] * 2,
            compiler_params=pltpu.CompilerParams(
                collective_id=0, has_side_effects=True, vmem_limit_bytes=60 * 1024 * 1024
            ),
        )(
            pressure.reshape(cells),
            source.reshape(cells),
            perm_modes,
            triples,
            coeffs,
        )
        applied = 0.5 * doubled
        relaxed = base - applied * inv
        return applied.reshape(pressure.shape), relaxed.reshape(pressure.shape)

    return jax.shard_map(
        on_device,
        mesh=mesh,
        in_specs=(
            P("modes", "space", None, None),
            P("modes", "space", None, None),
            P(None, "space", None, None),
            P(),
            P(),
        ),
        out_specs=(P("modes", "space", None, None), P("modes", "space", None, None)),
        check_vma=False,
    )
```

```python
import functools

import jax
import jax.numpy as jnp
from jax import lax
from jax.experimental import pallas as pl
from jax.experimental.pallas import tpu as pltpu
from jax.sharding import PartitionSpec as P

KA = 8
GROUPS = 8
LOCAL = 15
PAD = 16
LAYERS = 2
ROWS = 32
LANES = 128
OWN = ROWS // GROUPS
ENTRIES = 2880
HALVES = 2
QUAD = GROUPS // HALVES
RUN = 8
EDGE = 8
DATA = slice(EDGE, EDGE + ROWS)
WIDE = GROUPS * PAD
relax_weight = 0.8

MESH = pl.DeviceIdType.MESH
F32 = jnp.float32
BF16 = jnp.bfloat16


def kernel(
    space_count,
    p_hbm,
    s_hbm,
    a_hbm,
    tri_hbm,
    cf_hbm,
    out_a_hbm,
    out_b_hbm,
    out_i_hbm,
    p_v,
    s_v,
    a_v,
    tri_v,
    cf_v,
    t,
    q,
    r_out,
    ret,
    w_mat,
    a_hot,
    m_buf,
    w_f,
    a_str,
    a_y,
    dg,
    cdb,
    inv_v,
    base_v,
    oa_v,
    in_sem,
    out_sem,
    a2a_send,
    a2a_recv,
    low_send,
    low_recv,
    high_send,
    high_recv,
    perm_send,
    perm_recv,
    passing,
    pass_send,
    pass_recv,
    str_send,
    str_recv,
    ret_send,
    ret_recv,
):
    m = lax.axis_index("modes")
    s = lax.axis_index("space")
    has_dn = s > 0
    has_up = s < space_count - 1
    col = lax.rem(s, RUN)
    is_first = col == 0
    is_last = col == RUN - 1
    is_end = jnp.logical_or(is_first, is_last)
    run_up = s + RUN < space_count
    run_dn = s >= RUN
    steps_up = jnp.logical_and(is_last, has_up)
    steps_dn = jnp.logical_and(is_first, has_dn)
    passes_up = jnp.logical_and(is_first, run_up)
    passes_dn = jnp.logical_and(is_last, run_dn)

    half_of = m // QUAD

    def peer_to(d):
        return lax.rem(half_of + d // QUAD, HALVES) * QUAD + lax.rem(m + d, QUAD)

    def peer_from(d):
        return lax.rem(half_of + d // QUAD, HALVES) * QUAD + lax.rem(m + GROUPS - d, QUAD)

    def mode_rows(g):
        return pl.ds(pl.multiple_of(g * PAD, PAD), PAD)

    barrier = pltpu.get_barrier_semaphore()
    for d in range(1, GROUPS):
        pl.semaphore_signal(barrier, inc=1, device_id=(peer_to(d), s), device_id_type=MESH)

    @pl.when(has_dn)
    def _():
        pl.semaphore_signal(barrier, inc=1, device_id=(m, s - 1), device_id_type=MESH)

    @pl.when(has_up)
    def _():
        pl.semaphore_signal(barrier, inc=1, device_id=(m, s + 1), device_id_type=MESH)

    also = (
        (is_first, s + RUN - 1),
        (is_last, s - (RUN - 1)),
        (jnp.logical_and(is_end, run_up), s + RUN),
        (jnp.logical_and(is_end, run_dn), s - RUN),
    )
    for there, other in also:

        @pl.when(there)
        def _(other=other):
            pl.semaphore_signal(barrier, inc=1, device_id=(m, other), device_id_type=MESH)

    load_p = pltpu.make_async_copy(p_hbm, p_v.at[0 : LOCAL * 64], in_sem.at[0])
    load_a = pltpu.make_async_copy(a_hbm, a_v.at[:, 1:3, DATA], in_sem.at[1])
    load_t = pltpu.make_async_copy(tri_hbm, tri_v, in_sem.at[2])
    load_c = pltpu.make_async_copy(cf_hbm, cf_v, in_sem.at[3])
    load_s = pltpu.make_async_copy(s_hbm, s_v, in_sem.at[4])
    for load in (load_p, load_a, load_t, load_c, load_s):
        load.start()

    p_v[LOCAL * 64 :, :] = jnp.zeros((64, LANES), F32)
    t[:, 0] = jnp.zeros((LAYERS, PAD, LANES), F32)
    t[:, ROWS + 1] = jnp.zeros((LAYERS, PAD, LANES), F32)
    load_p.wait()

    def stage(row, carry):
        for layer in range(LAYERS):
            for half in range(2):
                start = half * 8 * 64 + layer * ROWS + row
                t[layer, row + 1, half * 8 : half * 8 + 8, :] = p_v[pl.ds(start, 8, stride=64), :]
        return carry

    lax.fori_loop(0, ROWS, stage, 0)
    q[1:3, :, mode_rows(m), :] = t[:, pl.ds(m * OWN, OWN + 2), :, :]

    def send_block(d):
        g = peer_to(d)
        return pltpu.make_async_remote_copy(
            src_ref=t.at[:, pl.ds(g * OWN, OWN + 2)],
            dst_ref=q.at[1:3, :, mode_rows(m), :],
            send_sem=a2a_send.at[d],
            recv_sem=a2a_recv.at[d],
            device_id=(g, s),
            device_id_type=MESH,
        )

    def edge(part, up):
        first = lax.rem(half_of + part, HALVES) * QUAD * PAD
        rows = pl.ds(pl.multiple_of(first, QUAD * PAD), QUAD * PAD)
        send, recv = (high_send, high_recv) if up else (low_send, low_recv)
        src = q.at[2 if up else 1, 1 : OWN + 1, rows, :]
        dst = q.at[0 if up else 3, 1 : OWN + 1, rows, :]
        return src, dst, send.at[part], recv.at[part]

    def along(src, dst, send, recv, place):
        return pltpu.make_async_remote_copy(
            src_ref=src,
            dst_ref=dst,
            send_sem=send,
            recv_sem=recv,
            device_id=(m, place),
            device_id_type=MESH,
        )

    def halo(part, up):
        return along(*edge(part, up), s + 1 if up else s - 1)

    def first_leg(up):
        src, _, send, _ = edge(0, up)
        place = s - (RUN - 1) if up else s + RUN - 1
        return along(src, passing, send, pass_recv.at[0], place)

    def second_leg(up):
        _, dst, _, recv = edge(0, up)
        return along(passing, dst, pass_send.at[0], recv, s + RUN if up else s - RUN)

    def first_half(act):
        for up, there, steps in ((True, has_up, steps_up), (False, has_dn, steps_dn)):

            @pl.when(steps)
            def _(up=up):
                getattr(first_leg(up), act)()

            @pl.when(jnp.logical_and(there, jnp.logical_not(steps)))
            def _(up=up):
                getattr(halo(0, up), act)()

    def pass_on(act):
        for up, passes in ((True, passes_up), (False, passes_dn)):

            @pl.when(passes)
            def _(up=up):
                if act == "start":
                    first_leg(up).wait_recv()
                getattr(second_leg(up), act)()

    def perm_halo(up):
        return pltpu.make_async_remote_copy(
            src_ref=a_v.at[:, 2 if up else 1, DATA],
            dst_ref=a_v.at[:, 0 if up else 3, DATA],
            send_sem=perm_send.at[1 if up else 0],
            recv_sem=perm_recv.at[1 if up else 0],
            device_id=(m, s + 1 if up else s - 1),
            device_id_type=MESH,
        )

    def strip(up):
        return pltpu.make_async_remote_copy(
            src_ref=a_str.at[2 if up else 1],
            dst_ref=a_str.at[0 if up else 3],
            send_sem=str_send.at[1 if up else 0],
            recv_sem=str_recv.at[1 if up else 0],
            device_id=(m, s + 1 if up else s - 1),
            device_id_type=MESH,
        )

    def send_back(d):
        g = peer_to(d)
        return pltpu.make_async_remote_copy(
            src_ref=r_out.at[g],
            dst_ref=ret.at[:, pl.ds(pl.multiple_of(m * OWN * PAD, OWN * PAD), OWN * PAD), :],
            send_sem=ret_send.at[d],
            recv_sem=ret_recv.at[d],
            device_id=(g, s),
            device_id_type=MESH,
        )

    def both_ways(make, act):
        @pl.when(has_up)
        def _():
            getattr(make(True), act)()

        @pl.when(has_dn)
        def _():
            getattr(make(False), act)()

    def arrived(make):
        @pl.when(has_dn)
        def _():
            make(True).wait_recv()

        @pl.when(has_up)
        def _():
            make(False).wait_recv()

    load_a.wait()
    for layer in range(LAYERS):
        a_v[:, layer + 1, 0:EDGE] = jnp.zeros((KA, EDGE, LANES), F32)
        a_v[:, layer + 1, EDGE + ROWS :] = jnp.zeros((KA, EDGE, LANES), F32)
        for k in range(KA):
            to = slice(k * OWN, (k + 1) * OWN)
            a_str[layer + 1, to, :] = a_v[k, layer + 1, pl.ds(EDGE + m * OWN, OWN), :]
            a_y[0, layer, to, :] = a_v[k, layer + 1, pl.ds(EDGE + m * OWN - 1, OWN), :]
            a_y[1, layer, to, :] = a_v[k, layer + 1, pl.ds(EDGE + m * OWN + 1, OWN), :]

    neighbours = GROUPS - 1 + has_dn.astype(jnp.int32) + has_up.astype(jnp.int32)
    for there, _ in also:
        neighbours = neighbours + there.astype(jnp.int32)
    pl.semaphore_wait(barrier, neighbours)
    both_ways(strip, "start")
    for d in range(1, GROUPS):
        send_block(d).start()

    @pl.when(jnp.logical_not(has_dn))
    def _():
        q[0] = jnp.zeros(q.shape[1:], F32)
        a_v[:, 0, DATA] = jnp.zeros((KA, ROWS, LANES), F32)
        a_str[0] = jnp.zeros((KA * OWN, LANES), F32)

    @pl.when(jnp.logical_not(has_up))
    def _():
        q[3] = jnp.zeros(q.shape[1:], F32)
        a_v[:, 3, DATA] = jnp.zeros((KA, ROWS, LANES), F32)
        a_str[3] = jnp.zeros((KA * OWN, LANES), F32)

    load_t.wait()
    load_c.wait()
    mode_i = tri_v[0:1, :]
    mode_j = tri_v[1:2, :]
    mode_k = tri_v[2:3, :]
    row_i = mode_i + ((mode_i * 274) >> 12)
    col_jk = mode_j + 113 * ((mode_j * 274) >> 12) + PAD * mode_k
    cf = cf_v[...].reshape(1, ENTRIES)
    cf_hi = cf.astype(BF16).astype(F32)
    cf_lo = cf - cf_hi
    is_row = lax.broadcasted_iota(jnp.int32, (WIDE, ENTRIES), 0) == row_i
    a_hot[0:WIDE, :] = jnp.where(is_row, cf_hi, 0.0).astype(BF16)
    a_hot[WIDE:, :] = jnp.where(is_row, cf_lo, 0.0).astype(BF16)

    def table(c, carry):
        cols = lax.broadcasted_iota(jnp.int32, (2 * WIDE, ENTRIES), 0) + c * (2 * WIDE)
        b_hot = jnp.where(cols == col_jk, 1.0, 0.0).astype(BF16)
        both = lax.dot_general(
            a_hot[...], b_hot, (((1,), (1,)), ((), ())), preferred_element_type=F32
        )
        coupled = both[:WIDE] + both[WIDE:]
        for part in range(2):
            one = coupled[:, part * WIDE : (part + 1) * WIDE]
            hi = one.astype(BF16)
            lo = (one - hi.astype(F32)).astype(BF16)
            for side in range(2):
                at = pl.multiple_of(c * 4 * WIDE + (2 * part + side) * WIDE, WIDE)
                w_mat[0:WIDE, pl.ds(at, WIDE)] = hi
                w_mat[WIDE:, pl.ds(at, WIDE)] = lo
        return carry

    def hand_on(part):
        for d in range(max(part * QUAD, 1), (part + 1) * QUAD):
            send_block(d).wait_recv()
        if part == 0:
            first_half("start")
        else:
            both_ways(functools.partial(halo, part), "start")

    lax.fori_loop(0, GROUPS // 4, table, 0)
    hand_on(0)
    lax.fori_loop(GROUPS // 4, GROUPS // 2, table, 0)
    arrived(strip)
    lane_ids = lax.broadcasted_iota(jnp.int32, (ROWS, LANES), 1)

    def beside(a):
        return (
            jnp.where(lane_ids > 0, pltpu.roll(a, 1, 1), 0.0),
            jnp.where(lane_ids < LANES - 1, pltpu.roll(a, LANES - 1, 1), 0.0),
        )

    for layer in range(LAYERS):
        a = a_str[layer + 1]
        sides = (a_str[layer], a_str[layer + 2], a_y[0, layer], a_y[1, layer]) + beside(a)
        for f, side in enumerate(sides):
            w_f[f, layer] = a + side
    pass_on("start")
    hand_on(1)

    def chunk(d):
        g = peer_from(d)
        rows = mode_rows(g)
        lanes = lax.broadcasted_iota(jnp.int32, (PAD, LANES), 1)
        for layer in range(LAYERS):
            for r in range(OWN):
                p = q[layer + 1, r + 1, rows, :]
                diffs = (
                    p - q[layer, r + 1, rows, :],
                    p - q[layer + 2, r + 1, rows, :],
                    p - q[layer + 1, r, rows, :],
                    p - q[layer + 1, r + 2, rows, :],
                    p - jnp.where(lanes > 0, pltpu.roll(p, 1, 1), 0.0),
                    p - jnp.where(lanes < LANES - 1, pltpu.roll(p, LANES - 1, 1), 0.0),
                )
                at = (layer * OWN + r) * LANES
                for k in range(KA):
                    total = None
                    for f in range(6):
                        term = w_f[f, layer, k * OWN + r : k * OWN + r + 1, :] * diffs[f]
                        total = term if total is None else total + term
                    hi = total.astype(BF16)
                    lo = (total - hi.astype(F32)).astype(BF16)
                    for part, piece in enumerate((hi, lo)):
                        to = pl.multiple_of((2 * g + part) * WIDE + k * PAD, PAD)
                        m_buf[pl.ds(to, PAD), at : at + LANES] = piece

    def step(d, carry):
        chunk(d)
        return carry

    for part in range(HALVES):
        arrived(functools.partial(halo, part))
        if part == HALVES - 1:
            both_ways(perm_halo, "start")
        lax.fori_loop(part * QUAD, (part + 1) * QUAD, step, 0)

    for layer in range(LAYERS):
        half = OWN * LANES
        prod = jnp.dot(
            w_mat[...],
            m_buf[:, layer * half : (layer + 1) * half],
            preferred_element_type=F32,
        )
        prod = prod[:WIDE] + prod[WIDE:]
        for r in range(OWN):
            for go in range(GROUPS):
                r_out[go, layer, r * PAD : (r + 1) * PAD, :] = prod[
                    go * PAD : (go + 1) * PAD, r * LANES : (r + 1) * LANES
                ]
    for d in range(1, GROUPS):
        send_back(d).start()
    ret[:, pl.ds(pl.multiple_of(m * OWN * PAD, OWN * PAD), OWN * PAD), :] = r_out[m]

    own_cols = pl.ds(pl.multiple_of(2 * WIDE * m, 2 * WIDE), WIDE)
    own_rows = w_mat[mode_rows(m), own_cols].astype(F32) + w_mat[
        pl.ds(pl.multiple_of(WIDE + m * PAD, PAD), PAD), own_cols
    ].astype(F32)
    sub = lax.broadcasted_iota(jnp.int32, (PAD, LANES), 0)
    lane = lax.broadcasted_iota(jnp.int32, (PAD, LANES), 1)
    for k in range(KA):
        picked = jnp.where(lane == sub + k * PAD, own_rows, 0.0)
        cdb[k] = jnp.broadcast_to(jnp.sum(picked, axis=1, keepdims=True), (PAD, LANES))

    arrived(perm_halo)

    def diagonal(k, carry):
        for layer in range(LAYERS):
            a = a_v[k, layer + 1, DATA]
            sides = (
                a_v[k, layer, DATA],
                a_v[k, layer + 2, DATA],
                a_v[k, layer + 1, EDGE - 1 : EDGE - 1 + ROWS],
                a_v[k, layer + 1, EDGE + 1 : EDGE + 1 + ROWS],
            ) + beside(a)
            total = 6.0 * a
            for side in sides:
                total = total + side
            dg[k, layer] = 0.5 * total
        return carry

    lax.fori_loop(0, KA, diagonal, 0)
    load_s.wait()

    def scales(j, carry):
        for layer in range(LAYERS):
            scale = jnp.zeros((ROWS, LANES), F32)
            for k in range(KA):
                scale = scale + cdb[k, pl.ds(j, 1), :] * dg[k, layer]
            at = pl.ds(pl.multiple_of(j * 64 + layer * ROWS, ROWS), ROWS)
            inv = relax_weight / scale
            inv_v[at, :] = inv
            base_v[at, :] = p_v[at, :] + s_v[at, :] * inv
        return carry

    lax.fori_loop(0, LOCAL, scales, 0)

    def finish(layer, j, carry):
        for r8 in range(ROWS // 8):
            got = ret[layer, pl.ds(r8 * 8 * PAD + j, 8, stride=PAD), :]
            at = pl.ds(pl.multiple_of(j * 64 + layer * ROWS + r8 * 8, 8), 8)
            oa_v[at, :] = got
        return carry

    out_b = pltpu.make_async_copy(base_v, out_b_hbm, out_sem.at[0])
    out_i = pltpu.make_async_copy(inv_v, out_i_hbm, out_sem.at[1])
    out_b.start()
    out_i.start()

    for d in range(1, GROUPS):
        send_back(d).wait_recv()
    for layer in range(LAYERS):
        lax.fori_loop(0, LOCAL, functools.partial(finish, layer), 0)
    out_a = pltpu.make_async_copy(oa_v, out_a_hbm, out_sem.at[2])
    out_a.start()

    for d in range(1, GROUPS):
        send_block(d).wait_send()
        send_back(d).wait_send()
    first_half("wait_send")
    pass_on("wait_send")
    both_ways(functools.partial(halo, 1), "wait_send")
    both_ways(perm_halo, "wait_send")
    both_ways(strip, "wait_send")
    out_b.wait()
    out_i.wait()
    out_a.wait()


def solution(mesh):
    space_count = mesh.shape["space"]
    cells = (LOCAL * LAYERS * ROWS, LANES)

    def on_device(pressure, source, perm_modes, triples, coeffs):
        doubled, base, inv = pl.pallas_call(
            functools.partial(kernel, space_count),
            out_shape=[jax.ShapeDtypeStruct(cells, F32)] * 3,
            in_specs=[pl.BlockSpec(memory_space=pltpu.HBM)] * 5,
            out_specs=[pl.BlockSpec(memory_space=pl.ANY)] * 3,
            scratch_shapes=[
                pltpu.VMEM((PAD * LAYERS * ROWS, LANES), F32),
                pltpu.VMEM(cells, F32),
                pltpu.VMEM((KA, LAYERS + 2, ROWS + 2 * EDGE, LANES), F32),
                pltpu.VMEM((3, ENTRIES), jnp.int32),
                pltpu.VMEM((ENTRIES,), F32),
                pltpu.VMEM((LAYERS, ROWS + 2, PAD, LANES), F32),
                pltpu.VMEM((LAYERS + 2, OWN + 2, WIDE, LANES), F32),
                pltpu.VMEM((GROUPS, LAYERS, OWN * PAD, LANES), F32),
                pltpu.VMEM((LAYERS, ROWS * PAD, LANES), F32),
                pltpu.VMEM((2 * WIDE, GROUPS * 2 * WIDE), BF16),
                pltpu.VMEM((2 * WIDE, ENTRIES), BF16),
                pltpu.VMEM((GROUPS * 2 * WIDE, LAYERS * OWN * LANES), BF16),
                pltpu.VMEM((6, LAYERS, KA * OWN, LANES), F32),
                pltpu.VMEM((LAYERS + 2, KA * OWN, LANES), F32),
                pltpu.VMEM((2, LAYERS, KA * OWN, LANES), F32),
                pltpu.VMEM((KA, LAYERS, ROWS, LANES), F32),
                pltpu.VMEM((KA, PAD, LANES), F32),
                pltpu.VMEM(cells, F32),
                pltpu.VMEM(cells, F32),
                pltpu.VMEM(cells, F32),
                pltpu.SemaphoreType.DMA((5,)),
                pltpu.SemaphoreType.DMA((3,)),
            ]
            + [pltpu.SemaphoreType.DMA((GROUPS,))] * 2
            + [pltpu.SemaphoreType.DMA((HALVES,))] * 4
            + [pltpu.SemaphoreType.DMA((2,))] * 2
            + [pltpu.VMEM((OWN, QUAD * PAD, LANES), F32)]
            + [pltpu.SemaphoreType.DMA((1,))] * 2
            + [pltpu.SemaphoreType.DMA((2,))] * 2
            + [pltpu.SemaphoreType.DMA((GROUPS,))] * 2,
            compiler_params=pltpu.CompilerParams(
                collective_id=0, has_side_effects=True, vmem_limit_bytes=60 * 1024 * 1024
            ),
        )(
            pressure.reshape(cells),
            source.reshape(cells),
            perm_modes,
            triples,
            coeffs,
        )
        applied = 0.5 * doubled
        relaxed = base - applied * inv
        return applied.reshape(pressure.shape), relaxed.reshape(pressure.shape)

    return jax.shard_map(
        on_device,
        mesh=mesh,
        in_specs=(
            P("modes", "space", None, None),
            P("modes", "space", None, None),
            P(None, "space", None, None),
            P(),
            P(),
        ),
        out_specs=(P("modes", "space", None, None), P("modes", "space", None, None)),
        check_vma=False,
    )
```

```python
import functools

import jax
import jax.numpy as jnp
from jax import lax
from jax.experimental import pallas as pl
from jax.experimental.pallas import tpu as pltpu
from jax.sharding import PartitionSpec as P

KA = 8
GROUPS = 8
LOCAL = 15
PAD = 16
LAYERS = 2
ROWS = 32
LANES = 128
OWN = ROWS // GROUPS
ENTRIES = 2880
HALVES = 2
QUAD = GROUPS // HALVES
EDGE = 8
DATA = slice(EDGE, EDGE + ROWS)
WIDE = GROUPS * PAD
relax_weight = 0.8

MESH = pl.DeviceIdType.MESH
F32 = jnp.float32
BF16 = jnp.bfloat16


def kernel(
    space_count,
    p_hbm,
    s_hbm,
    a_hbm,
    tri_hbm,
    cf_hbm,
    out_a_hbm,
    out_b_hbm,
    out_i_hbm,
    p_v,
    s_v,
    a_v,
    tri_v,
    cf_v,
    t,
    q,
    r_out,
    ret,
    w_mat,
    a_hot,
    m_buf,
    w_f,
    a_str,
    a_y,
    dg,
    cdb,
    inv_v,
    base_v,
    oa_v,
    in_sem,
    out_sem,
    a2a_send,
    a2a_recv,
    low_send,
    low_recv,
    high_send,
    high_recv,
    far_send,
    far_recv,
    row_send,
    row_recv,
    perm_send,
    perm_recv,
    str_send,
    str_recv,
    ret_send,
    ret_recv,
):
    m = lax.axis_index("modes")
    s = lax.axis_index("space")
    has_dn = s > 0
    has_up = s < space_count - 1

    half_of = m // QUAD

    def peer_to(d):
        return lax.rem(half_of + d // QUAD, HALVES) * QUAD + lax.rem(m + d, QUAD)

    def peer_from(d):
        return lax.rem(half_of + d // QUAD, HALVES) * QUAD + lax.rem(m + GROUPS - d, QUAD)

    def block_of(g):
        return jnp.where(g < QUAD, g, GROUPS + QUAD - 1 - g)

    block = block_of(m)
    turned = half_of == 1
    ahead = lax.rem(m, QUAD) < QUAD - 1
    behind = lax.rem(m, QUAD) > 0
    row_up, row_up_to = jnp.where(turned, 1, OWN), jnp.where(turned, OWN + 1, 0)
    row_dn, row_dn_to = jnp.where(turned, OWN, 1), jnp.where(turned, 0, OWN + 1)

    row_dn_to_far = jnp.where(turned, 0, OWN + 1)

    def far_row(b):
        return jnp.where(b == QUAD, QUAD * OWN, QUAD * OWN + 1)

    def mode_rows(g):
        return pl.ds(pl.multiple_of(g * PAD, PAD), PAD)

    barrier = pltpu.get_barrier_semaphore()
    for d in range(1, GROUPS):
        pl.semaphore_signal(barrier, inc=1, device_id=(peer_to(d), s), device_id_type=MESH)

    @pl.when(has_dn)
    def _():
        pl.semaphore_signal(barrier, inc=1, device_id=(m, s - 1), device_id_type=MESH)

    @pl.when(has_up)
    def _():
        pl.semaphore_signal(barrier, inc=1, device_id=(m, s + 1), device_id_type=MESH)

    load_p = pltpu.make_async_copy(p_hbm, p_v.at[0 : LOCAL * 64], in_sem.at[0])
    load_a = pltpu.make_async_copy(a_hbm, a_v.at[:, 1:3, DATA], in_sem.at[1])
    load_t = pltpu.make_async_copy(tri_hbm, tri_v, in_sem.at[2])
    load_c = pltpu.make_async_copy(cf_hbm, cf_v, in_sem.at[3])
    load_s = pltpu.make_async_copy(s_hbm, s_v, in_sem.at[4])
    for load in (load_p, load_a, load_t, load_c, load_s):
        load.start()

    p_v[LOCAL * 64 :, :] = jnp.zeros((64, LANES), F32)
    t[:, 0] = jnp.zeros((LAYERS, PAD, LANES), F32)
    t[:, ROWS + 1] = jnp.zeros((LAYERS, PAD, LANES), F32)
    load_p.wait()

    def stage(row, carry):
        for layer in range(LAYERS):
            for half in range(2):
                start = half * 8 * 64 + layer * ROWS + row
                t[layer, row + 1, half * 8 : half * 8 + 8, :] = p_v[pl.ds(start, 8, stride=64), :]
        return carry

    lax.fori_loop(0, ROWS, stage, 0)
    q[1:3, 1 : OWN + 1, mode_rows(m), :] = t[:, pl.ds(block * OWN + 1, OWN), :, :]

    @pl.when(jnp.logical_not(ahead))
    def _():
        q[1:3, pl.ds(row_dn_to_far, 1), mode_rows(m), :] = t[:, pl.ds(far_row(block), 1), :, :]

    @pl.when(jnp.logical_not(behind))
    def _():
        q[1:3, pl.ds(row_up_to, 1), :, :] = jnp.zeros((LAYERS, 1, WIDE, LANES), F32)

    def send_block(d):
        g = peer_to(d)
        return pltpu.make_async_remote_copy(
            src_ref=t.at[:, pl.ds(block_of(g) * OWN + 1, OWN)],
            dst_ref=q.at[1:3, 1 : OWN + 1, mode_rows(m), :],
            send_sem=a2a_send.at[d],
            recv_sem=a2a_recv.at[d],
            device_id=(g, s),
            device_id_type=MESH,
        )

    def send_far(d):
        g = peer_to(d)
        b = block_of(g)
        to = jnp.where(b == QUAD, 0, OWN + 1)
        return pltpu.make_async_remote_copy(
            src_ref=t.at[:, pl.ds(far_row(b), 1)],
            dst_ref=q.at[1:3, pl.ds(to, 1), mode_rows(m), :],
            send_sem=far_send.at[d],
            recv_sem=far_recv.at[d],
            device_id=(g, s),
            device_id_type=MESH,
        )

    def is_middle(d):
        b = block_of(peer_to(d))
        return jnp.logical_or(b == QUAD - 1, b == QUAD)

    def halves(part):
        first = lax.rem(half_of + part, HALVES) * QUAD * PAD
        return pl.ds(pl.multiple_of(first, QUAD * PAD), QUAD * PAD)

    def row_halo(part, up):
        src, dst = (row_up, row_up_to) if up else (row_dn, row_dn_to)
        return pltpu.make_async_remote_copy(
            src_ref=q.at[1:3, pl.ds(src, 1), halves(part), :],
            dst_ref=q.at[1:3, pl.ds(dst, 1), halves(part), :],
            send_sem=row_send.at[part, 1 if up else 0],
            recv_sem=row_recv.at[part, 1 if up else 0],
            device_id=(m + 1 if up else m - 1, s),
            device_id_type=MESH,
        )

    def rows_out(part, act):
        @pl.when(ahead)
        def _():
            getattr(row_halo(part, True), act)()

        @pl.when(behind)
        def _():
            getattr(row_halo(part, False), act)()

    def rows_in(part):
        @pl.when(behind)
        def _():
            row_halo(part, True).wait_recv()

        @pl.when(ahead)
        def _():
            row_halo(part, False).wait_recv()

        @pl.when(jnp.logical_not(ahead))
        def _():
            for d in range(max(part * QUAD, 1), (part + 1) * QUAD):
                send_far(d).wait_recv()

    def halo(part, up):
        rows = halves(part)
        sems = (high_send, high_recv) if up else (low_send, low_recv)
        return pltpu.make_async_remote_copy(
            src_ref=q.at[2 if up else 1, 1 : OWN + 1, rows, :],
            dst_ref=q.at[0 if up else 3, 1 : OWN + 1, rows, :],
            send_sem=sems[0].at[part],
            recv_sem=sems[1].at[part],
            device_id=(m, s + 1 if up else s - 1),
            device_id_type=MESH,
        )

    def perm_halo(up):
        return pltpu.make_async_remote_copy(
            src_ref=a_v.at[:, 2 if up else 1, DATA],
            dst_ref=a_v.at[:, 0 if up else 3, DATA],
            send_sem=perm_send.at[1 if up else 0],
            recv_sem=perm_recv.at[1 if up else 0],
            device_id=(m, s + 1 if up else s - 1),
            device_id_type=MESH,
        )

    def strip(up):
        return pltpu.make_async_remote_copy(
            src_ref=a_str.at[2 if up else 1],
            dst_ref=a_str.at[0 if up else 3],
            send_sem=str_send.at[1 if up else 0],
            recv_sem=str_recv.at[1 if up else 0],
            device_id=(m, s + 1 if up else s - 1),
            device_id_type=MESH,
        )

    own_rows_back = pl.ds(pl.multiple_of(block * OWN * PAD, OWN * PAD), OWN * PAD)

    def send_back(d):
        g = peer_to(d)
        return pltpu.make_async_remote_copy(
            src_ref=r_out.at[g],
            dst_ref=ret.at[:, own_rows_back, :],
            send_sem=ret_send.at[d],
            recv_sem=ret_recv.at[d],
            device_id=(g, s),
            device_id_type=MESH,
        )

    def both_ways(make, act):
        @pl.when(has_up)
        def _():
            getattr(make(True), act)()

        @pl.when(has_dn)
        def _():
            getattr(make(False), act)()

    def arrived(make):
        @pl.when(has_dn)
        def _():
            make(True).wait_recv()

        @pl.when(has_up)
        def _():
            make(False).wait_recv()

    load_a.wait()
    for layer in range(LAYERS):
        a_v[:, layer + 1, 0:EDGE] = jnp.zeros((KA, EDGE, LANES), F32)
        a_v[:, layer + 1, EDGE + ROWS :] = jnp.zeros((KA, EDGE, LANES), F32)
        for k in range(KA):
            to = slice(k * OWN, (k + 1) * OWN)
            a_str[layer + 1, to, :] = a_v[k, layer + 1, pl.ds(EDGE + block * OWN, OWN), :]
            a_y[0, layer, to, :] = a_v[k, layer + 1, pl.ds(EDGE + block * OWN - 1, OWN), :]
            a_y[1, layer, to, :] = a_v[k, layer + 1, pl.ds(EDGE + block * OWN + 1, OWN), :]

    neighbours = GROUPS - 1 + has_dn.astype(jnp.int32) + has_up.astype(jnp.int32)
    pl.semaphore_wait(barrier, neighbours)
    both_ways(strip, "start")
    for d in range(1, GROUPS):
        send_block(d).start()

        @pl.when(is_middle(d))
        def _(d=d):
            send_far(d).start()


    @pl.when(jnp.logical_not(has_dn))
    def _():
        q[0] = jnp.zeros(q.shape[1:], F32)
        a_v[:, 0, DATA] = jnp.zeros((KA, ROWS, LANES), F32)
        a_str[0] = jnp.zeros((KA * OWN, LANES), F32)

    @pl.when(jnp.logical_not(has_up))
    def _():
        q[3] = jnp.zeros(q.shape[1:], F32)
        a_v[:, 3, DATA] = jnp.zeros((KA, ROWS, LANES), F32)
        a_str[3] = jnp.zeros((KA * OWN, LANES), F32)

    load_t.wait()
    load_c.wait()
    mode_i = tri_v[0:1, :]
    mode_j = tri_v[1:2, :]
    mode_k = tri_v[2:3, :]
    row_i = mode_i + ((mode_i * 274) >> 12)
    col_jk = mode_j + 113 * ((mode_j * 274) >> 12) + PAD * mode_k
    cf = cf_v[...].reshape(1, ENTRIES)
    cf_hi = cf.astype(BF16).astype(F32)
    cf_lo = cf - cf_hi
    is_row = lax.broadcasted_iota(jnp.int32, (WIDE, ENTRIES), 0) == row_i
    a_hot[0:WIDE, :] = jnp.where(is_row, cf_hi, 0.0).astype(BF16)
    a_hot[WIDE:, :] = jnp.where(is_row, cf_lo, 0.0).astype(BF16)

    def table(c, carry):
        cols = lax.broadcasted_iota(jnp.int32, (2 * WIDE, ENTRIES), 0) + c * (2 * WIDE)
        b_hot = jnp.where(cols == col_jk, 1.0, 0.0).astype(BF16)
        both = lax.dot_general(
            a_hot[...], b_hot, (((1,), (1,)), ((), ())), preferred_element_type=F32
        )
        coupled = both[:WIDE] + both[WIDE:]
        for part in range(2):
            one = coupled[:, part * WIDE : (part + 1) * WIDE]
            hi = one.astype(BF16)
            lo = (one - hi.astype(F32)).astype(BF16)
            for side in range(2):
                at = pl.multiple_of(c * 4 * WIDE + (2 * part + side) * WIDE, WIDE)
                w_mat[0:WIDE, pl.ds(at, WIDE)] = hi
                w_mat[WIDE:, pl.ds(at, WIDE)] = lo
        return carry

    def hand_on(part):
        for d in range(max(part * QUAD, 1), (part + 1) * QUAD):
            send_block(d).wait_recv()
        both_ways(functools.partial(halo, part), "start")
        rows_out(part, "start")

    lax.fori_loop(0, GROUPS // 4, table, 0)
    hand_on(0)
    lax.fori_loop(GROUPS // 4, GROUPS // 2, table, 0)
    arrived(strip)
    lane_ids = lax.broadcasted_iota(jnp.int32, (ROWS, LANES), 1)

    def beside(a):
        return (
            jnp.where(lane_ids > 0, pltpu.roll(a, 1, 1), 0.0),
            jnp.where(lane_ids < LANES - 1, pltpu.roll(a, LANES - 1, 1), 0.0),
        )

    for layer in range(LAYERS):
        a = a_str[layer + 1]
        sides = (a_str[layer], a_str[layer + 2], a_y[0, layer], a_y[1, layer]) + beside(a)
        for f, side in enumerate(sides):
            w_f[f, layer] = a + side
    hand_on(1)

    def chunk(d):
        g = peer_from(d)
        rows = mode_rows(g)
        lanes = lax.broadcasted_iota(jnp.int32, (PAD, LANES), 1)
        for layer in range(LAYERS):
            for r in range(OWN):
                p = q[layer + 1, r + 1, rows, :]
                diffs = (
                    p - q[layer, r + 1, rows, :],
                    p - q[layer + 2, r + 1, rows, :],
                    p - q[layer + 1, r, rows, :],
                    p - q[layer + 1, r + 2, rows, :],
                    p - jnp.where(lanes > 0, pltpu.roll(p, 1, 1), 0.0),
                    p - jnp.where(lanes < LANES - 1, pltpu.roll(p, LANES - 1, 1), 0.0),
                )
                at = (layer * OWN + r) * LANES
                for k in range(KA):
                    total = None
                    for f in range(6):
                        term = w_f[f, layer, k * OWN + r : k * OWN + r + 1, :] * diffs[f]
                        total = term if total is None else total + term
                    hi = total.astype(BF16)
                    lo = (total - hi.astype(F32)).astype(BF16)
                    for part, piece in enumerate((hi, lo)):
                        to = pl.multiple_of((2 * g + part) * WIDE + k * PAD, PAD)
                        m_buf[pl.ds(to, PAD), at : at + LANES] = piece

    def step(d, carry):
        chunk(d)
        return carry

    for part in range(HALVES):
        rows_in(part)
        arrived(functools.partial(halo, part))
        if part == HALVES - 1:
            both_ways(perm_halo, "start")
        lax.fori_loop(part * QUAD, (part + 1) * QUAD, step, 0)

    for layer in range(LAYERS):
        half = OWN * LANES
        prod = jnp.dot(
            w_mat[...],
            m_buf[:, layer * half : (layer + 1) * half],
            preferred_element_type=F32,
        )
        prod = prod[:WIDE] + prod[WIDE:]
        for r in range(OWN):
            for go in range(GROUPS):
                r_out[go, layer, r * PAD : (r + 1) * PAD, :] = prod[
                    go * PAD : (go + 1) * PAD, r * LANES : (r + 1) * LANES
                ]
    for d in range(1, GROUPS):
        send_back(d).start()
    ret[:, own_rows_back, :] = r_out[m]

    own_cols = pl.ds(pl.multiple_of(2 * WIDE * m, 2 * WIDE), WIDE)
    own_rows = w_mat[mode_rows(m), own_cols].astype(F32) + w_mat[
        pl.ds(pl.multiple_of(WIDE + m * PAD, PAD), PAD), own_cols
    ].astype(F32)
    sub = lax.broadcasted_iota(jnp.int32, (PAD, LANES), 0)
    lane = lax.broadcasted_iota(jnp.int32, (PAD, LANES), 1)
    for k in range(KA):
        picked = jnp.where(lane == sub + k * PAD, own_rows, 0.0)
        cdb[k] = jnp.broadcast_to(jnp.sum(picked, axis=1, keepdims=True), (PAD, LANES))

    arrived(perm_halo)

    def diagonal(k, carry):
        for layer in range(LAYERS):
            a = a_v[k, layer + 1, DATA]
            sides = (
                a_v[k, layer, DATA],
                a_v[k, layer + 2, DATA],
                a_v[k, layer + 1, EDGE - 1 : EDGE - 1 + ROWS],
                a_v[k, layer + 1, EDGE + 1 : EDGE + 1 + ROWS],
            ) + beside(a)
            total = 6.0 * a
            for side in sides:
                total = total + side
            dg[k, layer] = 0.5 * total
        return carry

    lax.fori_loop(0, KA, diagonal, 0)
    load_s.wait()

    def scales(j, carry):
        for layer in range(LAYERS):
            scale = jnp.zeros((ROWS, LANES), F32)
            for k in range(KA):
                scale = scale + cdb[k, pl.ds(j, 1), :] * dg[k, layer]
            at = pl.ds(pl.multiple_of(j * 64 + layer * ROWS, ROWS), ROWS)
            inv = relax_weight / scale
            inv_v[at, :] = inv
            base_v[at, :] = p_v[at, :] + s_v[at, :] * inv
        return carry

    lax.fori_loop(0, LOCAL, scales, 0)

    def finish(layer, j, carry):
        for r8 in range(ROWS // 8):
            got = ret[layer, pl.ds(r8 * 8 * PAD + j, 8, stride=PAD), :]
            at = pl.ds(pl.multiple_of(j * 64 + layer * ROWS + r8 * 8, 8), 8)
            oa_v[at, :] = got
        return carry

    out_b = pltpu.make_async_copy(base_v, out_b_hbm, out_sem.at[0])
    out_i = pltpu.make_async_copy(inv_v, out_i_hbm, out_sem.at[1])
    out_b.start()
    out_i.start()

    for d in range(1, GROUPS):
        send_back(d).wait_recv()
    for layer in range(LAYERS):
        lax.fori_loop(0, LOCAL, functools.partial(finish, layer), 0)
    out_a = pltpu.make_async_copy(oa_v, out_a_hbm, out_sem.at[2])
    out_a.start()

    for d in range(1, GROUPS):
        send_block(d).wait_send()
        send_back(d).wait_send()

        @pl.when(is_middle(d))
        def _(d=d):
            send_far(d).wait_send()

    for part in range(HALVES):
        both_ways(functools.partial(halo, part), "wait_send")
        rows_out(part, "wait_send")
    both_ways(perm_halo, "wait_send")
    both_ways(strip, "wait_send")
    out_b.wait()
    out_i.wait()
    out_a.wait()


def solution(mesh):
    space_count = mesh.shape["space"]
    cells = (LOCAL * LAYERS * ROWS, LANES)

    def on_device(pressure, source, perm_modes, triples, coeffs):
        doubled, base, inv = pl.pallas_call(
            functools.partial(kernel, space_count),
            out_shape=[jax.ShapeDtypeStruct(cells, F32)] * 3,
            in_specs=[pl.BlockSpec(memory_space=pltpu.HBM)] * 5,
            out_specs=[pl.BlockSpec(memory_space=pl.ANY)] * 3,
            scratch_shapes=[
                pltpu.VMEM((PAD * LAYERS * ROWS, LANES), F32),
                pltpu.VMEM(cells, F32),
                pltpu.VMEM((KA, LAYERS + 2, ROWS + 2 * EDGE, LANES), F32),
                pltpu.VMEM((3, ENTRIES), jnp.int32),
                pltpu.VMEM((ENTRIES,), F32),
                pltpu.VMEM((LAYERS, ROWS + 2, PAD, LANES), F32),
                pltpu.VMEM((LAYERS + 2, OWN + 2, WIDE, LANES), F32),
                pltpu.VMEM((GROUPS, LAYERS, OWN * PAD, LANES), F32),
                pltpu.VMEM((LAYERS, ROWS * PAD, LANES), F32),
                pltpu.VMEM((2 * WIDE, GROUPS * 2 * WIDE), BF16),
                pltpu.VMEM((2 * WIDE, ENTRIES), BF16),
                pltpu.VMEM((GROUPS * 2 * WIDE, LAYERS * OWN * LANES), BF16),
                pltpu.VMEM((6, LAYERS, KA * OWN, LANES), F32),
                pltpu.VMEM((LAYERS + 2, KA * OWN, LANES), F32),
                pltpu.VMEM((2, LAYERS, KA * OWN, LANES), F32),
                pltpu.VMEM((KA, LAYERS, ROWS, LANES), F32),
                pltpu.VMEM((KA, PAD, LANES), F32),
                pltpu.VMEM(cells, F32),
                pltpu.VMEM(cells, F32),
                pltpu.VMEM(cells, F32),
                pltpu.SemaphoreType.DMA((5,)),
                pltpu.SemaphoreType.DMA((3,)),
            ]
            + [pltpu.SemaphoreType.DMA((GROUPS,))] * 2
            + [pltpu.SemaphoreType.DMA((HALVES,))] * 4
            + [pltpu.SemaphoreType.DMA((GROUPS,))] * 2
            + [pltpu.SemaphoreType.DMA((HALVES, 2))] * 2
            + [pltpu.SemaphoreType.DMA((2,))] * 4
            + [pltpu.SemaphoreType.DMA((GROUPS,))] * 2,
            compiler_params=pltpu.CompilerParams(
                collective_id=0, has_side_effects=True, vmem_limit_bytes=60 * 1024 * 1024
            ),
        )(
            pressure.reshape(cells),
            source.reshape(cells),
            perm_modes,
            triples,
            coeffs,
        )
        applied = 0.5 * doubled
        relaxed = base - applied * inv
        return applied.reshape(pressure.shape), relaxed.reshape(pressure.shape)

    return jax.shard_map(
        on_device,
        mesh=mesh,
        in_specs=(
            P("modes", "space", None, None),
            P("modes", "space", None, None),
            P(None, "space", None, None),
            P(),
            P(),
        ),
        out_specs=(P("modes", "space", None, None), P("modes", "space", None, None)),
        check_vma=False,
    )
```

```python
import functools

import jax
import jax.numpy as jnp
from jax import lax
from jax.experimental import pallas as pl
from jax.experimental.pallas import tpu as pltpu
from jax.sharding import PartitionSpec as P

KA = 8
GROUPS = 8
LOCAL = 15
PAD = 16
LAYERS = 2
ROWS = 32
LANES = 128
OWN = ROWS // GROUPS
ENTRIES = 2880
DEPTH = 3072
HALVES = 2
QUAD = GROUPS // HALVES
EDGE = 8
DATA = slice(EDGE, EDGE + ROWS)
WIDE = GROUPS * PAD
relax_weight = 0.8

MESH = pl.DeviceIdType.MESH
F32 = jnp.float32
BF16 = jnp.bfloat16


def kernel(
    space_count,
    p_hbm,
    s_hbm,
    a_hbm,
    tri_hbm,
    cf_hbm,
    out_a_hbm,
    out_b_hbm,
    out_i_hbm,
    p_v,
    s_v,
    a_v,
    tri_v,
    cf_v,
    t,
    q,
    r_out,
    ret,
    w_mat,
    i_hot,
    l_hot,
    b_hot,
    m_buf,
    w_f,
    a_str,
    a_y,
    dg,
    cdb,
    inv_v,
    base_v,
    oa_v,
    in_sem,
    out_sem,
    a2a_send,
    a2a_recv,
    low_send,
    low_recv,
    high_send,
    high_recv,
    far_send,
    far_recv,
    row_send,
    row_recv,
    perm_send,
    perm_recv,
    str_send,
    str_recv,
    ret_send,
    ret_recv,
):
    m = lax.axis_index("modes")
    s = lax.axis_index("space")
    has_dn = s > 0
    has_up = s < space_count - 1

    half_of = m // QUAD

    def peer_to(d):
        return lax.rem(half_of + d // QUAD, HALVES) * QUAD + lax.rem(m + d, QUAD)

    def peer_from(d):
        return lax.rem(half_of + d // QUAD, HALVES) * QUAD + lax.rem(m + GROUPS - d, QUAD)

    def block_of(g):
        return jnp.where(g < QUAD, g, GROUPS + QUAD - 1 - g)

    block = block_of(m)
    turned = half_of == 1
    ahead = lax.rem(m, QUAD) < QUAD - 1
    behind = lax.rem(m, QUAD) > 0
    row_up, row_up_to = jnp.where(turned, 1, OWN), jnp.where(turned, OWN + 1, 0)
    row_dn, row_dn_to = jnp.where(turned, OWN, 1), jnp.where(turned, 0, OWN + 1)

    row_dn_to_far = jnp.where(turned, 0, OWN + 1)

    def far_row(b):
        return jnp.where(b == QUAD, QUAD * OWN, QUAD * OWN + 1)

    def mode_rows(g):
        return pl.ds(pl.multiple_of(g * PAD, PAD), PAD)

    barrier = pltpu.get_barrier_semaphore()
    for d in range(1, GROUPS):
        pl.semaphore_signal(barrier, inc=1, device_id=(peer_to(d), s), device_id_type=MESH)

    @pl.when(has_dn)
    def _():
        pl.semaphore_signal(barrier, inc=1, device_id=(m, s - 1), device_id_type=MESH)

    @pl.when(has_up)
    def _():
        pl.semaphore_signal(barrier, inc=1, device_id=(m, s + 1), device_id_type=MESH)

    load_p = pltpu.make_async_copy(p_hbm, p_v.at[0 : LOCAL * 64], in_sem.at[0])
    load_a = pltpu.make_async_copy(a_hbm, a_v.at[:, 1:3, DATA], in_sem.at[1])
    load_t = pltpu.make_async_copy(tri_hbm, tri_v, in_sem.at[2])
    load_c = pltpu.make_async_copy(cf_hbm, cf_v, in_sem.at[3])
    load_s = pltpu.make_async_copy(s_hbm, s_v, in_sem.at[4])
    for load in (load_p, load_a, load_t, load_c, load_s):
        load.start()

    p_v[LOCAL * 64 :, :] = jnp.zeros((64, LANES), F32)
    t[:, 0] = jnp.zeros((LAYERS, PAD, LANES), F32)
    t[:, ROWS + 1] = jnp.zeros((LAYERS, PAD, LANES), F32)
    load_p.wait()

    def stage(row, carry):
        for layer in range(LAYERS):
            for half in range(2):
                start = half * 8 * 64 + layer * ROWS + row
                t[layer, row + 1, half * 8 : half * 8 + 8, :] = p_v[pl.ds(start, 8, stride=64), :]
        return carry

    lax.fori_loop(0, ROWS, stage, 0)
    q[1:3, 1 : OWN + 1, mode_rows(m), :] = t[:, pl.ds(block * OWN + 1, OWN), :, :]

    @pl.when(jnp.logical_not(ahead))
    def _():
        q[1:3, pl.ds(row_dn_to_far, 1), mode_rows(m), :] = t[:, pl.ds(far_row(block), 1), :, :]

    @pl.when(jnp.logical_not(behind))
    def _():
        q[1:3, pl.ds(row_up_to, 1), :, :] = jnp.zeros((LAYERS, 1, WIDE, LANES), F32)

    def send_block(d):
        g = peer_to(d)
        return pltpu.make_async_remote_copy(
            src_ref=t.at[:, pl.ds(block_of(g) * OWN + 1, OWN)],
            dst_ref=q.at[1:3, 1 : OWN + 1, mode_rows(m), :],
            send_sem=a2a_send.at[d],
            recv_sem=a2a_recv.at[d],
            device_id=(g, s),
            device_id_type=MESH,
        )

    def send_far(d):
        g = peer_to(d)
        b = block_of(g)
        to = jnp.where(b == QUAD, 0, OWN + 1)
        return pltpu.make_async_remote_copy(
            src_ref=t.at[:, pl.ds(far_row(b), 1)],
            dst_ref=q.at[1:3, pl.ds(to, 1), mode_rows(m), :],
            send_sem=far_send.at[d],
            recv_sem=far_recv.at[d],
            device_id=(g, s),
            device_id_type=MESH,
        )

    def is_middle(d):
        b = block_of(peer_to(d))
        return jnp.logical_or(b == QUAD - 1, b == QUAD)

    def halves(part):
        first = lax.rem(half_of + part, HALVES) * QUAD * PAD
        return pl.ds(pl.multiple_of(first, QUAD * PAD), QUAD * PAD)

    def row_halo(part, up):
        src, dst = (row_up, row_up_to) if up else (row_dn, row_dn_to)
        return pltpu.make_async_remote_copy(
            src_ref=q.at[1:3, pl.ds(src, 1), halves(part), :],
            dst_ref=q.at[1:3, pl.ds(dst, 1), halves(part), :],
            send_sem=row_send.at[part, 1 if up else 0],
            recv_sem=row_recv.at[part, 1 if up else 0],
            device_id=(m + 1 if up else m - 1, s),
            device_id_type=MESH,
        )

    def rows_out(part, act):
        @pl.when(ahead)
        def _():
            getattr(row_halo(part, True), act)()

        @pl.when(behind)
        def _():
            getattr(row_halo(part, False), act)()

    def rows_in(part):
        @pl.when(behind)
        def _():
            row_halo(part, True).wait_recv()

        @pl.when(ahead)
        def _():
            row_halo(part, False).wait_recv()

        @pl.when(jnp.logical_not(ahead))
        def _():
            for d in range(max(part * QUAD, 1), (part + 1) * QUAD):
                send_far(d).wait_recv()

    def halo(part, up):
        rows = halves(part)
        sems = (high_send, high_recv) if up else (low_send, low_recv)
        return pltpu.make_async_remote_copy(
            src_ref=q.at[2 if up else 1, 1 : OWN + 1, rows, :],
            dst_ref=q.at[0 if up else 3, 1 : OWN + 1, rows, :],
            send_sem=sems[0].at[part],
            recv_sem=sems[1].at[part],
            device_id=(m, s + 1 if up else s - 1),
            device_id_type=MESH,
        )

    def perm_halo(up):
        return pltpu.make_async_remote_copy(
            src_ref=a_v.at[:, 2 if up else 1, DATA],
            dst_ref=a_v.at[:, 0 if up else 3, DATA],
            send_sem=perm_send.at[1 if up else 0],
            recv_sem=perm_recv.at[1 if up else 0],
            device_id=(m, s + 1 if up else s - 1),
            device_id_type=MESH,
        )

    def strip(up):
        return pltpu.make_async_remote_copy(
            src_ref=a_str.at[2 if up else 1],
            dst_ref=a_str.at[0 if up else 3],
            send_sem=str_send.at[1 if up else 0],
            recv_sem=str_recv.at[1 if up else 0],
            device_id=(m, s + 1 if up else s - 1),
            device_id_type=MESH,
        )

    own_rows_back = pl.ds(pl.multiple_of(block * OWN * PAD, OWN * PAD), OWN * PAD)

    def send_back(d):
        g = peer_to(d)
        return pltpu.make_async_remote_copy(
            src_ref=r_out.at[g],
            dst_ref=ret.at[:, own_rows_back, :],
            send_sem=ret_send.at[d],
            recv_sem=ret_recv.at[d],
            device_id=(g, s),
            device_id_type=MESH,
        )

    def both_ways(make, act):
        @pl.when(has_up)
        def _():
            getattr(make(True), act)()

        @pl.when(has_dn)
        def _():
            getattr(make(False), act)()

    def arrived(make):
        @pl.when(has_dn)
        def _():
            make(True).wait_recv()

        @pl.when(has_up)
        def _():
            make(False).wait_recv()

    load_a.wait()
    for layer in range(LAYERS):
        a_v[:, layer + 1, 0:EDGE] = jnp.zeros((KA, EDGE, LANES), F32)
        a_v[:, layer + 1, EDGE + ROWS :] = jnp.zeros((KA, EDGE, LANES), F32)
        for k in range(KA):
            to = slice(k * OWN, (k + 1) * OWN)
            a_str[layer + 1, to, :] = a_v[k, layer + 1, pl.ds(EDGE + block * OWN, OWN), :]
            a_y[0, layer, to, :] = a_v[k, layer + 1, pl.ds(EDGE + block * OWN - 1, OWN), :]
            a_y[1, layer, to, :] = a_v[k, layer + 1, pl.ds(EDGE + block * OWN + 1, OWN), :]

    neighbours = GROUPS - 1 + has_dn.astype(jnp.int32) + has_up.astype(jnp.int32)
    pl.semaphore_wait(barrier, neighbours)
    both_ways(strip, "start")
    for d in range(1, GROUPS):
        send_block(d).start()

        @pl.when(is_middle(d))
        def _(d=d):
            send_far(d).start()


    @pl.when(jnp.logical_not(has_dn))
    def _():
        q[0] = jnp.zeros(q.shape[1:], F32)
        a_v[:, 0, DATA] = jnp.zeros((KA, ROWS, LANES), F32)
        a_str[0] = jnp.zeros((KA * OWN, LANES), F32)

    @pl.when(jnp.logical_not(has_up))
    def _():
        q[3] = jnp.zeros(q.shape[1:], F32)
        a_v[:, 3, DATA] = jnp.zeros((KA, ROWS, LANES), F32)
        a_str[3] = jnp.zeros((KA * OWN, LANES), F32)

    load_t.wait()
    load_c.wait()
    mode_i = tri_v[0:1, :]
    mode_j = tri_v[1:2, :]
    mode_k = tri_v[2:3, :]
    row_i = mode_i + ((mode_i * 274) >> 12)
    group_j = (mode_j * 274) >> 12
    col_jk = mode_j - LOCAL * group_j + PAD * mode_k
    cf = cf_v[...].reshape(1, ENTRIES)
    cf_hi = cf.astype(BF16).astype(F32)
    cf_lo = cf - cf_hi
    ids = lax.broadcasted_iota(jnp.int32, (WIDE, ENTRIES), 0)
    tail = ENTRIES // WIDE * WIDE
    for hot in (i_hot, l_hot, b_hot):
        hot[:, tail:] = jnp.zeros((hot.shape[0], DEPTH - tail), BF16)
    i_hot[:, 0:ENTRIES] = jnp.where(ids == row_i, 1.0, 0.0).astype(BF16)
    is_col = ids == col_jk
    b_hot[0:WIDE, 0:ENTRIES] = jnp.where(is_col, cf_hi, 0.0).astype(BF16)
    b_hot[WIDE:, 0:ENTRIES] = jnp.where(is_col, cf_lo, 0.0).astype(BF16)

    def table(c, carry):
        for part in range(QUAD):
            mask = jnp.where(group_j == c * QUAD + part, 1.0, 0.0).astype(BF16)
            rows = slice(part * WIDE, (part + 1) * WIDE)
            l_hot[rows, 0:ENTRIES] = i_hot[:, 0:ENTRIES] * mask
        both = lax.dot_general(
            l_hot[...], b_hot[...], (((1,), (1,)), ((), ())), preferred_element_type=F32
        )
        coupled = both[:, 0:WIDE] + both[:, WIDE:]
        hi = coupled.astype(BF16)
        lo = (coupled - hi.astype(F32)).astype(BF16)
        for part in range(QUAD):
            rows = slice(part * WIDE, (part + 1) * WIDE)
            for side in range(2):
                at = pl.multiple_of((c * QUAD + part) * 2 * WIDE + side * WIDE, WIDE)
                w_mat[0:WIDE, pl.ds(at, WIDE)] = hi[rows]
                w_mat[WIDE:, pl.ds(at, WIDE)] = lo[rows]
        return carry

    def hand_on(part):
        for d in range(max(part * QUAD, 1), (part + 1) * QUAD):
            send_block(d).wait_recv()
        both_ways(functools.partial(halo, part), "start")
        rows_out(part, "start")

    lax.fori_loop(0, 1, table, 0)
    hand_on(0)
    lax.fori_loop(1, 2, table, 0)
    arrived(strip)
    lane_ids = lax.broadcasted_iota(jnp.int32, (ROWS, LANES), 1)

    def beside(a):
        return (
            jnp.where(lane_ids > 0, pltpu.roll(a, 1, 1), 0.0),
            jnp.where(lane_ids < LANES - 1, pltpu.roll(a, LANES - 1, 1), 0.0),
        )

    for layer in range(LAYERS):
        a = a_str[layer + 1]
        sides = (a_str[layer], a_str[layer + 2], a_y[0, layer], a_y[1, layer]) + beside(a)
        for f, side in enumerate(sides):
            w_f[f, layer] = a + side
    hand_on(1)

    def chunk(d):
        g = peer_from(d)
        rows = mode_rows(g)
        lanes = lax.broadcasted_iota(jnp.int32, (PAD, LANES), 1)
        for layer in range(LAYERS):
            for r in range(OWN):
                p = q[layer + 1, r + 1, rows, :]
                diffs = (
                    p - q[layer, r + 1, rows, :],
                    p - q[layer + 2, r + 1, rows, :],
                    p - q[layer + 1, r, rows, :],
                    p - q[layer + 1, r + 2, rows, :],
                    p - jnp.where(lanes > 0, pltpu.roll(p, 1, 1), 0.0),
                    p - jnp.where(lanes < LANES - 1, pltpu.roll(p, LANES - 1, 1), 0.0),
                )
                at = (layer * OWN + r) * LANES
                for k in range(KA):
                    total = None
                    for f in range(6):
                        term = w_f[f, layer, k * OWN + r : k * OWN + r + 1, :] * diffs[f]
                        total = term if total is None else total + term
                    hi = total.astype(BF16)
                    lo = (total - hi.astype(F32)).astype(BF16)
                    for part, piece in enumerate((hi, lo)):
                        to = pl.multiple_of((2 * g + part) * WIDE + k * PAD, PAD)
                        m_buf[pl.ds(to, PAD), at : at + LANES] = piece

    def step(d, carry):
        chunk(d)
        return carry

    for part in range(HALVES):
        rows_in(part)
        arrived(functools.partial(halo, part))
        if part == HALVES - 1:
            both_ways(perm_halo, "start")
        lax.fori_loop(part * QUAD, (part + 1) * QUAD, step, 0)

    for layer in range(LAYERS):
        half = OWN * LANES
        prod = jnp.dot(
            w_mat[...],
            m_buf[:, layer * half : (layer + 1) * half],
            preferred_element_type=F32,
        )
        prod = prod[:WIDE] + prod[WIDE:]
        for r in range(OWN):
            for go in range(GROUPS):
                r_out[go, layer, r * PAD : (r + 1) * PAD, :] = prod[
                    go * PAD : (go + 1) * PAD, r * LANES : (r + 1) * LANES
                ]
    for d in range(1, GROUPS):
        send_back(d).start()
    ret[:, own_rows_back, :] = r_out[m]

    own_cols = pl.ds(pl.multiple_of(2 * WIDE * m, 2 * WIDE), WIDE)
    own_rows = w_mat[mode_rows(m), own_cols].astype(F32) + w_mat[
        pl.ds(pl.multiple_of(WIDE + m * PAD, PAD), PAD), own_cols
    ].astype(F32)
    sub = lax.broadcasted_iota(jnp.int32, (PAD, LANES), 0)
    lane = lax.broadcasted_iota(jnp.int32, (PAD, LANES), 1)
    for k in range(KA):
        picked = jnp.where(lane == sub + k * PAD, own_rows, 0.0)
        cdb[k] = jnp.broadcast_to(jnp.sum(picked, axis=1, keepdims=True), (PAD, LANES))

    arrived(perm_halo)

    def diagonal(k, carry):
        for layer in range(LAYERS):
            a = a_v[k, layer + 1, DATA]
            sides = (
                a_v[k, layer, DATA],
                a_v[k, layer + 2, DATA],
                a_v[k, layer + 1, EDGE - 1 : EDGE - 1 + ROWS],
                a_v[k, layer + 1, EDGE + 1 : EDGE + 1 + ROWS],
            ) + beside(a)
            total = 6.0 * a
            for side in sides:
                total = total + side
            dg[k, layer] = 0.5 * total
        return carry

    lax.fori_loop(0, KA, diagonal, 0)
    load_s.wait()

    def scales(j, carry):
        for layer in range(LAYERS):
            scale = jnp.zeros((ROWS, LANES), F32)
            for k in range(KA):
                scale = scale + cdb[k, pl.ds(j, 1), :] * dg[k, layer]
            at = pl.ds(pl.multiple_of(j * 64 + layer * ROWS, ROWS), ROWS)
            inv = relax_weight / scale
            inv_v[at, :] = inv
            base_v[at, :] = p_v[at, :] + s_v[at, :] * inv
        return carry

    lax.fori_loop(0, LOCAL, scales, 0)

    def finish(layer, j, carry):
        for r8 in range(ROWS // 8):
            got = ret[layer, pl.ds(r8 * 8 * PAD + j, 8, stride=PAD), :]
            at = pl.ds(pl.multiple_of(j * 64 + layer * ROWS + r8 * 8, 8), 8)
            oa_v[at, :] = got
        return carry

    out_b = pltpu.make_async_copy(base_v, out_b_hbm, out_sem.at[0])
    out_i = pltpu.make_async_copy(inv_v, out_i_hbm, out_sem.at[1])
    out_b.start()
    out_i.start()

    for d in range(1, GROUPS):
        send_back(d).wait_recv()
    for layer in range(LAYERS):
        lax.fori_loop(0, LOCAL, functools.partial(finish, layer), 0)
    out_a = pltpu.make_async_copy(oa_v, out_a_hbm, out_sem.at[2])
    out_a.start()

    for d in range(1, GROUPS):
        send_block(d).wait_send()
        send_back(d).wait_send()

        @pl.when(is_middle(d))
        def _(d=d):
            send_far(d).wait_send()

    for part in range(HALVES):
        both_ways(functools.partial(halo, part), "wait_send")
        rows_out(part, "wait_send")
    both_ways(perm_halo, "wait_send")
    both_ways(strip, "wait_send")
    out_b.wait()
    out_i.wait()
    out_a.wait()


def solution(mesh):
    space_count = mesh.shape["space"]
    cells = (LOCAL * LAYERS * ROWS, LANES)

    def on_device(pressure, source, perm_modes, triples, coeffs):
        doubled, base, inv = pl.pallas_call(
            functools.partial(kernel, space_count),
            out_shape=[jax.ShapeDtypeStruct(cells, F32)] * 3,
            in_specs=[pl.BlockSpec(memory_space=pltpu.HBM)] * 5,
            out_specs=[pl.BlockSpec(memory_space=pl.ANY)] * 3,
            scratch_shapes=[
                pltpu.VMEM((PAD * LAYERS * ROWS, LANES), F32),
                pltpu.VMEM(cells, F32),
                pltpu.VMEM((KA, LAYERS + 2, ROWS + 2 * EDGE, LANES), F32),
                pltpu.VMEM((3, ENTRIES), jnp.int32),
                pltpu.VMEM((ENTRIES,), F32),
                pltpu.VMEM((LAYERS, ROWS + 2, PAD, LANES), F32),
                pltpu.VMEM((LAYERS + 2, OWN + 2, WIDE, LANES), F32),
                pltpu.VMEM((GROUPS, LAYERS, OWN * PAD, LANES), F32),
                pltpu.VMEM((LAYERS, ROWS * PAD, LANES), F32),
                pltpu.VMEM((2 * WIDE, GROUPS * 2 * WIDE), BF16),
                pltpu.VMEM((WIDE, DEPTH), BF16),
                pltpu.VMEM((QUAD * WIDE, DEPTH), BF16),
                pltpu.VMEM((2 * WIDE, DEPTH), BF16),
                pltpu.VMEM((GROUPS * 2 * WIDE, LAYERS * OWN * LANES), BF16),
                pltpu.VMEM((6, LAYERS, KA * OWN, LANES), F32),
                pltpu.VMEM((LAYERS + 2, KA * OWN, LANES), F32),
                pltpu.VMEM((2, LAYERS, KA * OWN, LANES), F32),
                pltpu.VMEM((KA, LAYERS, ROWS, LANES), F32),
                pltpu.VMEM((KA, PAD, LANES), F32),
                pltpu.VMEM(cells, F32),
                pltpu.VMEM(cells, F32),
                pltpu.VMEM(cells, F32),
                pltpu.SemaphoreType.DMA((5,)),
                pltpu.SemaphoreType.DMA((3,)),
            ]
            + [pltpu.SemaphoreType.DMA((GROUPS,))] * 2
            + [pltpu.SemaphoreType.DMA((HALVES,))] * 4
            + [pltpu.SemaphoreType.DMA((GROUPS,))] * 2
            + [pltpu.SemaphoreType.DMA((HALVES, 2))] * 2
            + [pltpu.SemaphoreType.DMA((2,))] * 4
            + [pltpu.SemaphoreType.DMA((GROUPS,))] * 2,
            compiler_params=pltpu.CompilerParams(
                collective_id=0, has_side_effects=True, vmem_limit_bytes=60 * 1024 * 1024
            ),
        )(
            pressure.reshape(cells),
            source.reshape(cells),
            perm_modes,
            triples,
            coeffs,
        )
        applied = 0.5 * doubled
        relaxed = base - applied * inv
        return applied.reshape(pressure.shape), relaxed.reshape(pressure.shape)

    return jax.shard_map(
        on_device,
        mesh=mesh,
        in_specs=(
            P("modes", "space", None, None),
            P("modes", "space", None, None),
            P(None, "space", None, None),
            P(),
            P(),
        ),
        out_specs=(P("modes", "space", None, None), P("modes", "space", None, None)),
        check_vma=False,
    )
```

```python
import functools

import jax
import jax.numpy as jnp
from jax import lax
from jax.experimental import pallas as pl
from jax.experimental.pallas import tpu as pltpu
from jax.sharding import PartitionSpec as P

KA = 8
GROUPS = 8
LOCAL = 15
PAD = 16
LAYERS = 2
ROWS = 32
LANES = 128
OWN = ROWS // GROUPS
ENTRIES = 2880
HALVES = 2
QUAD = GROUPS // HALVES
EDGE = 8
DATA = slice(EDGE, EDGE + ROWS)
WIDE = GROUPS * PAD
relax_weight = 0.8

MESH = pl.DeviceIdType.MESH
F32 = jnp.float32
BF16 = jnp.bfloat16


def kernel(
    space_count,
    p_hbm,
    s_hbm,
    a_hbm,
    tri_hbm,
    cf_hbm,
    ret,
    out_b_hbm,
    out_i_hbm,
    p_v,
    s_v,
    a_v,
    tri_v,
    cf_v,
    t,
    q,
    r_out,
    w_mat,
    a_hot,
    m_buf,
    w_f,
    a_str,
    a_y,
    dg,
    cdb,
    inv_v,
    base_v,
    in_sem,
    out_sem,
    a2a_send,
    a2a_recv,
    low_send,
    low_recv,
    high_send,
    high_recv,
    far_send,
    far_recv,
    row_send,
    row_recv,
    perm_send,
    perm_recv,
    str_send,
    str_recv,
    ret_send,
    ret_recv,
):
    m = lax.axis_index("modes")
    s = lax.axis_index("space")
    has_dn = s > 0
    has_up = s < space_count - 1

    half_of = m // QUAD

    def peer_to(d):
        return lax.rem(half_of + d // QUAD, HALVES) * QUAD + lax.rem(m + d, QUAD)

    def peer_from(d):
        return lax.rem(half_of + d // QUAD, HALVES) * QUAD + lax.rem(m + GROUPS - d, QUAD)

    def block_of(g):
        return jnp.where(g < QUAD, g, GROUPS + QUAD - 1 - g)

    block = block_of(m)
    turned = half_of == 1
    ahead = lax.rem(m, QUAD) < QUAD - 1
    behind = lax.rem(m, QUAD) > 0
    row_up, row_up_to = jnp.where(turned, 1, OWN), jnp.where(turned, OWN + 1, 0)
    row_dn, row_dn_to = jnp.where(turned, OWN, 1), jnp.where(turned, 0, OWN + 1)

    row_dn_to_far = jnp.where(turned, 0, OWN + 1)

    def far_row(b):
        return jnp.where(b == QUAD, QUAD * OWN, QUAD * OWN + 1)

    def mode_rows(g):
        return pl.ds(pl.multiple_of(g * PAD, PAD), PAD)

    barrier = pltpu.get_barrier_semaphore()
    for d in range(1, GROUPS):
        pl.semaphore_signal(barrier, inc=1, device_id=(peer_to(d), s), device_id_type=MESH)

    @pl.when(has_dn)
    def _():
        pl.semaphore_signal(barrier, inc=1, device_id=(m, s - 1), device_id_type=MESH)

    @pl.when(has_up)
    def _():
        pl.semaphore_signal(barrier, inc=1, device_id=(m, s + 1), device_id_type=MESH)

    load_p = pltpu.make_async_copy(p_hbm, p_v.at[0 : LOCAL * 64], in_sem.at[0])
    load_a = pltpu.make_async_copy(a_hbm, a_v.at[:, 1:3, DATA], in_sem.at[1])
    load_t = pltpu.make_async_copy(tri_hbm, tri_v, in_sem.at[2])
    load_c = pltpu.make_async_copy(cf_hbm, cf_v, in_sem.at[3])
    load_s = pltpu.make_async_copy(s_hbm, s_v, in_sem.at[4])
    for load in (load_p, load_a, load_t, load_c, load_s):
        load.start()

    p_v[LOCAL * 64 :, :] = jnp.zeros((64, LANES), F32)
    t[:, 0] = jnp.zeros((LAYERS, PAD, LANES), F32)
    t[:, ROWS + 1] = jnp.zeros((LAYERS, PAD, LANES), F32)
    load_p.wait()

    def stage(row, carry):
        for layer in range(LAYERS):
            for half in range(2):
                start = half * 8 * 64 + layer * ROWS + row
                t[layer, row + 1, half * 8 : half * 8 + 8, :] = p_v[pl.ds(start, 8, stride=64), :]
        return carry

    lax.fori_loop(0, ROWS, stage, 0)
    q[1:3, 1 : OWN + 1, mode_rows(m), :] = t[:, pl.ds(block * OWN + 1, OWN), :, :]

    @pl.when(jnp.logical_not(ahead))
    def _():
        q[1:3, pl.ds(row_dn_to_far, 1), mode_rows(m), :] = t[:, pl.ds(far_row(block), 1), :, :]

    @pl.when(jnp.logical_not(behind))
    def _():
        q[1:3, pl.ds(row_up_to, 1), :, :] = jnp.zeros((LAYERS, 1, WIDE, LANES), F32)

    def send_block(d):
        g = peer_to(d)
        return pltpu.make_async_remote_copy(
            src_ref=t.at[:, pl.ds(block_of(g) * OWN + 1, OWN)],
            dst_ref=q.at[1:3, 1 : OWN + 1, mode_rows(m), :],
            send_sem=a2a_send.at[d],
            recv_sem=a2a_recv.at[d],
            device_id=(g, s),
            device_id_type=MESH,
        )

    def send_far(d):
        g = peer_to(d)
        b = block_of(g)
        to = jnp.where(b == QUAD, 0, OWN + 1)
        return pltpu.make_async_remote_copy(
            src_ref=t.at[:, pl.ds(far_row(b), 1)],
            dst_ref=q.at[1:3, pl.ds(to, 1), mode_rows(m), :],
            send_sem=far_send.at[d],
            recv_sem=far_recv.at[d],
            device_id=(g, s),
            device_id_type=MESH,
        )

    def is_middle(d):
        b = block_of(peer_to(d))
        return jnp.logical_or(b == QUAD - 1, b == QUAD)

    def halves(part):
        first = lax.rem(half_of + part, HALVES) * QUAD * PAD
        return pl.ds(pl.multiple_of(first, QUAD * PAD), QUAD * PAD)

    def row_halo(part, up):
        src, dst = (row_up, row_up_to) if up else (row_dn, row_dn_to)
        return pltpu.make_async_remote_copy(
            src_ref=q.at[1:3, pl.ds(src, 1), halves(part), :],
            dst_ref=q.at[1:3, pl.ds(dst, 1), halves(part), :],
            send_sem=row_send.at[part, 1 if up else 0],
            recv_sem=row_recv.at[part, 1 if up else 0],
            device_id=(m + 1 if up else m - 1, s),
            device_id_type=MESH,
        )

    def rows_out(part, act):
        @pl.when(ahead)
        def _():
            getattr(row_halo(part, True), act)()

        @pl.when(behind)
        def _():
            getattr(row_halo(part, False), act)()

    def rows_in(part):
        @pl.when(behind)
        def _():
            row_halo(part, True).wait_recv()

        @pl.when(ahead)
        def _():
            row_halo(part, False).wait_recv()

        @pl.when(jnp.logical_not(ahead))
        def _():
            for d in range(max(part * QUAD, 1), (part + 1) * QUAD):
                send_far(d).wait_recv()

    def halo(part, up):
        rows = halves(part)
        sems = (high_send, high_recv) if up else (low_send, low_recv)
        return pltpu.make_async_remote_copy(
            src_ref=q.at[2 if up else 1, 1 : OWN + 1, rows, :],
            dst_ref=q.at[0 if up else 3, 1 : OWN + 1, rows, :],
            send_sem=sems[0].at[part],
            recv_sem=sems[1].at[part],
            device_id=(m, s + 1 if up else s - 1),
            device_id_type=MESH,
        )

    def perm_halo(up):
        return pltpu.make_async_remote_copy(
            src_ref=a_v.at[:, 2 if up else 1, DATA],
            dst_ref=a_v.at[:, 0 if up else 3, DATA],
            send_sem=perm_send.at[1 if up else 0],
            recv_sem=perm_recv.at[1 if up else 0],
            device_id=(m, s + 1 if up else s - 1),
            device_id_type=MESH,
        )

    def strip(up):
        return pltpu.make_async_remote_copy(
            src_ref=a_str.at[2 if up else 1],
            dst_ref=a_str.at[0 if up else 3],
            send_sem=str_send.at[1 if up else 0],
            recv_sem=str_recv.at[1 if up else 0],
            device_id=(m, s + 1 if up else s - 1),
            device_id_type=MESH,
        )

    own_rows_back = pl.ds(pl.multiple_of(block * OWN * PAD, OWN * PAD), OWN * PAD)

    def send_back(d):
        g = peer_to(d)
        return pltpu.make_async_remote_copy(
            src_ref=r_out.at[g],
            dst_ref=ret.at[:, own_rows_back, :],
            send_sem=ret_send.at[d],
            recv_sem=ret_recv.at[d],
            device_id=(g, s),
            device_id_type=MESH,
        )

    def both_ways(make, act):
        @pl.when(has_up)
        def _():
            getattr(make(True), act)()

        @pl.when(has_dn)
        def _():
            getattr(make(False), act)()

    def arrived(make):
        @pl.when(has_dn)
        def _():
            make(True).wait_recv()

        @pl.when(has_up)
        def _():
            make(False).wait_recv()

    load_a.wait()
    for layer in range(LAYERS):
        a_v[:, layer + 1, 0:EDGE] = jnp.zeros((KA, EDGE, LANES), F32)
        a_v[:, layer + 1, EDGE + ROWS :] = jnp.zeros((KA, EDGE, LANES), F32)
        for k in range(KA):
            to = slice(k * OWN, (k + 1) * OWN)
            a_str[layer + 1, to, :] = a_v[k, layer + 1, pl.ds(EDGE + block * OWN, OWN), :]
            a_y[0, layer, to, :] = a_v[k, layer + 1, pl.ds(EDGE + block * OWN - 1, OWN), :]
            a_y[1, layer, to, :] = a_v[k, layer + 1, pl.ds(EDGE + block * OWN + 1, OWN), :]

    neighbours = GROUPS - 1 + has_dn.astype(jnp.int32) + has_up.astype(jnp.int32)
    pl.semaphore_wait(barrier, neighbours)
    both_ways(strip, "start")
    for d in range(1, GROUPS):
        send_block(d).start()

        @pl.when(is_middle(d))
        def _(d=d):
            send_far(d).start()


    @pl.when(jnp.logical_not(has_dn))
    def _():
        q[0] = jnp.zeros(q.shape[1:], F32)
        a_v[:, 0, DATA] = jnp.zeros((KA, ROWS, LANES), F32)
        a_str[0] = jnp.zeros((KA * OWN, LANES), F32)

    @pl.when(jnp.logical_not(has_up))
    def _():
        q[3] = jnp.zeros(q.shape[1:], F32)
        a_v[:, 3, DATA] = jnp.zeros((KA, ROWS, LANES), F32)
        a_str[3] = jnp.zeros((KA * OWN, LANES), F32)

    load_t.wait()
    load_c.wait()
    mode_i = tri_v[0:1, :]
    mode_j = tri_v[1:2, :]
    mode_k = tri_v[2:3, :]
    row_i = mode_i + ((mode_i * 274) >> 12)
    col_jk = mode_j + 113 * ((mode_j * 274) >> 12) + PAD * mode_k
    cf = cf_v[...].reshape(1, ENTRIES)
    cf_hi = cf.astype(BF16).astype(F32)
    cf_lo = cf - cf_hi
    is_row = lax.broadcasted_iota(jnp.int32, (WIDE, ENTRIES), 0) == row_i
    a_hot[0:WIDE, :] = jnp.where(is_row, cf_hi, 0.0).astype(BF16)
    a_hot[WIDE:, :] = jnp.where(is_row, cf_lo, 0.0).astype(BF16)

    def table(c, carry):
        cols = lax.broadcasted_iota(jnp.int32, (2 * WIDE, ENTRIES), 0) + c * (2 * WIDE)
        b_hot = jnp.where(cols == col_jk, 1.0, 0.0).astype(BF16)
        both = lax.dot_general(
            a_hot[...], b_hot, (((1,), (1,)), ((), ())), preferred_element_type=F32
        )
        coupled = both[:WIDE] + both[WIDE:]
        for part in range(2):
            one = coupled[:, part * WIDE : (part + 1) * WIDE]
            hi = one.astype(BF16)
            lo = (one - hi.astype(F32)).astype(BF16)
            for side in range(2):
                at = pl.multiple_of(c * 4 * WIDE + (2 * part + side) * WIDE, WIDE)
                w_mat[0:WIDE, pl.ds(at, WIDE)] = hi
                w_mat[WIDE:, pl.ds(at, WIDE)] = lo
        return carry

    def hand_on(part):
        for d in range(max(part * QUAD, 1), (part + 1) * QUAD):
            send_block(d).wait_recv()
        both_ways(functools.partial(halo, part), "start")
        rows_out(part, "start")

    lax.fori_loop(0, GROUPS // 4, table, 0)
    hand_on(0)
    lax.fori_loop(GROUPS // 4, GROUPS // 2, table, 0)
    arrived(strip)
    lane_ids = lax.broadcasted_iota(jnp.int32, (ROWS, LANES), 1)

    def beside(a):
        return (
            jnp.where(lane_ids > 0, pltpu.roll(a, 1, 1), 0.0),
            jnp.where(lane_ids < LANES - 1, pltpu.roll(a, LANES - 1, 1), 0.0),
        )

    for layer in range(LAYERS):
        a = a_str[layer + 1]
        sides = (a_str[layer], a_str[layer + 2], a_y[0, layer], a_y[1, layer]) + beside(a)
        for f, side in enumerate(sides):
            w_f[f, layer] = a + side
    hand_on(1)

    def chunk(d):
        g = peer_from(d)
        rows = mode_rows(g)
        lanes = lax.broadcasted_iota(jnp.int32, (PAD, LANES), 1)
        for layer in range(LAYERS):
            for r in range(OWN):
                p = q[layer + 1, r + 1, rows, :]
                diffs = (
                    p - q[layer, r + 1, rows, :],
                    p - q[layer + 2, r + 1, rows, :],
                    p - q[layer + 1, r, rows, :],
                    p - q[layer + 1, r + 2, rows, :],
                    p - jnp.where(lanes > 0, pltpu.roll(p, 1, 1), 0.0),
                    p - jnp.where(lanes < LANES - 1, pltpu.roll(p, LANES - 1, 1), 0.0),
                )
                at = (layer * OWN + r) * LANES
                for k in range(KA):
                    total = None
                    for f in range(6):
                        term = w_f[f, layer, k * OWN + r : k * OWN + r + 1, :] * diffs[f]
                        total = term if total is None else total + term
                    hi = total.astype(BF16)
                    lo = (total - hi.astype(F32)).astype(BF16)
                    for part, piece in enumerate((hi, lo)):
                        to = pl.multiple_of((2 * g + part) * WIDE + k * PAD, PAD)
                        m_buf[pl.ds(to, PAD), at : at + LANES] = piece

    def step(d, carry):
        chunk(d)
        return carry

    for part in range(HALVES):
        rows_in(part)
        arrived(functools.partial(halo, part))
        if part == HALVES - 1:
            both_ways(perm_halo, "start")
        lax.fori_loop(part * QUAD, (part + 1) * QUAD, step, 0)

    for layer in range(LAYERS):
        half = OWN * LANES
        prod = jnp.dot(
            w_mat[...],
            m_buf[:, layer * half : (layer + 1) * half],
            preferred_element_type=F32,
        )
        prod = prod[:WIDE] + prod[WIDE:]
        for r in range(OWN):
            for go in range(GROUPS):
                r_out[go, layer, r * PAD : (r + 1) * PAD, :] = prod[
                    go * PAD : (go + 1) * PAD, r * LANES : (r + 1) * LANES
                ]
    for d in range(1, GROUPS):
        send_back(d).start()
    keep = pltpu.make_async_copy(r_out.at[m], ret.at[:, own_rows_back, :], out_sem.at[2])
    keep.start()

    own_cols = pl.ds(pl.multiple_of(2 * WIDE * m, 2 * WIDE), WIDE)
    own_rows = w_mat[mode_rows(m), own_cols].astype(F32) + w_mat[
        pl.ds(pl.multiple_of(WIDE + m * PAD, PAD), PAD), own_cols
    ].astype(F32)
    sub = lax.broadcasted_iota(jnp.int32, (PAD, LANES), 0)
    lane = lax.broadcasted_iota(jnp.int32, (PAD, LANES), 1)
    for k in range(KA):
        picked = jnp.where(lane == sub + k * PAD, own_rows, 0.0)
        cdb[k] = jnp.broadcast_to(jnp.sum(picked, axis=1, keepdims=True), (PAD, LANES))

    arrived(perm_halo)

    def diagonal(k, carry):
        for layer in range(LAYERS):
            a = a_v[k, layer + 1, DATA]
            sides = (
                a_v[k, layer, DATA],
                a_v[k, layer + 2, DATA],
                a_v[k, layer + 1, EDGE - 1 : EDGE - 1 + ROWS],
                a_v[k, layer + 1, EDGE + 1 : EDGE + 1 + ROWS],
            ) + beside(a)
            total = 6.0 * a
            for side in sides:
                total = total + side
            dg[k, layer] = 0.5 * total
        return carry

    lax.fori_loop(0, KA, diagonal, 0)
    load_s.wait()

    def scales(j, carry):
        for layer in range(LAYERS):
            scale = jnp.zeros((ROWS, LANES), F32)
            for k in range(KA):
                scale = scale + cdb[k, pl.ds(j, 1), :] * dg[k, layer]
            at = pl.ds(pl.multiple_of(j * 64 + layer * ROWS, ROWS), ROWS)
            inv = relax_weight / scale
            inv_v[at, :] = inv
            base_v[at, :] = p_v[at, :] + s_v[at, :] * inv
        return carry

    lax.fori_loop(0, LOCAL, scales, 0)

    out_b = pltpu.make_async_copy(base_v, out_b_hbm, out_sem.at[0])
    out_i = pltpu.make_async_copy(inv_v, out_i_hbm, out_sem.at[1])
    out_b.start()
    out_i.start()

    for d in range(1, GROUPS):
        send_block(d).wait_send()
        send_back(d).wait_send()

        @pl.when(is_middle(d))
        def _(d=d):
            send_far(d).wait_send()

    for part in range(HALVES):
        both_ways(functools.partial(halo, part), "wait_send")
        rows_out(part, "wait_send")
    both_ways(perm_halo, "wait_send")
    both_ways(strip, "wait_send")
    out_b.wait()
    out_i.wait()
    keep.wait()
    for d in range(1, GROUPS):
        send_back(d).wait_recv()


def finish(ret, base, inv, applied, relaxed):
    for j in range(LOCAL):
        for r8 in range(ROWS // 8):
            rows = slice(r8 * 8, r8 * 8 + 8)
            got = 0.5 * ret[0, pl.ds(r8 * 8 * PAD + j, 8, stride=PAD), :]
            applied[j, 0, rows, :] = got
            relaxed[j, 0, rows, :] = base[j, 0, rows, :] - got * inv[j, 0, rows, :]


def solution(mesh):
    space_count = mesh.shape["space"]
    cells = (LOCAL * LAYERS * ROWS, LANES)

    def on_device(pressure, source, perm_modes, triples, coeffs):
        returned, base, inv = pl.pallas_call(
            functools.partial(kernel, space_count),
            out_shape=[jax.ShapeDtypeStruct((LAYERS, ROWS * PAD, LANES), F32)]
            + [jax.ShapeDtypeStruct(cells, F32)] * 2,
            in_specs=[pl.BlockSpec(memory_space=pltpu.HBM)] * 5,
            out_specs=[pl.BlockSpec(memory_space=pl.ANY)] * 3,
            scratch_shapes=[
                pltpu.VMEM((PAD * LAYERS * ROWS, LANES), F32),
                pltpu.VMEM(cells, F32),
                pltpu.VMEM((KA, LAYERS + 2, ROWS + 2 * EDGE, LANES), F32),
                pltpu.VMEM((3, ENTRIES), jnp.int32),
                pltpu.VMEM((ENTRIES,), F32),
                pltpu.VMEM((LAYERS, ROWS + 2, PAD, LANES), F32),
                pltpu.VMEM((LAYERS + 2, OWN + 2, WIDE, LANES), F32),
                pltpu.VMEM((GROUPS, LAYERS, OWN * PAD, LANES), F32),
                pltpu.VMEM((2 * WIDE, GROUPS * 2 * WIDE), BF16),
                pltpu.VMEM((2 * WIDE, ENTRIES), BF16),
                pltpu.VMEM((GROUPS * 2 * WIDE, LAYERS * OWN * LANES), BF16),
                pltpu.VMEM((6, LAYERS, KA * OWN, LANES), F32),
                pltpu.VMEM((LAYERS + 2, KA * OWN, LANES), F32),
                pltpu.VMEM((2, LAYERS, KA * OWN, LANES), F32),
                pltpu.VMEM((KA, LAYERS, ROWS, LANES), F32),
                pltpu.VMEM((KA, PAD, LANES), F32),
                pltpu.VMEM(cells, F32),
                pltpu.VMEM(cells, F32),
                pltpu.SemaphoreType.DMA((5,)),
                pltpu.SemaphoreType.DMA((3,)),
            ]
            + [pltpu.SemaphoreType.DMA((GROUPS,))] * 2
            + [pltpu.SemaphoreType.DMA((HALVES,))] * 4
            + [pltpu.SemaphoreType.DMA((GROUPS,))] * 2
            + [pltpu.SemaphoreType.DMA((HALVES, 2))] * 2
            + [pltpu.SemaphoreType.DMA((2,))] * 4
            + [pltpu.SemaphoreType.DMA((GROUPS,))] * 2,
            compiler_params=pltpu.CompilerParams(
                collective_id=0, has_side_effects=True, vmem_limit_bytes=60 * 1024 * 1024
            ),
        )(
            pressure.reshape(cells),
            source.reshape(cells),
            perm_modes,
            triples,
            coeffs,
        )
        whole = (LOCAL, LAYERS, ROWS, LANES)
        one_layer = pl.BlockSpec((LOCAL, 1, ROWS, LANES), lambda layer: (0, layer, 0, 0))
        return pl.pallas_call(
            finish,
            grid=(LAYERS,),
            out_shape=[jax.ShapeDtypeStruct(whole, F32)] * 2,
            in_specs=[
                pl.BlockSpec((1, ROWS * PAD, LANES), lambda layer: (layer, 0, 0)),
                one_layer,
                one_layer,
            ],
            out_specs=[one_layer] * 2,
            compiler_params=pltpu.CompilerParams(vmem_limit_bytes=60 * 1024 * 1024),
        )(returned, base.reshape(whole), inv.reshape(whole))

    return jax.shard_map(
        on_device,
        mesh=mesh,
        in_specs=(
            P("modes", "space", None, None),
            P("modes", "space", None, None),
            P(None, "space", None, None),
            P(),
            P(),
        ),
        out_specs=(P("modes", "space", None, None), P("modes", "space", None, None)),
        check_vma=False,
    )
```

```python
import functools

import jax
import jax.numpy as jnp
from jax import lax
from jax.experimental import pallas as pl
from jax.experimental.pallas import tpu as pltpu
from jax.sharding import PartitionSpec as P

KA = 8
GROUPS = 8
LOCAL = 15
PAD = 16
LAYERS = 2
ROWS = 32
LANES = 128
OWN = ROWS // GROUPS
ENTRIES = 2880
HALVES = 2
QUAD = GROUPS // HALVES
EDGE = 8
DATA = slice(EDGE, EDGE + ROWS)
WIDE = GROUPS * PAD
relax_weight = 0.8

MESH = pl.DeviceIdType.MESH
F32 = jnp.float32
BF16 = jnp.bfloat16


def kernel(
    space_count,
    p_hbm,
    s_hbm,
    a_hbm,
    tri_hbm,
    cf_hbm,
    ret,
    out_b_hbm,
    out_i_hbm,
    p_v,
    s_v,
    a_v,
    tri_v,
    cf_v,
    t,
    q,
    r_out,
    w_mat,
    a_hot,
    m_buf,
    w_f,
    a_str,
    a_y,
    dg,
    cdb,
    inv_v,
    base_v,
    in_sem,
    out_sem,
    a2a_send,
    a2a_recv,
    low_send,
    low_recv,
    high_send,
    high_recv,
    far_send,
    far_recv,
    row_send,
    row_recv,
    perm_send,
    perm_recv,
    str_send,
    str_recv,
    ret_send,
    ret_recv,
    keep_sem,
):
    m = lax.axis_index("modes")
    s = lax.axis_index("space")
    has_dn = s > 0
    has_up = s < space_count - 1

    half_of = m // QUAD

    def peer_to(d):
        return lax.rem(half_of + d // QUAD, HALVES) * QUAD + lax.rem(m + d, QUAD)

    def peer_from(d):
        return lax.rem(half_of + d // QUAD, HALVES) * QUAD + lax.rem(m + GROUPS - d, QUAD)

    def block_of(g):
        return jnp.where(g < QUAD, g, GROUPS + QUAD - 1 - g)

    block = block_of(m)
    turned = half_of == 1
    ahead = lax.rem(m, QUAD) < QUAD - 1
    behind = lax.rem(m, QUAD) > 0
    row_up, row_up_to = jnp.where(turned, 1, OWN), jnp.where(turned, OWN + 1, 0)
    row_dn, row_dn_to = jnp.where(turned, OWN, 1), jnp.where(turned, 0, OWN + 1)

    row_dn_to_far = jnp.where(turned, 0, OWN + 1)

    def far_row(b):
        return jnp.where(b == QUAD, QUAD * OWN, QUAD * OWN + 1)

    def mode_rows(g):
        return pl.ds(pl.multiple_of(g * PAD, PAD), PAD)

    barrier = pltpu.get_barrier_semaphore()
    for d in range(1, GROUPS):
        pl.semaphore_signal(barrier, inc=1, device_id=(peer_to(d), s), device_id_type=MESH)

    @pl.when(has_dn)
    def _():
        pl.semaphore_signal(barrier, inc=1, device_id=(m, s - 1), device_id_type=MESH)

    @pl.when(has_up)
    def _():
        pl.semaphore_signal(barrier, inc=1, device_id=(m, s + 1), device_id_type=MESH)

    load_p = pltpu.make_async_copy(p_hbm, p_v.at[0 : LOCAL * 64], in_sem.at[0])
    load_a = pltpu.make_async_copy(a_hbm, a_v.at[:, 1:3, DATA], in_sem.at[1])
    load_t = pltpu.make_async_copy(tri_hbm, tri_v, in_sem.at[2])
    load_c = pltpu.make_async_copy(cf_hbm, cf_v, in_sem.at[3])
    load_s = pltpu.make_async_copy(s_hbm, s_v, in_sem.at[4])
    for load in (load_p, load_a, load_t, load_c, load_s):
        load.start()

    p_v[LOCAL * 64 :, :] = jnp.zeros((64, LANES), F32)
    t[:, 0] = jnp.zeros((LAYERS, PAD, LANES), F32)
    t[:, ROWS + 1] = jnp.zeros((LAYERS, PAD, LANES), F32)
    load_p.wait()

    def stage(row, carry):
        for layer in range(LAYERS):
            for half in range(2):
                start = half * 8 * 64 + layer * ROWS + row
                t[layer, row + 1, half * 8 : half * 8 + 8, :] = p_v[pl.ds(start, 8, stride=64), :]
        return carry

    lax.fori_loop(0, ROWS, stage, 0)
    q[1:3, 1 : OWN + 1, mode_rows(m), :] = t[:, pl.ds(block * OWN + 1, OWN), :, :]

    @pl.when(jnp.logical_not(ahead))
    def _():
        q[1:3, pl.ds(row_dn_to_far, 1), mode_rows(m), :] = t[:, pl.ds(far_row(block), 1), :, :]

    @pl.when(jnp.logical_not(behind))
    def _():
        q[1:3, pl.ds(row_up_to, 1), :, :] = jnp.zeros((LAYERS, 1, WIDE, LANES), F32)

    def send_block(d):
        g = peer_to(d)
        return pltpu.make_async_remote_copy(
            src_ref=t.at[:, pl.ds(block_of(g) * OWN + 1, OWN)],
            dst_ref=q.at[1:3, 1 : OWN + 1, mode_rows(m), :],
            send_sem=a2a_send.at[d],
            recv_sem=a2a_recv.at[d],
            device_id=(g, s),
            device_id_type=MESH,
        )

    def send_far(d):
        g = peer_to(d)
        b = block_of(g)
        to = jnp.where(b == QUAD, 0, OWN + 1)
        return pltpu.make_async_remote_copy(
            src_ref=t.at[:, pl.ds(far_row(b), 1)],
            dst_ref=q.at[1:3, pl.ds(to, 1), mode_rows(m), :],
            send_sem=far_send.at[d],
            recv_sem=far_recv.at[d],
            device_id=(g, s),
            device_id_type=MESH,
        )

    def is_middle(d):
        b = block_of(peer_to(d))
        return jnp.logical_or(b == QUAD - 1, b == QUAD)

    def halves(part):
        first = lax.rem(half_of + part, HALVES) * QUAD * PAD
        return pl.ds(pl.multiple_of(first, QUAD * PAD), QUAD * PAD)

    def row_halo(part, up):
        src, dst = (row_up, row_up_to) if up else (row_dn, row_dn_to)
        return pltpu.make_async_remote_copy(
            src_ref=q.at[1:3, pl.ds(src, 1), halves(part), :],
            dst_ref=q.at[1:3, pl.ds(dst, 1), halves(part), :],
            send_sem=row_send.at[part, 1 if up else 0],
            recv_sem=row_recv.at[part, 1 if up else 0],
            device_id=(m + 1 if up else m - 1, s),
            device_id_type=MESH,
        )

    def rows_out(part, act):
        @pl.when(ahead)
        def _():
            getattr(row_halo(part, True), act)()

        @pl.when(behind)
        def _():
            getattr(row_halo(part, False), act)()

    def rows_in(part):
        @pl.when(behind)
        def _():
            row_halo(part, True).wait_recv()

        @pl.when(ahead)
        def _():
            row_halo(part, False).wait_recv()

        @pl.when(jnp.logical_not(ahead))
        def _():
            for d in range(max(part * QUAD, 1), (part + 1) * QUAD):
                send_far(d).wait_recv()

    def halo(part, up):
        rows = halves(part)
        sems = (high_send, high_recv) if up else (low_send, low_recv)
        return pltpu.make_async_remote_copy(
            src_ref=q.at[2 if up else 1, 1 : OWN + 1, rows, :],
            dst_ref=q.at[0 if up else 3, 1 : OWN + 1, rows, :],
            send_sem=sems[0].at[part],
            recv_sem=sems[1].at[part],
            device_id=(m, s + 1 if up else s - 1),
            device_id_type=MESH,
        )

    def perm_halo(up):
        return pltpu.make_async_remote_copy(
            src_ref=a_v.at[:, 2 if up else 1, DATA],
            dst_ref=a_v.at[:, 0 if up else 3, DATA],
            send_sem=perm_send.at[1 if up else 0],
            recv_sem=perm_recv.at[1 if up else 0],
            device_id=(m, s + 1 if up else s - 1),
            device_id_type=MESH,
        )

    def strip(up):
        return pltpu.make_async_remote_copy(
            src_ref=a_str.at[2 if up else 1],
            dst_ref=a_str.at[0 if up else 3],
            send_sem=str_send.at[1 if up else 0],
            recv_sem=str_recv.at[1 if up else 0],
            device_id=(m, s + 1 if up else s - 1),
            device_id_type=MESH,
        )

    own_rows_back = pl.ds(pl.multiple_of(block * OWN * PAD, OWN * PAD), OWN * PAD)

    def keep(layer):
        return pltpu.make_async_copy(
            r_out.at[m, layer], ret.at[layer, own_rows_back, :], keep_sem.at[layer]
        )

    def send_back(d, layer):
        g = peer_to(d)
        return pltpu.make_async_remote_copy(
            src_ref=r_out.at[g, layer],
            dst_ref=ret.at[layer, own_rows_back, :],
            send_sem=ret_send.at[layer, d],
            recv_sem=ret_recv.at[layer, d],
            device_id=(g, s),
            device_id_type=MESH,
        )

    def both_ways(make, act):
        @pl.when(has_up)
        def _():
            getattr(make(True), act)()

        @pl.when(has_dn)
        def _():
            getattr(make(False), act)()

    def arrived(make):
        @pl.when(has_dn)
        def _():
            make(True).wait_recv()

        @pl.when(has_up)
        def _():
            make(False).wait_recv()

    load_a.wait()
    for layer in range(LAYERS):
        a_v[:, layer + 1, 0:EDGE] = jnp.zeros((KA, EDGE, LANES), F32)
        a_v[:, layer + 1, EDGE + ROWS :] = jnp.zeros((KA, EDGE, LANES), F32)
        for k in range(KA):
            to = slice(k * OWN, (k + 1) * OWN)
            a_str[layer + 1, to, :] = a_v[k, layer + 1, pl.ds(EDGE + block * OWN, OWN), :]
            a_y[0, layer, to, :] = a_v[k, layer + 1, pl.ds(EDGE + block * OWN - 1, OWN), :]
            a_y[1, layer, to, :] = a_v[k, layer + 1, pl.ds(EDGE + block * OWN + 1, OWN), :]

    neighbours = GROUPS - 1 + has_dn.astype(jnp.int32) + has_up.astype(jnp.int32)
    pl.semaphore_wait(barrier, neighbours)
    both_ways(strip, "start")
    for d in range(1, GROUPS):
        send_block(d).start()

        @pl.when(is_middle(d))
        def _(d=d):
            send_far(d).start()


    @pl.when(jnp.logical_not(has_dn))
    def _():
        q[0] = jnp.zeros(q.shape[1:], F32)
        a_v[:, 0, DATA] = jnp.zeros((KA, ROWS, LANES), F32)
        a_str[0] = jnp.zeros((KA * OWN, LANES), F32)

    @pl.when(jnp.logical_not(has_up))
    def _():
        q[3] = jnp.zeros(q.shape[1:], F32)
        a_v[:, 3, DATA] = jnp.zeros((KA, ROWS, LANES), F32)
        a_str[3] = jnp.zeros((KA * OWN, LANES), F32)

    load_t.wait()
    load_c.wait()
    mode_i = tri_v[0:1, :]
    mode_j = tri_v[1:2, :]
    mode_k = tri_v[2:3, :]
    row_i = mode_i + ((mode_i * 274) >> 12)
    col_jk = mode_j + 113 * ((mode_j * 274) >> 12) + PAD * mode_k
    cf = cf_v[...].reshape(1, ENTRIES)
    cf_hi = cf.astype(BF16).astype(F32)
    cf_lo = cf - cf_hi
    is_row = lax.broadcasted_iota(jnp.int32, (WIDE, ENTRIES), 0) == row_i
    a_hot[0:WIDE, :] = jnp.where(is_row, cf_hi, 0.0).astype(BF16)
    a_hot[WIDE:, :] = jnp.where(is_row, cf_lo, 0.0).astype(BF16)

    def table(c, carry):
        cols = lax.broadcasted_iota(jnp.int32, (2 * WIDE, ENTRIES), 0) + c * (2 * WIDE)
        b_hot = jnp.where(cols == col_jk, 1.0, 0.0).astype(BF16)
        both = lax.dot_general(
            a_hot[...], b_hot, (((1,), (1,)), ((), ())), preferred_element_type=F32
        )
        coupled = both[:WIDE] + both[WIDE:]
        for part in range(2):
            one = coupled[:, part * WIDE : (part + 1) * WIDE]
            hi = one.astype(BF16)
            lo = (one - hi.astype(F32)).astype(BF16)
            for side in range(2):
                at = pl.multiple_of(c * 4 * WIDE + (2 * part + side) * WIDE, WIDE)
                w_mat[0:WIDE, pl.ds(at, WIDE)] = hi
                w_mat[WIDE:, pl.ds(at, WIDE)] = lo
        return carry

    def hand_on(part):
        for d in range(max(part * QUAD, 1), (part + 1) * QUAD):
            send_block(d).wait_recv()
        both_ways(functools.partial(halo, part), "start")
        rows_out(part, "start")

    lax.fori_loop(0, GROUPS // 4, table, 0)
    hand_on(0)
    lax.fori_loop(GROUPS // 4, GROUPS // 2, table, 0)
    arrived(strip)
    lane_ids = lax.broadcasted_iota(jnp.int32, (ROWS, LANES), 1)

    def beside(a):
        return (
            jnp.where(lane_ids > 0, pltpu.roll(a, 1, 1), 0.0),
            jnp.where(lane_ids < LANES - 1, pltpu.roll(a, LANES - 1, 1), 0.0),
        )

    for layer in range(LAYERS):
        a = a_str[layer + 1]
        sides = (a_str[layer], a_str[layer + 2], a_y[0, layer], a_y[1, layer]) + beside(a)
        for f, side in enumerate(sides):
            w_f[f, layer] = a + side
    hand_on(1)

    first_layer = lax.rem(s + 1, 2)

    def edge_arrived(part, layer):
        @pl.when(jnp.logical_and(layer == 0, has_dn))
        def _():
            halo(part, True).wait_recv()

        @pl.when(jnp.logical_and(layer == 1, has_up))
        def _():
            halo(part, False).wait_recv()

    def chunk(layer, d, carry):
        g = peer_from(d)
        rows = mode_rows(g)
        lanes = lax.broadcasted_iota(jnp.int32, (PAD, LANES), 1)
        for r in range(OWN):
            p = q[layer + 1, r + 1, rows, :]
            diffs = (
                p - q[layer, r + 1, rows, :],
                p - q[layer + 2, r + 1, rows, :],
                p - q[layer + 1, r, rows, :],
                p - q[layer + 1, r + 2, rows, :],
                p - jnp.where(lanes > 0, pltpu.roll(p, 1, 1), 0.0),
                p - jnp.where(lanes < LANES - 1, pltpu.roll(p, LANES - 1, 1), 0.0),
            )
            for k in range(KA):
                total = None
                for f in range(6):
                    term = w_f[f, layer, k * OWN + r : k * OWN + r + 1, :] * diffs[f]
                    total = term if total is None else total + term
                hi = total.astype(BF16)
                lo = (total - hi.astype(F32)).astype(BF16)
                for part, piece in enumerate((hi, lo)):
                    to = pl.multiple_of((2 * g + part) * WIDE + k * PAD, PAD)
                    m_buf[layer, pl.ds(to, PAD), r * LANES : (r + 1) * LANES] = piece
        return carry

    for part in range(HALVES):
        rows_in(part)
        depth = QUAD * 2 * WIDE
        half_first = lax.rem(half_of + part, HALVES) * depth
        deep = pl.ds(pl.multiple_of(half_first, depth), depth)
        for turn in range(LAYERS):
            layer = lax.rem(first_layer + turn, LAYERS)
            edge_arrived(part, layer)
            if part == HALVES - 1 and turn == LAYERS - 1:
                both_ways(perm_halo, "start")
            lax.fori_loop(part * QUAD, (part + 1) * QUAD, functools.partial(chunk, layer), 0)
            prod = jnp.dot(w_mat[:, deep], m_buf[layer, deep, :], preferred_element_type=F32)
            prod = prod[:WIDE] + prod[WIDE:]
            for r in range(OWN):
                for go in range(GROUPS):
                    to = (go, layer, slice(r * PAD, (r + 1) * PAD))
                    piece = prod[go * PAD : (go + 1) * PAD, r * LANES : (r + 1) * LANES]
                    r_out[to] = piece if part == 0 else r_out[to] + piece
            if part == HALVES - 1:
                for d in range(1, GROUPS):
                    send_back(d, layer).start()
                keep(layer).start()

    own_cols = pl.ds(pl.multiple_of(2 * WIDE * m, 2 * WIDE), WIDE)
    own_rows = w_mat[mode_rows(m), own_cols].astype(F32) + w_mat[
        pl.ds(pl.multiple_of(WIDE + m * PAD, PAD), PAD), own_cols
    ].astype(F32)
    sub = lax.broadcasted_iota(jnp.int32, (PAD, LANES), 0)
    lane = lax.broadcasted_iota(jnp.int32, (PAD, LANES), 1)
    for k in range(KA):
        picked = jnp.where(lane == sub + k * PAD, own_rows, 0.0)
        cdb[k] = jnp.broadcast_to(jnp.sum(picked, axis=1, keepdims=True), (PAD, LANES))

    arrived(perm_halo)

    def diagonal(k, carry):
        for layer in range(LAYERS):
            a = a_v[k, layer + 1, DATA]
            sides = (
                a_v[k, layer, DATA],
                a_v[k, layer + 2, DATA],
                a_v[k, layer + 1, EDGE - 1 : EDGE - 1 + ROWS],
                a_v[k, layer + 1, EDGE + 1 : EDGE + 1 + ROWS],
            ) + beside(a)
            total = 6.0 * a
            for side in sides:
                total = total + side
            dg[k, layer] = 0.5 * total
        return carry

    lax.fori_loop(0, KA, diagonal, 0)
    load_s.wait()

    def scales(j, carry):
        for layer in range(LAYERS):
            scale = jnp.zeros((ROWS, LANES), F32)
            for k in range(KA):
                scale = scale + cdb[k, pl.ds(j, 1), :] * dg[k, layer]
            at = pl.ds(pl.multiple_of(j * 64 + layer * ROWS, ROWS), ROWS)
            inv = relax_weight / scale
            inv_v[at, :] = inv
            base_v[at, :] = p_v[at, :] + s_v[at, :] * inv
        return carry

    lax.fori_loop(0, LOCAL, scales, 0)

    out_b = pltpu.make_async_copy(base_v, out_b_hbm, out_sem.at[0])
    out_i = pltpu.make_async_copy(inv_v, out_i_hbm, out_sem.at[1])
    out_b.start()
    out_i.start()

    for d in range(1, GROUPS):
        send_block(d).wait_send()
        for layer in range(LAYERS):
            send_back(d, layer).wait_send()

        @pl.when(is_middle(d))
        def _(d=d):
            send_far(d).wait_send()

    for part in range(HALVES):
        both_ways(functools.partial(halo, part), "wait_send")
        rows_out(part, "wait_send")
    both_ways(perm_halo, "wait_send")
    both_ways(strip, "wait_send")
    out_b.wait()
    out_i.wait()
    for layer in range(LAYERS):
        keep(layer).wait()
        for d in range(1, GROUPS):
            send_back(d, layer).wait_recv()


def finish(ret, base, inv, applied, relaxed):
    for j in range(LOCAL):
        for r8 in range(ROWS // 8):
            rows = slice(r8 * 8, r8 * 8 + 8)
            got = 0.5 * ret[0, pl.ds(r8 * 8 * PAD + j, 8, stride=PAD), :]
            applied[j, 0, rows, :] = got
            relaxed[j, 0, rows, :] = base[j, 0, rows, :] - got * inv[j, 0, rows, :]


def solution(mesh):
    space_count = mesh.shape["space"]
    cells = (LOCAL * LAYERS * ROWS, LANES)

    def on_device(pressure, source, perm_modes, triples, coeffs):
        returned, base, inv = pl.pallas_call(
            functools.partial(kernel, space_count),
            out_shape=[jax.ShapeDtypeStruct((LAYERS, ROWS * PAD, LANES), F32)]
            + [jax.ShapeDtypeStruct(cells, F32)] * 2,
            in_specs=[pl.BlockSpec(memory_space=pltpu.HBM)] * 5,
            out_specs=[pl.BlockSpec(memory_space=pl.ANY)] * 3,
            scratch_shapes=[
                pltpu.VMEM((PAD * LAYERS * ROWS, LANES), F32),
                pltpu.VMEM(cells, F32),
                pltpu.VMEM((KA, LAYERS + 2, ROWS + 2 * EDGE, LANES), F32),
                pltpu.VMEM((3, ENTRIES), jnp.int32),
                pltpu.VMEM((ENTRIES,), F32),
                pltpu.VMEM((LAYERS, ROWS + 2, PAD, LANES), F32),
                pltpu.VMEM((LAYERS + 2, OWN + 2, WIDE, LANES), F32),
                pltpu.VMEM((GROUPS, LAYERS, OWN * PAD, LANES), F32),
                pltpu.VMEM((2 * WIDE, GROUPS * 2 * WIDE), BF16),
                pltpu.VMEM((2 * WIDE, ENTRIES), BF16),
                pltpu.VMEM((LAYERS, GROUPS * 2 * WIDE, OWN * LANES), BF16),
                pltpu.VMEM((6, LAYERS, KA * OWN, LANES), F32),
                pltpu.VMEM((LAYERS + 2, KA * OWN, LANES), F32),
                pltpu.VMEM((2, LAYERS, KA * OWN, LANES), F32),
                pltpu.VMEM((KA, LAYERS, ROWS, LANES), F32),
                pltpu.VMEM((KA, PAD, LANES), F32),
                pltpu.VMEM(cells, F32),
                pltpu.VMEM(cells, F32),
                pltpu.SemaphoreType.DMA((5,)),
                pltpu.SemaphoreType.DMA((2,)),
            ]
            + [pltpu.SemaphoreType.DMA((GROUPS,))] * 2
            + [pltpu.SemaphoreType.DMA((HALVES,))] * 4
            + [pltpu.SemaphoreType.DMA((GROUPS,))] * 2
            + [pltpu.SemaphoreType.DMA((HALVES, 2))] * 2
            + [pltpu.SemaphoreType.DMA((2,))] * 4
            + [pltpu.SemaphoreType.DMA((LAYERS, GROUPS))] * 2
            + [pltpu.SemaphoreType.DMA((LAYERS,))],
            compiler_params=pltpu.CompilerParams(
                collective_id=0, has_side_effects=True, vmem_limit_bytes=60 * 1024 * 1024
            ),
        )(
            pressure.reshape(cells),
            source.reshape(cells),
            perm_modes,
            triples,
            coeffs,
        )
        whole = (LOCAL, LAYERS, ROWS, LANES)
        one_layer = pl.BlockSpec((LOCAL, 1, ROWS, LANES), lambda layer: (0, layer, 0, 0))
        return pl.pallas_call(
            finish,
            grid=(LAYERS,),
            out_shape=[jax.ShapeDtypeStruct(whole, F32)] * 2,
            in_specs=[
                pl.BlockSpec((1, ROWS * PAD, LANES), lambda layer: (layer, 0, 0)),
                one_layer,
                one_layer,
            ],
            out_specs=[one_layer] * 2,
            compiler_params=pltpu.CompilerParams(vmem_limit_bytes=60 * 1024 * 1024),
        )(returned, base.reshape(whole), inv.reshape(whole))

    return jax.shard_map(
        on_device,
        mesh=mesh,
        in_specs=(
            P("modes", "space", None, None),
            P("modes", "space", None, None),
            P(None, "space", None, None),
            P(),
            P(),
        ),
        out_specs=(P("modes", "space", None, None), P("modes", "space", None, None)),
        check_vma=False,
    )
```

```python
import functools

import jax
import jax.numpy as jnp
from jax import lax
from jax.experimental import pallas as pl
from jax.experimental.pallas import tpu as pltpu
from jax.sharding import PartitionSpec as P

KA = 8
GROUPS = 8
LOCAL = 15
PAD = 16
LAYERS = 2
ROWS = 32
LANES = 128
OWN = ROWS // GROUPS
ENTRIES = 2880
HALVES = 2
QUAD = GROUPS // HALVES
RUN = 8
EDGE = 8
DATA = slice(EDGE, EDGE + ROWS)
WIDE = GROUPS * PAD
relax_weight = 0.8

MESH = pl.DeviceIdType.MESH
F32 = jnp.float32
BF16 = jnp.bfloat16


def kernel(
    space_count,
    p_hbm,
    s_hbm,
    a_hbm,
    tri_hbm,
    cf_hbm,
    ret,
    out_b_hbm,
    out_i_hbm,
    p_v,
    s_v,
    a_v,
    tri_v,
    cf_v,
    t,
    q,
    r_out,
    w_mat,
    a_hot,
    m_buf,
    w_f,
    a_str,
    a_y,
    dg,
    cdb,
    inv_v,
    base_v,
    in_sem,
    out_sem,
    a2a_send,
    a2a_recv,
    low_send,
    low_recv,
    high_send,
    high_recv,
    far_send,
    far_recv,
    row_send,
    row_recv,
    perm_send,
    perm_recv,
    str_send,
    str_recv,
    ret_send,
    ret_recv,
    keep_sem,
    shared,
    share_send,
    share_recv,
):
    m = lax.axis_index("modes")
    s = lax.axis_index("space")
    has_dn = s > 0
    has_up = s < space_count - 1
    steps_up = jnp.logical_and(has_up, lax.rem(s, RUN) == RUN - 1)
    steps_dn = jnp.logical_and(has_dn, lax.rem(s, RUN) == 0)
    near_up = jnp.logical_and(has_up, jnp.logical_not(steps_up))
    near_dn = jnp.logical_and(has_dn, jnp.logical_not(steps_dn))

    half_of = m // QUAD

    def peer_to(d):
        return lax.rem(half_of + d // QUAD, HALVES) * QUAD + lax.rem(m + d, QUAD)

    def peer_from(d):
        return lax.rem(half_of + d // QUAD, HALVES) * QUAD + lax.rem(m + GROUPS - d, QUAD)

    def block_of(g):
        return jnp.where(g < QUAD, g, GROUPS + QUAD - 1 - g)

    block = block_of(m)
    turned = half_of == 1
    ahead = lax.rem(m, QUAD) < QUAD - 1
    behind = lax.rem(m, QUAD) > 0
    row_up, row_up_to = jnp.where(turned, 1, OWN), jnp.where(turned, OWN + 1, 0)
    row_dn, row_dn_to = jnp.where(turned, OWN, 1), jnp.where(turned, 0, OWN + 1)

    row_dn_to_far = jnp.where(turned, 0, OWN + 1)

    def far_row(b):
        return jnp.where(b == QUAD, QUAD * OWN, QUAD * OWN + 1)

    def mode_rows(g):
        return pl.ds(pl.multiple_of(g * PAD, PAD), PAD)

    barrier = pltpu.get_barrier_semaphore()
    for d in range(1, GROUPS):
        pl.semaphore_signal(barrier, inc=1, device_id=(peer_to(d), s), device_id_type=MESH)

    @pl.when(has_dn)
    def _():
        pl.semaphore_signal(barrier, inc=1, device_id=(m, s - 1), device_id_type=MESH)

    @pl.when(has_up)
    def _():
        pl.semaphore_signal(barrier, inc=1, device_id=(m, s + 1), device_id_type=MESH)

    load_p = pltpu.make_async_copy(p_hbm, p_v.at[0 : LOCAL * 64], in_sem.at[0])
    load_a = pltpu.make_async_copy(a_hbm, a_v.at[:, 1:3, DATA], in_sem.at[1])
    load_t = pltpu.make_async_copy(tri_hbm, tri_v, in_sem.at[2])
    load_c = pltpu.make_async_copy(cf_hbm, cf_v, in_sem.at[3])
    load_s = pltpu.make_async_copy(s_hbm, s_v, in_sem.at[4])
    for load in (load_p, load_a, load_t, load_c, load_s):
        load.start()

    p_v[LOCAL * 64 :, :] = jnp.zeros((64, LANES), F32)
    t[:, 0] = jnp.zeros((LAYERS, PAD, LANES), F32)
    t[:, ROWS + 1] = jnp.zeros((LAYERS, PAD, LANES), F32)
    load_p.wait()

    def stage(row, carry):
        for layer in range(LAYERS):
            for half in range(2):
                start = half * 8 * 64 + layer * ROWS + row
                t[layer, row + 1, half * 8 : half * 8 + 8, :] = p_v[pl.ds(start, 8, stride=64), :]
        return carry

    lax.fori_loop(0, ROWS, stage, 0)
    q[1:3, 1 : OWN + 1, mode_rows(m), :] = t[:, pl.ds(block * OWN + 1, OWN), :, :]

    @pl.when(jnp.logical_not(ahead))
    def _():
        q[1:3, pl.ds(row_dn_to_far, 1), mode_rows(m), :] = t[:, pl.ds(far_row(block), 1), :, :]

    @pl.when(jnp.logical_not(behind))
    def _():
        q[1:3, pl.ds(row_up_to, 1), :, :] = jnp.zeros((LAYERS, 1, WIDE, LANES), F32)

    def send_block(d):
        g = peer_to(d)
        return pltpu.make_async_remote_copy(
            src_ref=t.at[:, pl.ds(block_of(g) * OWN + 1, OWN)],
            dst_ref=q.at[1:3, 1 : OWN + 1, mode_rows(m), :],
            send_sem=a2a_send.at[d],
            recv_sem=a2a_recv.at[d],
            device_id=(g, s),
            device_id_type=MESH,
        )

    def send_far(d):
        g = peer_to(d)
        b = block_of(g)
        to = jnp.where(b == QUAD, 0, OWN + 1)
        return pltpu.make_async_remote_copy(
            src_ref=t.at[:, pl.ds(far_row(b), 1)],
            dst_ref=q.at[1:3, pl.ds(to, 1), mode_rows(m), :],
            send_sem=far_send.at[d],
            recv_sem=far_recv.at[d],
            device_id=(g, s),
            device_id_type=MESH,
        )

    def is_middle(d):
        b = block_of(peer_to(d))
        return jnp.logical_or(b == QUAD - 1, b == QUAD)

    def halves(part):
        first = lax.rem(half_of + part, HALVES) * QUAD * PAD
        return pl.ds(pl.multiple_of(first, QUAD * PAD), QUAD * PAD)

    def row_halo(part, up):
        src, dst = (row_up, row_up_to) if up else (row_dn, row_dn_to)
        return pltpu.make_async_remote_copy(
            src_ref=q.at[1:3, pl.ds(src, 1), halves(part), :],
            dst_ref=q.at[1:3, pl.ds(dst, 1), halves(part), :],
            send_sem=row_send.at[part, 1 if up else 0],
            recv_sem=row_recv.at[part, 1 if up else 0],
            device_id=(m + 1 if up else m - 1, s),
            device_id_type=MESH,
        )

    def rows_out(part, act):
        @pl.when(ahead)
        def _():
            getattr(row_halo(part, True), act)()

        @pl.when(behind)
        def _():
            getattr(row_halo(part, False), act)()

    def rows_in(part):
        @pl.when(behind)
        def _():
            row_halo(part, True).wait_recv()

        @pl.when(ahead)
        def _():
            row_halo(part, False).wait_recv()

        @pl.when(jnp.logical_not(ahead))
        def _():
            for d in range(max(part * QUAD, 1), (part + 1) * QUAD):
                send_far(d).wait_recv()

    def halo(part, up):
        rows = halves(part)
        sems = (high_send, high_recv) if up else (low_send, low_recv)
        return pltpu.make_async_remote_copy(
            src_ref=q.at[2 if up else 1, 1 : OWN + 1, rows, :],
            dst_ref=q.at[0 if up else 3, 1 : OWN + 1, rows, :],
            send_sem=sems[0].at[part],
            recv_sem=sems[1].at[part],
            device_id=(m, s + 1 if up else s - 1),
            device_id_type=MESH,
        )

    def perm_halo(up):
        return pltpu.make_async_remote_copy(
            src_ref=a_v.at[:, 2 if up else 1, DATA],
            dst_ref=a_v.at[:, 0 if up else 3, DATA],
            send_sem=perm_send.at[1 if up else 0],
            recv_sem=perm_recv.at[1 if up else 0],
            device_id=(m, s + 1 if up else s - 1),
            device_id_type=MESH,
        )

    def perm_out(act):
        @pl.when(near_up)
        def _():
            getattr(perm_halo(True), act)()

        @pl.when(near_dn)
        def _():
            getattr(perm_halo(False), act)()

    def perm_in():
        @pl.when(near_dn)
        def _():
            perm_halo(True).wait_recv()

        @pl.when(near_up)
        def _():
            perm_halo(False).wait_recv()

    def share(d, layer):
        return pltpu.make_async_remote_copy(
            src_ref=a_str.at[layer],
            dst_ref=shared.at[block],
            send_sem=share_send.at[d],
            recv_sem=share_recv.at[d],
            device_id=(peer_to(d), s),
            device_id_type=MESH,
        )

    def share_all(act):
        for there, layer in ((steps_dn, 0), (steps_up, 3)):

            @pl.when(there)
            def _(layer=layer):
                for d in range(1, GROUPS):
                    getattr(share(d, layer), act)()

    def share_in():
        for there, layer in ((steps_dn, 0), (steps_up, 3)):

            @pl.when(there)
            def _(layer=layer):
                shared[pl.ds(block, 1)] = a_str[layer : layer + 1]
                for d in range(1, GROUPS):
                    share(d, layer).wait_recv()
                for b in range(GROUPS):
                    for k in range(KA):
                        to = slice(EDGE + b * OWN, EDGE + (b + 1) * OWN)
                        a_v[k, layer, to, :] = shared[b, k * OWN : (k + 1) * OWN, :]

    def strip(up):
        return pltpu.make_async_remote_copy(
            src_ref=a_str.at[2 if up else 1],
            dst_ref=a_str.at[0 if up else 3],
            send_sem=str_send.at[1 if up else 0],
            recv_sem=str_recv.at[1 if up else 0],
            device_id=(m, s + 1 if up else s - 1),
            device_id_type=MESH,
        )

    own_rows_back = pl.ds(pl.multiple_of(block * OWN * PAD, OWN * PAD), OWN * PAD)

    def keep(layer):
        return pltpu.make_async_copy(
            r_out.at[m, layer], ret.at[layer, own_rows_back, :], keep_sem.at[layer]
        )

    def send_back(d, layer):
        g = peer_to(d)
        return pltpu.make_async_remote_copy(
            src_ref=r_out.at[g, layer],
            dst_ref=ret.at[layer, own_rows_back, :],
            send_sem=ret_send.at[layer, d],
            recv_sem=ret_recv.at[layer, d],
            device_id=(g, s),
            device_id_type=MESH,
        )

    def both_ways(make, act):
        @pl.when(has_up)
        def _():
            getattr(make(True), act)()

        @pl.when(has_dn)
        def _():
            getattr(make(False), act)()

    def arrived(make):
        @pl.when(has_dn)
        def _():
            make(True).wait_recv()

        @pl.when(has_up)
        def _():
            make(False).wait_recv()

    load_a.wait()
    for layer in range(LAYERS):
        a_v[:, layer + 1, 0:EDGE] = jnp.zeros((KA, EDGE, LANES), F32)
        a_v[:, layer + 1, EDGE + ROWS :] = jnp.zeros((KA, EDGE, LANES), F32)
        for k in range(KA):
            to = slice(k * OWN, (k + 1) * OWN)
            a_str[layer + 1, to, :] = a_v[k, layer + 1, pl.ds(EDGE + block * OWN, OWN), :]
            a_y[0, layer, to, :] = a_v[k, layer + 1, pl.ds(EDGE + block * OWN - 1, OWN), :]
            a_y[1, layer, to, :] = a_v[k, layer + 1, pl.ds(EDGE + block * OWN + 1, OWN), :]

    neighbours = GROUPS - 1 + has_dn.astype(jnp.int32) + has_up.astype(jnp.int32)
    pl.semaphore_wait(barrier, neighbours)
    both_ways(strip, "start")
    for d in range(1, GROUPS):
        send_block(d).start()

        @pl.when(is_middle(d))
        def _(d=d):
            send_far(d).start()


    @pl.when(jnp.logical_not(has_dn))
    def _():
        q[0] = jnp.zeros(q.shape[1:], F32)
        a_v[:, 0, DATA] = jnp.zeros((KA, ROWS, LANES), F32)
        a_str[0] = jnp.zeros((KA * OWN, LANES), F32)

    @pl.when(jnp.logical_not(has_up))
    def _():
        q[3] = jnp.zeros(q.shape[1:], F32)
        a_v[:, 3, DATA] = jnp.zeros((KA, ROWS, LANES), F32)
        a_str[3] = jnp.zeros((KA * OWN, LANES), F32)

    load_t.wait()
    load_c.wait()
    mode_i = tri_v[0:1, :]
    mode_j = tri_v[1:2, :]
    mode_k = tri_v[2:3, :]
    row_i = mode_i + ((mode_i * 274) >> 12)
    col_jk = mode_j + 113 * ((mode_j * 274) >> 12) + PAD * mode_k
    cf = cf_v[...].reshape(1, ENTRIES)
    cf_hi = cf.astype(BF16).astype(F32)
    cf_lo = cf - cf_hi
    is_row = lax.broadcasted_iota(jnp.int32, (WIDE, ENTRIES), 0) == row_i
    a_hot[0:WIDE, :] = jnp.where(is_row, cf_hi, 0.0).astype(BF16)
    a_hot[WIDE:, :] = jnp.where(is_row, cf_lo, 0.0).astype(BF16)

    def table(c, carry):
        cols = lax.broadcasted_iota(jnp.int32, (2 * WIDE, ENTRIES), 0) + c * (2 * WIDE)
        b_hot = jnp.where(cols == col_jk, 1.0, 0.0).astype(BF16)
        both = lax.dot_general(
            a_hot[...], b_hot, (((1,), (1,)), ((), ())), preferred_element_type=F32
        )
        coupled = both[:WIDE] + both[WIDE:]
        for part in range(2):
            one = coupled[:, part * WIDE : (part + 1) * WIDE]
            hi = one.astype(BF16)
            lo = (one - hi.astype(F32)).astype(BF16)
            for side in range(2):
                at = pl.multiple_of(c * 4 * WIDE + (2 * part + side) * WIDE, WIDE)
                w_mat[0:WIDE, pl.ds(at, WIDE)] = hi
                w_mat[WIDE:, pl.ds(at, WIDE)] = lo
        return carry

    def hand_on(part):
        for d in range(max(part * QUAD, 1), (part + 1) * QUAD):
            send_block(d).wait_recv()
        both_ways(functools.partial(halo, part), "start")
        rows_out(part, "start")

    lax.fori_loop(0, GROUPS // 4, table, 0)
    hand_on(0)
    lax.fori_loop(GROUPS // 4, GROUPS // 2, table, 0)
    arrived(strip)
    lane_ids = lax.broadcasted_iota(jnp.int32, (ROWS, LANES), 1)

    def beside(a):
        return (
            jnp.where(lane_ids > 0, pltpu.roll(a, 1, 1), 0.0),
            jnp.where(lane_ids < LANES - 1, pltpu.roll(a, LANES - 1, 1), 0.0),
        )

    for layer in range(LAYERS):
        a = a_str[layer + 1]
        sides = (a_str[layer], a_str[layer + 2], a_y[0, layer], a_y[1, layer]) + beside(a)
        for f, side in enumerate(sides):
            w_f[f, layer] = a + side
    hand_on(1)
    perm_out("start")
    share_all("start")

    first_layer = lax.rem(s + 1, 2)

    def edge_arrived(part, layer):
        @pl.when(jnp.logical_and(layer == 0, has_dn))
        def _():
            halo(part, True).wait_recv()

        @pl.when(jnp.logical_and(layer == 1, has_up))
        def _():
            halo(part, False).wait_recv()

    def chunk(layer, d, carry):
        g = peer_from(d)
        rows = mode_rows(g)
        lanes = lax.broadcasted_iota(jnp.int32, (PAD, LANES), 1)
        for r in range(OWN):
            p = q[layer + 1, r + 1, rows, :]
            diffs = (
                p - q[layer, r + 1, rows, :],
                p - q[layer + 2, r + 1, rows, :],
                p - q[layer + 1, r, rows, :],
                p - q[layer + 1, r + 2, rows, :],
                p - jnp.where(lanes > 0, pltpu.roll(p, 1, 1), 0.0),
                p - jnp.where(lanes < LANES - 1, pltpu.roll(p, LANES - 1, 1), 0.0),
            )
            for k in range(KA):
                total = None
                for f in range(6):
                    term = w_f[f, layer, k * OWN + r : k * OWN + r + 1, :] * diffs[f]
                    total = term if total is None else total + term
                hi = total.astype(BF16)
                lo = (total - hi.astype(F32)).astype(BF16)
                for part, piece in enumerate((hi, lo)):
                    to = pl.multiple_of((2 * g + part) * WIDE + k * PAD, PAD)
                    m_buf[layer, pl.ds(to, PAD), r * LANES : (r + 1) * LANES] = piece
        return carry

    for part in range(HALVES):
        rows_in(part)
        depth = QUAD * 2 * WIDE
        half_first = lax.rem(half_of + part, HALVES) * depth
        deep = pl.ds(pl.multiple_of(half_first, depth), depth)
        for turn in range(LAYERS):
            layer = lax.rem(first_layer + turn, LAYERS)
            edge_arrived(part, layer)
            lax.fori_loop(part * QUAD, (part + 1) * QUAD, functools.partial(chunk, layer), 0)
            prod = jnp.dot(w_mat[:, deep], m_buf[layer, deep, :], preferred_element_type=F32)
            prod = prod[:WIDE] + prod[WIDE:]
            for r in range(OWN):
                for go in range(GROUPS):
                    to = (go, layer, slice(r * PAD, (r + 1) * PAD))
                    piece = prod[go * PAD : (go + 1) * PAD, r * LANES : (r + 1) * LANES]
                    r_out[to] = piece if part == 0 else r_out[to] + piece
            if part == HALVES - 1:
                for d in range(1, GROUPS):
                    send_back(d, layer).start()
                keep(layer).start()

    own_cols = pl.ds(pl.multiple_of(2 * WIDE * m, 2 * WIDE), WIDE)
    own_rows = w_mat[mode_rows(m), own_cols].astype(F32) + w_mat[
        pl.ds(pl.multiple_of(WIDE + m * PAD, PAD), PAD), own_cols
    ].astype(F32)
    sub = lax.broadcasted_iota(jnp.int32, (PAD, LANES), 0)
    lane = lax.broadcasted_iota(jnp.int32, (PAD, LANES), 1)
    for k in range(KA):
        picked = jnp.where(lane == sub + k * PAD, own_rows, 0.0)
        cdb[k] = jnp.broadcast_to(jnp.sum(picked, axis=1, keepdims=True), (PAD, LANES))

    perm_in()
    share_in()

    def diagonal(k, carry):
        for layer in range(LAYERS):
            a = a_v[k, layer + 1, DATA]
            sides = (
                a_v[k, layer, DATA],
                a_v[k, layer + 2, DATA],
                a_v[k, layer + 1, EDGE - 1 : EDGE - 1 + ROWS],
                a_v[k, layer + 1, EDGE + 1 : EDGE + 1 + ROWS],
            ) + beside(a)
            total = 6.0 * a
            for side in sides:
                total = total + side
            dg[k, layer] = 0.5 * total
        return carry

    lax.fori_loop(0, KA, diagonal, 0)
    load_s.wait()

    def scales(j, carry):
        for layer in range(LAYERS):
            scale = jnp.zeros((ROWS, LANES), F32)
            for k in range(KA):
                scale = scale + cdb[k, pl.ds(j, 1), :] * dg[k, layer]
            at = pl.ds(pl.multiple_of(j * 64 + layer * ROWS, ROWS), ROWS)
            inv = relax_weight / scale
            inv_v[at, :] = inv
            base_v[at, :] = p_v[at, :] + s_v[at, :] * inv
        return carry

    lax.fori_loop(0, LOCAL, scales, 0)

    out_b = pltpu.make_async_copy(base_v, out_b_hbm, out_sem.at[0])
    out_i = pltpu.make_async_copy(inv_v, out_i_hbm, out_sem.at[1])
    out_b.start()
    out_i.start()

    for d in range(1, GROUPS):
        send_block(d).wait_send()
        for layer in range(LAYERS):
            send_back(d, layer).wait_send()

        @pl.when(is_middle(d))
        def _(d=d):
            send_far(d).wait_send()

    for part in range(HALVES):
        both_ways(functools.partial(halo, part), "wait_send")
        rows_out(part, "wait_send")
    perm_out("wait_send")
    share_all("wait_send")
    both_ways(strip, "wait_send")
    out_b.wait()
    out_i.wait()
    for layer in range(LAYERS):
        keep(layer).wait()
        for d in range(1, GROUPS):
            send_back(d, layer).wait_recv()


def finish(ret, base, inv, applied, relaxed):
    for j in range(LOCAL):
        for r8 in range(ROWS // 8):
            rows = slice(r8 * 8, r8 * 8 + 8)
            got = 0.5 * ret[0, pl.ds(r8 * 8 * PAD + j, 8, stride=PAD), :]
            applied[j, 0, rows, :] = got
            relaxed[j, 0, rows, :] = base[j, 0, rows, :] - got * inv[j, 0, rows, :]


def solution(mesh):
    space_count = mesh.shape["space"]
    cells = (LOCAL * LAYERS * ROWS, LANES)

    def on_device(pressure, source, perm_modes, triples, coeffs):
        returned, base, inv = pl.pallas_call(
            functools.partial(kernel, space_count),
            out_shape=[jax.ShapeDtypeStruct((LAYERS, ROWS * PAD, LANES), F32)]
            + [jax.ShapeDtypeStruct(cells, F32)] * 2,
            in_specs=[pl.BlockSpec(memory_space=pltpu.HBM)] * 5,
            out_specs=[pl.BlockSpec(memory_space=pl.ANY)] * 3,
            scratch_shapes=[
                pltpu.VMEM((PAD * LAYERS * ROWS, LANES), F32),
                pltpu.VMEM(cells, F32),
                pltpu.VMEM((KA, LAYERS + 2, ROWS + 2 * EDGE, LANES), F32),
                pltpu.VMEM((3, ENTRIES), jnp.int32),
                pltpu.VMEM((ENTRIES,), F32),
                pltpu.VMEM((LAYERS, ROWS + 2, PAD, LANES), F32),
                pltpu.VMEM((LAYERS + 2, OWN + 2, WIDE, LANES), F32),
                pltpu.VMEM((GROUPS, LAYERS, OWN * PAD, LANES), F32),
                pltpu.VMEM((2 * WIDE, GROUPS * 2 * WIDE), BF16),
                pltpu.VMEM((2 * WIDE, ENTRIES), BF16),
                pltpu.VMEM((LAYERS, GROUPS * 2 * WIDE, OWN * LANES), BF16),
                pltpu.VMEM((6, LAYERS, KA * OWN, LANES), F32),
                pltpu.VMEM((LAYERS + 2, KA * OWN, LANES), F32),
                pltpu.VMEM((2, LAYERS, KA * OWN, LANES), F32),
                pltpu.VMEM((KA, LAYERS, ROWS, LANES), F32),
                pltpu.VMEM((KA, PAD, LANES), F32),
                pltpu.VMEM(cells, F32),
                pltpu.VMEM(cells, F32),
                pltpu.SemaphoreType.DMA((5,)),
                pltpu.SemaphoreType.DMA((2,)),
            ]
            + [pltpu.SemaphoreType.DMA((GROUPS,))] * 2
            + [pltpu.SemaphoreType.DMA((HALVES,))] * 4
            + [pltpu.SemaphoreType.DMA((GROUPS,))] * 2
            + [pltpu.SemaphoreType.DMA((HALVES, 2))] * 2
            + [pltpu.SemaphoreType.DMA((2,))] * 4
            + [pltpu.SemaphoreType.DMA((LAYERS, GROUPS))] * 2
            + [pltpu.SemaphoreType.DMA((LAYERS,))]
            + [pltpu.VMEM((GROUPS, KA * OWN, LANES), F32)]
            + [pltpu.SemaphoreType.DMA((GROUPS,))] * 2,
            compiler_params=pltpu.CompilerParams(
                collective_id=0, has_side_effects=True, vmem_limit_bytes=60 * 1024 * 1024
            ),
        )(
            pressure.reshape(cells),
            source.reshape(cells),
            perm_modes,
            triples,
            coeffs,
        )
        whole = (LOCAL, LAYERS, ROWS, LANES)
        one_layer = pl.BlockSpec((LOCAL, 1, ROWS, LANES), lambda layer: (0, layer, 0, 0))
        return pl.pallas_call(
            finish,
            grid=(LAYERS,),
            out_shape=[jax.ShapeDtypeStruct(whole, F32)] * 2,
            in_specs=[
                pl.BlockSpec((1, ROWS * PAD, LANES), lambda layer: (layer, 0, 0)),
                one_layer,
                one_layer,
            ],
            out_specs=[one_layer] * 2,
            compiler_params=pltpu.CompilerParams(vmem_limit_bytes=60 * 1024 * 1024),
        )(returned, base.reshape(whole), inv.reshape(whole))

    return jax.shard_map(
        on_device,
        mesh=mesh,
        in_specs=(
            P("modes", "space", None, None),
            P("modes", "space", None, None),
            P(None, "space", None, None),
            P(),
            P(),
        ),
        out_specs=(P("modes", "space", None, None), P("modes", "space", None, None)),
        check_vma=False,
    )
```

```python
import functools

import jax
import jax.numpy as jnp
from jax import lax
from jax.experimental import pallas as pl
from jax.experimental.pallas import tpu as pltpu
from jax.sharding import PartitionSpec as P

KA = 8
GROUPS = 8
LOCAL = 15
PAD = 16
LAYERS = 2
ROWS = 32
LANES = 128
OWN = ROWS // GROUPS
ENTRIES = 2880
HALVES = 2
QUAD = GROUPS // HALVES
RUN = 8
EDGE = 8
DATA = slice(EDGE, EDGE + ROWS)
WIDE = GROUPS * PAD
relax_weight = 0.8

MESH = pl.DeviceIdType.MESH
F32 = jnp.float32
BF16 = jnp.bfloat16


def kernel(
    space_count,
    p_hbm,
    s_hbm,
    a_hbm,
    tri_hbm,
    cf_hbm,
    ret,
    out_b_hbm,
    out_i_hbm,
    p_v,
    s_v,
    a_v,
    tri_v,
    cf_v,
    t,
    q,
    r_out,
    w_mat,
    a_hot,
    m_buf,
    w_f,
    a_str,
    a_y,
    dg,
    cdb,
    inv_v,
    base_v,
    in_sem,
    out_sem,
    a2a_send,
    a2a_recv,
    low_send,
    low_recv,
    high_send,
    high_recv,
    far_send,
    far_recv,
    row_send,
    row_recv,
    perm_send,
    perm_recv,
    str_send,
    str_recv,
    ret_send,
    ret_recv,
    keep_sem,
    shared,
    share_send,
    share_recv,
):
    m = lax.axis_index("modes")
    s = lax.axis_index("space")
    has_dn = s > 0
    has_up = s < space_count - 1
    steps_up = jnp.logical_and(has_up, lax.rem(s, RUN) == RUN - 1)
    steps_dn = jnp.logical_and(has_dn, lax.rem(s, RUN) == 0)
    near_up = jnp.logical_and(has_up, jnp.logical_not(steps_up))
    near_dn = jnp.logical_and(has_dn, jnp.logical_not(steps_dn))

    half_of = m // QUAD

    def peer_to(d):
        return lax.rem(half_of + d // QUAD, HALVES) * QUAD + lax.rem(m + d, QUAD)

    def peer_from(d):
        return lax.rem(half_of + d // QUAD, HALVES) * QUAD + lax.rem(m + GROUPS - d, QUAD)

    def block_of(g):
        return jnp.where(g < QUAD, g, GROUPS + QUAD - 1 - g)

    block = block_of(m)
    turned = half_of == 1
    ahead = lax.rem(m, QUAD) < QUAD - 1
    behind = lax.rem(m, QUAD) > 0
    row_up, row_up_to = jnp.where(turned, 1, OWN), jnp.where(turned, OWN + 1, 0)
    row_dn, row_dn_to = jnp.where(turned, OWN, 1), jnp.where(turned, 0, OWN + 1)

    row_dn_to_far = jnp.where(turned, 0, OWN + 1)

    def far_row(b):
        return jnp.where(b == QUAD, QUAD * OWN, QUAD * OWN + 1)

    def mode_rows(g):
        return pl.ds(pl.multiple_of(g * PAD, PAD), PAD)

    barrier = pltpu.get_barrier_semaphore()
    for d in range(1, GROUPS):
        pl.semaphore_signal(barrier, inc=1, device_id=(peer_to(d), s), device_id_type=MESH)

    @pl.when(has_dn)
    def _():
        pl.semaphore_signal(barrier, inc=1, device_id=(m, s - 1), device_id_type=MESH)

    @pl.when(has_up)
    def _():
        pl.semaphore_signal(barrier, inc=1, device_id=(m, s + 1), device_id_type=MESH)

    load_p = pltpu.make_async_copy(p_hbm, p_v.at[0 : LOCAL * 64], in_sem.at[0])
    load_a = pltpu.make_async_copy(a_hbm, a_v.at[:, 1:3, DATA], in_sem.at[1])
    load_t = pltpu.make_async_copy(tri_hbm, tri_v, in_sem.at[2])
    load_c = pltpu.make_async_copy(cf_hbm, cf_v, in_sem.at[3])
    load_s = pltpu.make_async_copy(s_hbm, s_v, in_sem.at[4])
    for load in (load_p, load_a, load_t, load_c, load_s):
        load.start()

    p_v[LOCAL * 64 :, :] = jnp.zeros((64, LANES), F32)
    t[:, 0] = jnp.zeros((LAYERS, PAD, LANES), F32)
    t[:, ROWS + 1] = jnp.zeros((LAYERS, PAD, LANES), F32)
    load_p.wait()

    def stage(row, carry):
        for layer in range(LAYERS):
            for half in range(2):
                start = half * 8 * 64 + layer * ROWS + row
                t[layer, row + 1, half * 8 : half * 8 + 8, :] = p_v[pl.ds(start, 8, stride=64), :]
        return carry

    lax.fori_loop(0, ROWS, stage, 0)
    q[1:3, 1 : OWN + 1, mode_rows(m), :] = t[:, pl.ds(block * OWN + 1, OWN), :, :]

    @pl.when(jnp.logical_not(ahead))
    def _():
        q[1:3, pl.ds(row_dn_to_far, 1), mode_rows(m), :] = t[:, pl.ds(far_row(block), 1), :, :]

    @pl.when(jnp.logical_not(behind))
    def _():
        q[1:3, pl.ds(row_up_to, 1), :, :] = jnp.zeros((LAYERS, 1, WIDE, LANES), F32)

    def send_block(d):
        g = peer_to(d)
        return pltpu.make_async_remote_copy(
            src_ref=t.at[:, pl.ds(block_of(g) * OWN + 1, OWN)],
            dst_ref=q.at[1:3, 1 : OWN + 1, mode_rows(m), :],
            send_sem=a2a_send.at[d],
            recv_sem=a2a_recv.at[d],
            device_id=(g, s),
            device_id_type=MESH,
        )

    def send_far(d):
        g = peer_to(d)
        b = block_of(g)
        to = jnp.where(b == QUAD, 0, OWN + 1)
        return pltpu.make_async_remote_copy(
            src_ref=t.at[:, pl.ds(far_row(b), 1)],
            dst_ref=q.at[1:3, pl.ds(to, 1), mode_rows(m), :],
            send_sem=far_send.at[d],
            recv_sem=far_recv.at[d],
            device_id=(g, s),
            device_id_type=MESH,
        )

    def is_middle(d):
        b = block_of(peer_to(d))
        return jnp.logical_or(b == QUAD - 1, b == QUAD)

    def halves(part):
        first = lax.rem(half_of + part, HALVES) * QUAD * PAD
        return pl.ds(pl.multiple_of(first, QUAD * PAD), QUAD * PAD)

    def row_halo(part, up):
        src, dst = (row_up, row_up_to) if up else (row_dn, row_dn_to)
        return pltpu.make_async_remote_copy(
            src_ref=q.at[1:3, pl.ds(src, 1), halves(part), :],
            dst_ref=q.at[1:3, pl.ds(dst, 1), halves(part), :],
            send_sem=row_send.at[part, 1 if up else 0],
            recv_sem=row_recv.at[part, 1 if up else 0],
            device_id=(m + 1 if up else m - 1, s),
            device_id_type=MESH,
        )

    def rows_out(part, act):
        @pl.when(ahead)
        def _():
            getattr(row_halo(part, True), act)()

        @pl.when(behind)
        def _():
            getattr(row_halo(part, False), act)()

    def rows_in(part):
        @pl.when(behind)
        def _():
            row_halo(part, True).wait_recv()

        @pl.when(ahead)
        def _():
            row_halo(part, False).wait_recv()

        @pl.when(jnp.logical_not(ahead))
        def _():
            for d in range(max(part * QUAD, 1), (part + 1) * QUAD):
                send_far(d).wait_recv()

    def halo(part, up):
        rows = halves(part)
        sems = (high_send, high_recv) if up else (low_send, low_recv)
        return pltpu.make_async_remote_copy(
            src_ref=q.at[2 if up else 1, 1 : OWN + 1, rows, :],
            dst_ref=q.at[0 if up else 3, 1 : OWN + 1, rows, :],
            send_sem=sems[0].at[part],
            recv_sem=sems[1].at[part],
            device_id=(m, s + 1 if up else s - 1),
            device_id_type=MESH,
        )

    def perm_halo(up):
        return pltpu.make_async_remote_copy(
            src_ref=a_v.at[:, 2 if up else 1, DATA],
            dst_ref=a_v.at[:, 0 if up else 3, DATA],
            send_sem=perm_send.at[1 if up else 0],
            recv_sem=perm_recv.at[1 if up else 0],
            device_id=(m, s + 1 if up else s - 1),
            device_id_type=MESH,
        )

    def perm_out(act):
        @pl.when(near_up)
        def _():
            getattr(perm_halo(True), act)()

        @pl.when(near_dn)
        def _():
            getattr(perm_halo(False), act)()

    def perm_in():
        @pl.when(near_dn)
        def _():
            perm_halo(True).wait_recv()

        @pl.when(near_up)
        def _():
            perm_halo(False).wait_recv()

    def share(d, layer):
        return pltpu.make_async_remote_copy(
            src_ref=a_str.at[layer],
            dst_ref=shared.at[block],
            send_sem=share_send.at[d],
            recv_sem=share_recv.at[d],
            device_id=(peer_to(d), s),
            device_id_type=MESH,
        )

    def share_all(act):
        for there, layer in ((steps_dn, 0), (steps_up, 3)):

            @pl.when(there)
            def _(layer=layer):
                for d in range(1, GROUPS):
                    getattr(share(d, layer), act)()

    def share_in():
        for there, layer in ((steps_dn, 0), (steps_up, 3)):

            @pl.when(there)
            def _(layer=layer):
                shared[pl.ds(block, 1)] = a_str[layer : layer + 1]
                for d in range(1, GROUPS):
                    share(d, layer).wait_recv()
                for b in range(GROUPS):
                    for k in range(KA):
                        to = slice(EDGE + b * OWN, EDGE + (b + 1) * OWN)
                        a_v[k, layer, to, :] = shared[b, k * OWN : (k + 1) * OWN, :]

    def strip(up):
        return pltpu.make_async_remote_copy(
            src_ref=a_str.at[2 if up else 1],
            dst_ref=a_str.at[0 if up else 3],
            send_sem=str_send.at[1 if up else 0],
            recv_sem=str_recv.at[1 if up else 0],
            device_id=(m, s + 1 if up else s - 1),
            device_id_type=MESH,
        )

    own_rows_back = pl.ds(pl.multiple_of(block * OWN * PAD, OWN * PAD), OWN * PAD)

    def keep(layer):
        return pltpu.make_async_copy(
            r_out.at[m, layer], ret.at[layer, own_rows_back, :], keep_sem.at[layer]
        )

    def send_back(d, layer):
        g = peer_to(d)
        return pltpu.make_async_remote_copy(
            src_ref=r_out.at[g, layer],
            dst_ref=ret.at[layer, own_rows_back, :],
            send_sem=ret_send.at[layer, d],
            recv_sem=ret_recv.at[layer, d],
            device_id=(g, s),
            device_id_type=MESH,
        )

    def both_ways(make, act):
        @pl.when(has_up)
        def _():
            getattr(make(True), act)()

        @pl.when(has_dn)
        def _():
            getattr(make(False), act)()

    def arrived(make):
        @pl.when(has_dn)
        def _():
            make(True).wait_recv()

        @pl.when(has_up)
        def _():
            make(False).wait_recv()

    load_a.wait()
    for layer in range(LAYERS):
        a_v[:, layer + 1, 0:EDGE] = jnp.zeros((KA, EDGE, LANES), F32)
        a_v[:, layer + 1, EDGE + ROWS :] = jnp.zeros((KA, EDGE, LANES), F32)
        for k in range(KA):
            to = slice(k * OWN, (k + 1) * OWN)
            a_str[layer + 1, to, :] = a_v[k, layer + 1, pl.ds(EDGE + block * OWN, OWN), :]
            a_y[0, layer, to, :] = a_v[k, layer + 1, pl.ds(EDGE + block * OWN - 1, OWN), :]
            a_y[1, layer, to, :] = a_v[k, layer + 1, pl.ds(EDGE + block * OWN + 1, OWN), :]

    neighbours = GROUPS - 1 + has_dn.astype(jnp.int32) + has_up.astype(jnp.int32)
    pl.semaphore_wait(barrier, neighbours)
    both_ways(strip, "start")
    for d in range(1, GROUPS):
        send_block(d).start()

        @pl.when(is_middle(d))
        def _(d=d):
            send_far(d).start()


    @pl.when(jnp.logical_not(has_dn))
    def _():
        q[0] = jnp.zeros(q.shape[1:], F32)
        a_v[:, 0, DATA] = jnp.zeros((KA, ROWS, LANES), F32)
        a_str[0] = jnp.zeros((KA * OWN, LANES), F32)

    @pl.when(jnp.logical_not(has_up))
    def _():
        q[3] = jnp.zeros(q.shape[1:], F32)
        a_v[:, 3, DATA] = jnp.zeros((KA, ROWS, LANES), F32)
        a_str[3] = jnp.zeros((KA * OWN, LANES), F32)

    load_t.wait()
    load_c.wait()
    mode_i = tri_v[0:1, :]
    mode_j = tri_v[1:2, :]
    mode_k = tri_v[2:3, :]
    row_i = mode_i + ((mode_i * 274) >> 12)
    col_jk = mode_j + 113 * ((mode_j * 274) >> 12) + PAD * mode_k
    cf = cf_v[...].reshape(1, ENTRIES)
    cf_hi = cf.astype(BF16).astype(F32)
    cf_lo = cf - cf_hi
    is_row = lax.broadcasted_iota(jnp.int32, (WIDE, ENTRIES), 0) == row_i
    a_hot[0:WIDE, :] = jnp.where(is_row, cf_hi, 0.0).astype(BF16)
    a_hot[WIDE:, :] = jnp.where(is_row, cf_lo, 0.0).astype(BF16)

    def table(c, carry):
        cols = lax.broadcasted_iota(jnp.int32, (2 * WIDE, ENTRIES), 0) + c * (2 * WIDE)
        b_hot = jnp.where(cols == col_jk, 1.0, 0.0).astype(BF16)
        both = lax.dot_general(
            a_hot[...], b_hot, (((1,), (1,)), ((), ())), preferred_element_type=F32
        )
        coupled = both[:WIDE] + both[WIDE:]
        for part in range(2):
            one = coupled[:, part * WIDE : (part + 1) * WIDE]
            hi = one.astype(BF16)
            lo = (one - hi.astype(F32)).astype(BF16)
            for side in range(2):
                at = pl.multiple_of(c * 4 * WIDE + (2 * part + side) * WIDE, WIDE)
                w_mat[0:WIDE, pl.ds(at, WIDE)] = hi
                w_mat[WIDE:, pl.ds(at, WIDE)] = lo
        return carry

    def hand_on(part):
        for d in range(max(part * QUAD, 1), (part + 1) * QUAD):
            send_block(d).wait_recv()
        both_ways(functools.partial(halo, part), "start")
        rows_out(part, "start")

    lax.fori_loop(0, GROUPS // 4, table, 0)
    hand_on(0)
    lax.fori_loop(GROUPS // 4, GROUPS // 2, table, 0)
    arrived(strip)
    lane_ids = lax.broadcasted_iota(jnp.int32, (ROWS, LANES), 1)

    def beside(a):
        return (
            jnp.where(lane_ids > 0, pltpu.roll(a, 1, 1), 0.0),
            jnp.where(lane_ids < LANES - 1, pltpu.roll(a, LANES - 1, 1), 0.0),
        )

    for layer in range(LAYERS):
        a = a_str[layer + 1]
        sides = (a_str[layer], a_str[layer + 2], a_y[0, layer], a_y[1, layer]) + beside(a)
        for f, side in enumerate(sides):
            w = a + side
            for row in range(KA * OWN):
                w_f[f, layer, row] = jnp.broadcast_to(w[row : row + 1], (8, LANES))
    hand_on(1)
    perm_out("start")
    share_all("start")

    first_layer = lax.rem(s + 1, 2)

    def edge_arrived(part, layer):
        @pl.when(jnp.logical_and(layer == 0, has_dn))
        def _():
            halo(part, True).wait_recv()

        @pl.when(jnp.logical_and(layer == 1, has_up))
        def _():
            halo(part, False).wait_recv()

    def chunk(layer, d, carry):
        g = peer_from(d)
        rows = mode_rows(g)
        lanes = lax.broadcasted_iota(jnp.int32, (PAD, LANES), 1)
        for r in range(OWN):
            p = q[layer + 1, r + 1, rows, :]
            diffs = (
                p - q[layer, r + 1, rows, :],
                p - q[layer + 2, r + 1, rows, :],
                p - q[layer + 1, r, rows, :],
                p - q[layer + 1, r + 2, rows, :],
                p - jnp.where(lanes > 0, pltpu.roll(p, 1, 1), 0.0),
                p - jnp.where(lanes < LANES - 1, pltpu.roll(p, LANES - 1, 1), 0.0),
            )
            for k in range(KA):
                total = None
                for f in range(6):
                    w = w_f[f, layer, k * OWN + r]
                    term = jnp.concatenate([w, w], axis=0) * diffs[f]
                    total = term if total is None else total + term
                hi = total.astype(BF16)
                lo = (total - hi.astype(F32)).astype(BF16)
                for part, piece in enumerate((hi, lo)):
                    to = pl.multiple_of((2 * g + part) * WIDE + k * PAD, PAD)
                    m_buf[layer, pl.ds(to, PAD), r * LANES : (r + 1) * LANES] = piece
        return carry

    for part in range(HALVES):
        rows_in(part)
        depth = QUAD * 2 * WIDE
        half_first = lax.rem(half_of + part, HALVES) * depth
        deep = pl.ds(pl.multiple_of(half_first, depth), depth)
        for turn in range(LAYERS):
            layer = lax.rem(first_layer + turn, LAYERS)
            edge_arrived(part, layer)
            lax.fori_loop(part * QUAD, (part + 1) * QUAD, functools.partial(chunk, layer), 0)
            prod = jnp.dot(w_mat[:, deep], m_buf[layer, deep, :], preferred_element_type=F32)
            prod = prod[:WIDE] + prod[WIDE:]
            for r in range(OWN):
                for go in range(GROUPS):
                    to = (go, layer, slice(r * PAD, (r + 1) * PAD))
                    piece = prod[go * PAD : (go + 1) * PAD, r * LANES : (r + 1) * LANES]
                    r_out[to] = piece if part == 0 else r_out[to] + piece
            if part == HALVES - 1:
                for d in range(1, GROUPS):
                    send_back(d, layer).start()
                keep(layer).start()

    own_cols = pl.ds(pl.multiple_of(2 * WIDE * m, 2 * WIDE), WIDE)
    own_rows = w_mat[mode_rows(m), own_cols].astype(F32) + w_mat[
        pl.ds(pl.multiple_of(WIDE + m * PAD, PAD), PAD), own_cols
    ].astype(F32)
    sub = lax.broadcasted_iota(jnp.int32, (PAD, LANES), 0)
    lane = lax.broadcasted_iota(jnp.int32, (PAD, LANES), 1)
    for k in range(KA):
        picked = jnp.where(lane == sub + k * PAD, own_rows, 0.0)
        cdb[k] = jnp.broadcast_to(jnp.sum(picked, axis=1, keepdims=True), (PAD, LANES))

    perm_in()
    share_in()

    def diagonal(k, carry):
        for layer in range(LAYERS):
            a = a_v[k, layer + 1, DATA]
            sides = (
                a_v[k, layer, DATA],
                a_v[k, layer + 2, DATA],
                a_v[k, layer + 1, EDGE - 1 : EDGE - 1 + ROWS],
                a_v[k, layer + 1, EDGE + 1 : EDGE + 1 + ROWS],
            ) + beside(a)
            total = 6.0 * a
            for side in sides:
                total = total + side
            dg[k, layer] = 0.5 * total
        return carry

    lax.fori_loop(0, KA, diagonal, 0)
    load_s.wait()

    def scales(j, carry):
        for layer in range(LAYERS):
            scale = jnp.zeros((ROWS, LANES), F32)
            for k in range(KA):
                scale = scale + cdb[k, pl.ds(j, 1), :] * dg[k, layer]
            at = pl.ds(pl.multiple_of(j * 64 + layer * ROWS, ROWS), ROWS)
            inv = relax_weight / scale
            inv_v[at, :] = inv
            base_v[at, :] = p_v[at, :] + s_v[at, :] * inv
        return carry

    lax.fori_loop(0, LOCAL, scales, 0)

    out_b = pltpu.make_async_copy(base_v, out_b_hbm, out_sem.at[0])
    out_i = pltpu.make_async_copy(inv_v, out_i_hbm, out_sem.at[1])
    out_b.start()
    out_i.start()

    for d in range(1, GROUPS):
        send_block(d).wait_send()
        for layer in range(LAYERS):
            send_back(d, layer).wait_send()

        @pl.when(is_middle(d))
        def _(d=d):
            send_far(d).wait_send()

    for part in range(HALVES):
        both_ways(functools.partial(halo, part), "wait_send")
        rows_out(part, "wait_send")
    perm_out("wait_send")
    share_all("wait_send")
    both_ways(strip, "wait_send")
    out_b.wait()
    out_i.wait()
    for layer in range(LAYERS):
        keep(layer).wait()
        for d in range(1, GROUPS):
            send_back(d, layer).wait_recv()


def finish(ret, base, inv, applied, relaxed):
    for j in range(LOCAL):
        for r8 in range(ROWS // 8):
            rows = slice(r8 * 8, r8 * 8 + 8)
            got = 0.5 * ret[0, pl.ds(r8 * 8 * PAD + j, 8, stride=PAD), :]
            applied[j, 0, rows, :] = got
            relaxed[j, 0, rows, :] = base[j, 0, rows, :] - got * inv[j, 0, rows, :]


def solution(mesh):
    space_count = mesh.shape["space"]
    cells = (LOCAL * LAYERS * ROWS, LANES)

    def on_device(pressure, source, perm_modes, triples, coeffs):
        returned, base, inv = pl.pallas_call(
            functools.partial(kernel, space_count),
            out_shape=[jax.ShapeDtypeStruct((LAYERS, ROWS * PAD, LANES), F32)]
            + [jax.ShapeDtypeStruct(cells, F32)] * 2,
            in_specs=[pl.BlockSpec(memory_space=pltpu.HBM)] * 5,
            out_specs=[pl.BlockSpec(memory_space=pl.ANY)] * 3,
            scratch_shapes=[
                pltpu.VMEM((PAD * LAYERS * ROWS, LANES), F32),
                pltpu.VMEM(cells, F32),
                pltpu.VMEM((KA, LAYERS + 2, ROWS + 2 * EDGE, LANES), F32),
                pltpu.VMEM((3, ENTRIES), jnp.int32),
                pltpu.VMEM((ENTRIES,), F32),
                pltpu.VMEM((LAYERS, ROWS + 2, PAD, LANES), F32),
                pltpu.VMEM((LAYERS + 2, OWN + 2, WIDE, LANES), F32),
                pltpu.VMEM((GROUPS, LAYERS, OWN * PAD, LANES), F32),
                pltpu.VMEM((2 * WIDE, GROUPS * 2 * WIDE), BF16),
                pltpu.VMEM((2 * WIDE, ENTRIES), BF16),
                pltpu.VMEM((LAYERS, GROUPS * 2 * WIDE, OWN * LANES), BF16),
                pltpu.VMEM((6, LAYERS, KA * OWN, 8, LANES), F32),
                pltpu.VMEM((LAYERS + 2, KA * OWN, LANES), F32),
                pltpu.VMEM((2, LAYERS, KA * OWN, LANES), F32),
                pltpu.VMEM((KA, LAYERS, ROWS, LANES), F32),
                pltpu.VMEM((KA, PAD, LANES), F32),
                pltpu.VMEM(cells, F32),
                pltpu.VMEM(cells, F32),
                pltpu.SemaphoreType.DMA((5,)),
                pltpu.SemaphoreType.DMA((2,)),
            ]
            + [pltpu.SemaphoreType.DMA((GROUPS,))] * 2
            + [pltpu.SemaphoreType.DMA((HALVES,))] * 4
            + [pltpu.SemaphoreType.DMA((GROUPS,))] * 2
            + [pltpu.SemaphoreType.DMA((HALVES, 2))] * 2
            + [pltpu.SemaphoreType.DMA((2,))] * 4
            + [pltpu.SemaphoreType.DMA((LAYERS, GROUPS))] * 2
            + [pltpu.SemaphoreType.DMA((LAYERS,))]
            + [pltpu.VMEM((GROUPS, KA * OWN, LANES), F32)]
            + [pltpu.SemaphoreType.DMA((GROUPS,))] * 2,
            compiler_params=pltpu.CompilerParams(
                collective_id=0, has_side_effects=True, vmem_limit_bytes=60 * 1024 * 1024
            ),
        )(
            pressure.reshape(cells),
            source.reshape(cells),
            perm_modes,
            triples,
            coeffs,
        )
        whole = (LOCAL, LAYERS, ROWS, LANES)
        one_layer = pl.BlockSpec((LOCAL, 1, ROWS, LANES), lambda layer: (0, layer, 0, 0))
        return pl.pallas_call(
            finish,
            grid=(LAYERS,),
            out_shape=[jax.ShapeDtypeStruct(whole, F32)] * 2,
            in_specs=[
                pl.BlockSpec((1, ROWS * PAD, LANES), lambda layer: (layer, 0, 0)),
                one_layer,
                one_layer,
            ],
            out_specs=[one_layer] * 2,
            compiler_params=pltpu.CompilerParams(vmem_limit_bytes=60 * 1024 * 1024),
        )(returned, base.reshape(whole), inv.reshape(whole))

    return jax.shard_map(
        on_device,
        mesh=mesh,
        in_specs=(
            P("modes", "space", None, None),
            P("modes", "space", None, None),
            P(None, "space", None, None),
            P(),
            P(),
        ),
        out_specs=(P("modes", "space", None, None), P("modes", "space", None, None)),
        check_vma=False,
    )
```

```python
import functools

import jax
import jax.numpy as jnp
from jax import lax
from jax.experimental import pallas as pl
from jax.experimental.pallas import tpu as pltpu
from jax.sharding import PartitionSpec as P

KA = 8
GROUPS = 8
LOCAL = 15
PAD = 16
LAYERS = 2
ROWS = 32
LANES = 128
OWN = ROWS // GROUPS
ENTRIES = 2880
HALVES = 2
QUAD = GROUPS // HALVES
RUN = 8
EDGE = 8
DATA = slice(EDGE, EDGE + ROWS)
WIDE = GROUPS * PAD
relax_weight = 0.8

MESH = pl.DeviceIdType.MESH
F32 = jnp.float32
BF16 = jnp.bfloat16


def kernel(
    space_count,
    p_hbm,
    s_hbm,
    a_hbm,
    tri_hbm,
    cf_hbm,
    ret,
    out_b_hbm,
    out_i_hbm,
    p_v,
    s_v,
    a_v,
    tri_v,
    cf_v,
    t,
    q,
    r_out,
    w_mat,
    a_hot,
    m_buf,
    w_f,
    a_str,
    a_y,
    dg,
    cdb,
    inv_v,
    base_v,
    in_sem,
    out_sem,
    a2a_send,
    a2a_recv,
    low_send,
    low_recv,
    high_send,
    high_recv,
    far_send,
    far_recv,
    row_send,
    row_recv,
    perm_send,
    perm_recv,
    str_send,
    str_recv,
    ret_send,
    ret_recv,
    keep_sem,
    c_buf,
    swap_sem,
    shared,
    share_send,
    share_recv,
):
    m = lax.axis_index("modes")
    s = lax.axis_index("space")
    has_dn = s > 0
    has_up = s < space_count - 1
    steps_up = jnp.logical_and(has_up, lax.rem(s, RUN) == RUN - 1)
    steps_dn = jnp.logical_and(has_dn, lax.rem(s, RUN) == 0)
    near_up = jnp.logical_and(has_up, jnp.logical_not(steps_up))
    near_dn = jnp.logical_and(has_dn, jnp.logical_not(steps_dn))

    half_of = m // QUAD

    def peer_to(d):
        return lax.rem(half_of + d // QUAD, HALVES) * QUAD + lax.rem(m + d, QUAD)

    def peer_from(d):
        return lax.rem(half_of + d // QUAD, HALVES) * QUAD + lax.rem(m + GROUPS - d, QUAD)

    def block_of(g):
        return jnp.where(g < QUAD, g, GROUPS + QUAD - 1 - g)

    block = block_of(m)
    turned = half_of == 1
    ahead = lax.rem(m, QUAD) < QUAD - 1
    behind = lax.rem(m, QUAD) > 0
    row_up, row_up_to = jnp.where(turned, 1, OWN), jnp.where(turned, OWN + 1, 0)
    row_dn, row_dn_to = jnp.where(turned, OWN, 1), jnp.where(turned, 0, OWN + 1)

    row_dn_to_far = jnp.where(turned, 0, OWN + 1)

    def far_row(b):
        return jnp.where(b == QUAD, QUAD * OWN, QUAD * OWN + 1)

    def mode_rows(g):
        return pl.ds(pl.multiple_of(g * PAD, PAD), PAD)

    barrier = pltpu.get_barrier_semaphore()
    for d in range(1, GROUPS):
        pl.semaphore_signal(barrier, inc=1, device_id=(peer_to(d), s), device_id_type=MESH)

    @pl.when(has_dn)
    def _():
        pl.semaphore_signal(barrier, inc=1, device_id=(m, s - 1), device_id_type=MESH)

    @pl.when(has_up)
    def _():
        pl.semaphore_signal(barrier, inc=1, device_id=(m, s + 1), device_id_type=MESH)

    load_p = pltpu.make_async_copy(p_hbm, p_v.at[0 : LOCAL * 64], in_sem.at[0])
    load_a = pltpu.make_async_copy(a_hbm, a_v.at[:, 1:3, DATA], in_sem.at[1])
    load_t = pltpu.make_async_copy(tri_hbm, tri_v, in_sem.at[2])
    load_c = pltpu.make_async_copy(cf_hbm, cf_v, in_sem.at[3])
    load_s = pltpu.make_async_copy(s_hbm, s_v, in_sem.at[4])
    for load in (load_p, load_a, load_t, load_c, load_s):
        load.start()

    p_v[LOCAL * 64 :, :] = jnp.zeros((64, LANES), F32)
    t[:, 0] = jnp.zeros((LAYERS, PAD, LANES), F32)
    t[:, ROWS + 1] = jnp.zeros((LAYERS, PAD, LANES), F32)
    load_p.wait()

    def stage(row, carry):
        for layer in range(LAYERS):
            for half in range(2):
                start = half * 8 * 64 + layer * ROWS + row
                t[layer, row + 1, half * 8 : half * 8 + 8, :] = p_v[pl.ds(start, 8, stride=64), :]
        return carry

    lax.fori_loop(0, ROWS, stage, 0)
    q[1:3, 1 : OWN + 1, mode_rows(m), :] = t[:, pl.ds(block * OWN + 1, OWN), :, :]

    @pl.when(jnp.logical_not(ahead))
    def _():
        q[1:3, pl.ds(row_dn_to_far, 1), mode_rows(m), :] = t[:, pl.ds(far_row(block), 1), :, :]

    @pl.when(jnp.logical_not(behind))
    def _():
        q[1:3, pl.ds(row_up_to, 1), :, :] = jnp.zeros((LAYERS, 1, WIDE, LANES), F32)

    def send_block(d):
        g = peer_to(d)
        return pltpu.make_async_remote_copy(
            src_ref=t.at[:, pl.ds(block_of(g) * OWN + 1, OWN)],
            dst_ref=q.at[1:3, 1 : OWN + 1, mode_rows(m), :],
            send_sem=a2a_send.at[d],
            recv_sem=a2a_recv.at[d],
            device_id=(g, s),
            device_id_type=MESH,
        )

    def send_far(d):
        g = peer_to(d)
        b = block_of(g)
        to = jnp.where(b == QUAD, 0, OWN + 1)
        return pltpu.make_async_remote_copy(
            src_ref=t.at[:, pl.ds(far_row(b), 1)],
            dst_ref=q.at[1:3, pl.ds(to, 1), mode_rows(m), :],
            send_sem=far_send.at[d],
            recv_sem=far_recv.at[d],
            device_id=(g, s),
            device_id_type=MESH,
        )

    def is_middle(d):
        b = block_of(peer_to(d))
        return jnp.logical_or(b == QUAD - 1, b == QUAD)

    def halves(part):
        first = lax.rem(half_of + part, HALVES) * QUAD * PAD
        return pl.ds(pl.multiple_of(first, QUAD * PAD), QUAD * PAD)

    def row_halo(part, up):
        src, dst = (row_up, row_up_to) if up else (row_dn, row_dn_to)
        return pltpu.make_async_remote_copy(
            src_ref=q.at[1:3, pl.ds(src, 1), halves(part), :],
            dst_ref=q.at[1:3, pl.ds(dst, 1), halves(part), :],
            send_sem=row_send.at[part, 1 if up else 0],
            recv_sem=row_recv.at[part, 1 if up else 0],
            device_id=(m + 1 if up else m - 1, s),
            device_id_type=MESH,
        )

    def rows_out(part, act):
        @pl.when(ahead)
        def _():
            getattr(row_halo(part, True), act)()

        @pl.when(behind)
        def _():
            getattr(row_halo(part, False), act)()

    def rows_in(part):
        @pl.when(behind)
        def _():
            row_halo(part, True).wait_recv()

        @pl.when(ahead)
        def _():
            row_halo(part, False).wait_recv()

        @pl.when(jnp.logical_not(ahead))
        def _():
            for d in range(max(part * QUAD, 1), (part + 1) * QUAD):
                send_far(d).wait_recv()

    def halo(part, up):
        rows = halves(part)
        sems = (high_send, high_recv) if up else (low_send, low_recv)
        return pltpu.make_async_remote_copy(
            src_ref=q.at[2 if up else 1, 1 : OWN + 1, rows, :],
            dst_ref=q.at[0 if up else 3, 1 : OWN + 1, rows, :],
            send_sem=sems[0].at[part],
            recv_sem=sems[1].at[part],
            device_id=(m, s + 1 if up else s - 1),
            device_id_type=MESH,
        )

    def perm_halo(up):
        return pltpu.make_async_remote_copy(
            src_ref=a_v.at[:, 2 if up else 1, DATA],
            dst_ref=a_v.at[:, 0 if up else 3, DATA],
            send_sem=perm_send.at[1 if up else 0],
            recv_sem=perm_recv.at[1 if up else 0],
            device_id=(m, s + 1 if up else s - 1),
            device_id_type=MESH,
        )

    def perm_out(act):
        @pl.when(near_up)
        def _():
            getattr(perm_halo(True), act)()

        @pl.when(near_dn)
        def _():
            getattr(perm_halo(False), act)()

    def perm_in():
        @pl.when(near_dn)
        def _():
            perm_halo(True).wait_recv()

        @pl.when(near_up)
        def _():
            perm_halo(False).wait_recv()

    def share(d, layer):
        return pltpu.make_async_remote_copy(
            src_ref=a_str.at[layer],
            dst_ref=shared.at[block],
            send_sem=share_send.at[d],
            recv_sem=share_recv.at[d],
            device_id=(peer_to(d), s),
            device_id_type=MESH,
        )

    def share_all(act):
        for there, layer in ((steps_dn, 0), (steps_up, 3)):

            @pl.when(there)
            def _(layer=layer):
                for d in range(1, GROUPS):
                    getattr(share(d, layer), act)()

    def share_in():
        for there, layer in ((steps_dn, 0), (steps_up, 3)):

            @pl.when(there)
            def _(layer=layer):
                shared[pl.ds(block, 1)] = a_str[layer : layer + 1]
                for d in range(1, GROUPS):
                    share(d, layer).wait_recv()
                for b in range(GROUPS):
                    for k in range(KA):
                        to = slice(EDGE + b * OWN, EDGE + (b + 1) * OWN)
                        a_v[k, layer, to, :] = shared[b, k * OWN : (k + 1) * OWN, :]

    def strip(up):
        return pltpu.make_async_remote_copy(
            src_ref=a_str.at[2 if up else 1],
            dst_ref=a_str.at[0 if up else 3],
            send_sem=str_send.at[1 if up else 0],
            recv_sem=str_recv.at[1 if up else 0],
            device_id=(m, s + 1 if up else s - 1),
            device_id_type=MESH,
        )

    own_rows_back = pl.ds(pl.multiple_of(block * OWN * PAD, OWN * PAD), OWN * PAD)

    def keep(layer):
        return pltpu.make_async_copy(
            r_out.at[m, layer], ret.at[layer, own_rows_back, :], keep_sem.at[layer]
        )

    def send_back(d, layer):
        g = peer_to(d)
        return pltpu.make_async_remote_copy(
            src_ref=r_out.at[g, layer],
            dst_ref=ret.at[layer, own_rows_back, :],
            send_sem=ret_send.at[layer, d],
            recv_sem=ret_recv.at[layer, d],
            device_id=(g, s),
            device_id_type=MESH,
        )

    def both_ways(make, act):
        @pl.when(has_up)
        def _():
            getattr(make(True), act)()

        @pl.when(has_dn)
        def _():
            getattr(make(False), act)()

    def arrived(make):
        @pl.when(has_dn)
        def _():
            make(True).wait_recv()

        @pl.when(has_up)
        def _():
            make(False).wait_recv()

    load_a.wait()
    for layer in range(LAYERS):
        a_v[:, layer + 1, 0:EDGE] = jnp.zeros((KA, EDGE, LANES), F32)
        a_v[:, layer + 1, EDGE + ROWS :] = jnp.zeros((KA, EDGE, LANES), F32)
        for k in range(KA):
            to = slice(k * OWN, (k + 1) * OWN)
            a_str[layer + 1, to, :] = a_v[k, layer + 1, pl.ds(EDGE + block * OWN, OWN), :]
            a_y[0, layer, to, :] = a_v[k, layer + 1, pl.ds(EDGE + block * OWN - 1, OWN), :]
            a_y[1, layer, to, :] = a_v[k, layer + 1, pl.ds(EDGE + block * OWN + 1, OWN), :]

    neighbours = GROUPS - 1 + has_dn.astype(jnp.int32) + has_up.astype(jnp.int32)
    pl.semaphore_wait(barrier, neighbours)
    both_ways(strip, "start")
    for d in range(1, GROUPS):
        send_block(d).start()

        @pl.when(is_middle(d))
        def _(d=d):
            send_far(d).start()


    @pl.when(jnp.logical_not(has_dn))
    def _():
        q[0] = jnp.zeros(q.shape[1:], F32)
        a_v[:, 0, DATA] = jnp.zeros((KA, ROWS, LANES), F32)
        a_str[0] = jnp.zeros((KA * OWN, LANES), F32)

    @pl.when(jnp.logical_not(has_up))
    def _():
        q[3] = jnp.zeros(q.shape[1:], F32)
        a_v[:, 3, DATA] = jnp.zeros((KA, ROWS, LANES), F32)
        a_str[3] = jnp.zeros((KA * OWN, LANES), F32)

    load_t.wait()
    load_c.wait()
    mode_i = tri_v[0:1, :]
    mode_j = tri_v[1:2, :]
    mode_k = tri_v[2:3, :]
    row_i = mode_i + ((mode_i * 274) >> 12)
    col_jk = mode_j + 113 * ((mode_j * 274) >> 12) + PAD * mode_k
    cf = cf_v[...].reshape(1, ENTRIES)
    cf_hi = cf.astype(BF16).astype(F32)
    cf_lo = cf - cf_hi
    is_row = lax.broadcasted_iota(jnp.int32, (WIDE, ENTRIES), 0) == row_i
    a_hot[0:WIDE, :] = jnp.where(is_row, cf_hi, 0.0).astype(BF16)
    a_hot[WIDE:, :] = jnp.where(is_row, cf_lo, 0.0).astype(BF16)

    core = lax.rem(s, 2)
    my_half = pl.ds(core * 2, 2)
    swap = pltpu.make_async_remote_copy(
        src_ref=c_buf.at[my_half],
        dst_ref=c_buf.at[my_half],
        send_sem=swap_sem.at[0],
        recv_sem=swap_sem.at[1],
        device_id=(m, s + 1 - 2 * core),
        device_id_type=MESH,
    )

    def table(step, carry):
        c = core * 2 + step
        cols = lax.broadcasted_iota(jnp.int32, (2 * WIDE, ENTRIES), 0) + c * (2 * WIDE)
        b_hot = jnp.where(cols == col_jk, 1.0, 0.0).astype(BF16)
        both = lax.dot_general(
            a_hot[...], b_hot, (((1,), (1,)), ((), ())), preferred_element_type=F32
        )
        c_buf[c] = both[:WIDE] + both[WIDE:]
        return carry

    def place(first, step, carry):
        c = first + step
        for part in range(2):
            one = c_buf[c, :, part * WIDE : (part + 1) * WIDE]
            hi = one.astype(BF16)
            lo = (one - hi.astype(F32)).astype(BF16)
            for side in range(2):
                at = pl.multiple_of(c * 4 * WIDE + (2 * part + side) * WIDE, WIDE)
                w_mat[0:WIDE, pl.ds(at, WIDE)] = hi
                w_mat[WIDE:, pl.ds(at, WIDE)] = lo
        return carry

    def hand_on(part):
        for d in range(max(part * QUAD, 1), (part + 1) * QUAD):
            send_block(d).wait_recv()
        both_ways(functools.partial(halo, part), "start")
        rows_out(part, "start")

    lax.fori_loop(0, 1, table, 0)
    hand_on(0)
    lax.fori_loop(1, 2, table, 0)
    swap.start()
    arrived(strip)
    lane_ids = lax.broadcasted_iota(jnp.int32, (ROWS, LANES), 1)

    def beside(a):
        return (
            jnp.where(lane_ids > 0, pltpu.roll(a, 1, 1), 0.0),
            jnp.where(lane_ids < LANES - 1, pltpu.roll(a, LANES - 1, 1), 0.0),
        )

    for layer in range(LAYERS):
        a = a_str[layer + 1]
        sides = (a_str[layer], a_str[layer + 2], a_y[0, layer], a_y[1, layer]) + beside(a)
        for f, side in enumerate(sides):
            w_f[f, layer] = a + side
    hand_on(1)
    perm_out("start")
    share_all("start")
    lax.fori_loop(0, 2, functools.partial(place, core * 2), 0)

    first_layer = lax.rem(s + 1, 2)

    def edge_arrived(part, layer):
        @pl.when(jnp.logical_and(layer == 0, has_dn))
        def _():
            halo(part, True).wait_recv()

        @pl.when(jnp.logical_and(layer == 1, has_up))
        def _():
            halo(part, False).wait_recv()

    def chunk(layer, d, carry):
        g = peer_from(d)
        rows = mode_rows(g)
        lanes = lax.broadcasted_iota(jnp.int32, (PAD, LANES), 1)
        for r in range(OWN):
            p = q[layer + 1, r + 1, rows, :]
            diffs = (
                p - q[layer, r + 1, rows, :],
                p - q[layer + 2, r + 1, rows, :],
                p - q[layer + 1, r, rows, :],
                p - q[layer + 1, r + 2, rows, :],
                p - jnp.where(lanes > 0, pltpu.roll(p, 1, 1), 0.0),
                p - jnp.where(lanes < LANES - 1, pltpu.roll(p, LANES - 1, 1), 0.0),
            )
            for k in range(KA):
                total = None
                for f in range(6):
                    term = w_f[f, layer, k * OWN + r : k * OWN + r + 1, :] * diffs[f]
                    total = term if total is None else total + term
                hi = total.astype(BF16)
                lo = (total - hi.astype(F32)).astype(BF16)
                for part, piece in enumerate((hi, lo)):
                    to = pl.multiple_of((2 * g + part) * WIDE + k * PAD, PAD)
                    m_buf[layer, pl.ds(to, PAD), r * LANES : (r + 1) * LANES] = piece
        return carry

    for part in range(HALVES):
        rows_in(part)
        depth = QUAD * 2 * WIDE
        half_first = lax.rem(half_of + part, HALVES) * depth
        deep = pl.ds(pl.multiple_of(half_first, depth), depth)
        for turn in range(LAYERS):
            layer = lax.rem(first_layer + turn, LAYERS)
            edge_arrived(part, layer)
            lax.fori_loop(part * QUAD, (part + 1) * QUAD, functools.partial(chunk, layer), 0)
            if part == 0 and turn == 0:
                swap.wait_recv()
                lax.fori_loop(0, 2, functools.partial(place, 2 - core * 2), 0)
            prod = jnp.dot(w_mat[:, deep], m_buf[layer, deep, :], preferred_element_type=F32)
            prod = prod[:WIDE] + prod[WIDE:]
            for r in range(OWN):
                for go in range(GROUPS):
                    to = (go, layer, slice(r * PAD, (r + 1) * PAD))
                    piece = prod[go * PAD : (go + 1) * PAD, r * LANES : (r + 1) * LANES]
                    r_out[to] = piece if part == 0 else r_out[to] + piece
            if part == HALVES - 1:
                for d in range(1, GROUPS):
                    send_back(d, layer).start()
                keep(layer).start()

    own_cols = pl.ds(pl.multiple_of(2 * WIDE * m, 2 * WIDE), WIDE)
    own_rows = w_mat[mode_rows(m), own_cols].astype(F32) + w_mat[
        pl.ds(pl.multiple_of(WIDE + m * PAD, PAD), PAD), own_cols
    ].astype(F32)
    sub = lax.broadcasted_iota(jnp.int32, (PAD, LANES), 0)
    lane = lax.broadcasted_iota(jnp.int32, (PAD, LANES), 1)
    for k in range(KA):
        picked = jnp.where(lane == sub + k * PAD, own_rows, 0.0)
        cdb[k] = jnp.broadcast_to(jnp.sum(picked, axis=1, keepdims=True), (PAD, LANES))

    perm_in()
    share_in()

    def diagonal(k, carry):
        for layer in range(LAYERS):
            a = a_v[k, layer + 1, DATA]
            sides = (
                a_v[k, layer, DATA],
                a_v[k, layer + 2, DATA],
                a_v[k, layer + 1, EDGE - 1 : EDGE - 1 + ROWS],
                a_v[k, layer + 1, EDGE + 1 : EDGE + 1 + ROWS],
            ) + beside(a)
            total = 6.0 * a
            for side in sides:
                total = total + side
            dg[k, layer] = 0.5 * total
        return carry

    lax.fori_loop(0, KA, diagonal, 0)
    load_s.wait()

    def scales(j, carry):
        for layer in range(LAYERS):
            scale = jnp.zeros((ROWS, LANES), F32)
            for k in range(KA):
                scale = scale + cdb[k, pl.ds(j, 1), :] * dg[k, layer]
            at = pl.ds(pl.multiple_of(j * 64 + layer * ROWS, ROWS), ROWS)
            inv = relax_weight / scale
            inv_v[at, :] = inv
            base_v[at, :] = p_v[at, :] + s_v[at, :] * inv
        return carry

    lax.fori_loop(0, LOCAL, scales, 0)

    out_b = pltpu.make_async_copy(base_v, out_b_hbm, out_sem.at[0])
    out_i = pltpu.make_async_copy(inv_v, out_i_hbm, out_sem.at[1])
    out_b.start()
    out_i.start()

    for d in range(1, GROUPS):
        send_block(d).wait_send()
        for layer in range(LAYERS):
            send_back(d, layer).wait_send()

        @pl.when(is_middle(d))
        def _(d=d):
            send_far(d).wait_send()

    for part in range(HALVES):
        both_ways(functools.partial(halo, part), "wait_send")
        rows_out(part, "wait_send")
    swap.wait_send()
    perm_out("wait_send")
    share_all("wait_send")
    both_ways(strip, "wait_send")
    out_b.wait()
    out_i.wait()
    for layer in range(LAYERS):
        keep(layer).wait()
        for d in range(1, GROUPS):
            send_back(d, layer).wait_recv()


def finish(ret, base, inv, applied, relaxed):
    for j in range(LOCAL):
        for r8 in range(ROWS // 8):
            rows = slice(r8 * 8, r8 * 8 + 8)
            got = 0.5 * ret[0, pl.ds(r8 * 8 * PAD + j, 8, stride=PAD), :]
            applied[j, 0, rows, :] = got
            relaxed[j, 0, rows, :] = base[j, 0, rows, :] - got * inv[j, 0, rows, :]


def solution(mesh):
    space_count = mesh.shape["space"]
    cells = (LOCAL * LAYERS * ROWS, LANES)

    def on_device(pressure, source, perm_modes, triples, coeffs):
        returned, base, inv = pl.pallas_call(
            functools.partial(kernel, space_count),
            out_shape=[jax.ShapeDtypeStruct((LAYERS, ROWS * PAD, LANES), F32)]
            + [jax.ShapeDtypeStruct(cells, F32)] * 2,
            in_specs=[pl.BlockSpec(memory_space=pltpu.HBM)] * 5,
            out_specs=[pl.BlockSpec(memory_space=pl.ANY)] * 3,
            scratch_shapes=[
                pltpu.VMEM((PAD * LAYERS * ROWS, LANES), F32),
                pltpu.VMEM(cells, F32),
                pltpu.VMEM((KA, LAYERS + 2, ROWS + 2 * EDGE, LANES), F32),
                pltpu.VMEM((3, ENTRIES), jnp.int32),
                pltpu.VMEM((ENTRIES,), F32),
                pltpu.VMEM((LAYERS, ROWS + 2, PAD, LANES), F32),
                pltpu.VMEM((LAYERS + 2, OWN + 2, WIDE, LANES), F32),
                pltpu.VMEM((GROUPS, LAYERS, OWN * PAD, LANES), F32),
                pltpu.VMEM((2 * WIDE, GROUPS * 2 * WIDE), BF16),
                pltpu.VMEM((2 * WIDE, ENTRIES), BF16),
                pltpu.VMEM((LAYERS, GROUPS * 2 * WIDE, OWN * LANES), BF16),
                pltpu.VMEM((6, LAYERS, KA * OWN, LANES), F32),
                pltpu.VMEM((LAYERS + 2, KA * OWN, LANES), F32),
                pltpu.VMEM((2, LAYERS, KA * OWN, LANES), F32),
                pltpu.VMEM((KA, LAYERS, ROWS, LANES), F32),
                pltpu.VMEM((KA, PAD, LANES), F32),
                pltpu.VMEM(cells, F32),
                pltpu.VMEM(cells, F32),
                pltpu.SemaphoreType.DMA((5,)),
                pltpu.SemaphoreType.DMA((2,)),
            ]
            + [pltpu.SemaphoreType.DMA((GROUPS,))] * 2
            + [pltpu.SemaphoreType.DMA((HALVES,))] * 4
            + [pltpu.SemaphoreType.DMA((GROUPS,))] * 2
            + [pltpu.SemaphoreType.DMA((HALVES, 2))] * 2
            + [pltpu.SemaphoreType.DMA((2,))] * 4
            + [pltpu.SemaphoreType.DMA((LAYERS, GROUPS))] * 2
            + [pltpu.SemaphoreType.DMA((LAYERS,))]
            + [pltpu.VMEM((GROUPS // 2, WIDE, 2 * WIDE), F32), pltpu.SemaphoreType.DMA((2,))]
            + [pltpu.VMEM((GROUPS, KA * OWN, LANES), F32)]
            + [pltpu.SemaphoreType.DMA((GROUPS,))] * 2,
            compiler_params=pltpu.CompilerParams(
                collective_id=0, has_side_effects=True, vmem_limit_bytes=60 * 1024 * 1024
            ),
        )(
            pressure.reshape(cells),
            source.reshape(cells),
            perm_modes,
            triples,
            coeffs,
        )
        whole = (LOCAL, LAYERS, ROWS, LANES)
        one_layer = pl.BlockSpec((LOCAL, 1, ROWS, LANES), lambda layer: (0, layer, 0, 0))
        return pl.pallas_call(
            finish,
            grid=(LAYERS,),
            out_shape=[jax.ShapeDtypeStruct(whole, F32)] * 2,
            in_specs=[
                pl.BlockSpec((1, ROWS * PAD, LANES), lambda layer: (layer, 0, 0)),
                one_layer,
                one_layer,
            ],
            out_specs=[one_layer] * 2,
            compiler_params=pltpu.CompilerParams(vmem_limit_bytes=60 * 1024 * 1024),
        )(returned, base.reshape(whole), inv.reshape(whole))

    return jax.shard_map(
        on_device,
        mesh=mesh,
        in_specs=(
            P("modes", "space", None, None),
            P("modes", "space", None, None),
            P(None, "space", None, None),
            P(),
            P(),
        ),
        out_specs=(P("modes", "space", None, None), P("modes", "space", None, None)),
        check_vma=False,
    )
```

```python
import functools

import jax
import jax.numpy as jnp
from jax import lax
from jax.experimental import pallas as pl
from jax.experimental.pallas import tpu as pltpu
from jax.sharding import PartitionSpec as P

KA = 8
GROUPS = 8
LOCAL = 15
PAD = 16
LAYERS = 2
ROWS = 32
LANES = 128
OWN = ROWS // GROUPS
ENTRIES = 2880
HALVES = 2
QUAD = GROUPS // HALVES
RUN = 8
EDGE = 8
DATA = slice(EDGE, EDGE + ROWS)
WIDE = GROUPS * PAD
relax_weight = 0.8

MESH = pl.DeviceIdType.MESH
F32 = jnp.float32
BF16 = jnp.bfloat16


def kernel(
    space_count,
    p_hbm,
    s_hbm,
    a_hbm,
    tri_hbm,
    cf_hbm,
    ret,
    out_b_hbm,
    out_i_hbm,
    p_v,
    s_v,
    a_v,
    tri_v,
    cf_v,
    t,
    q,
    r_out,
    w_mat,
    a_hot,
    m_buf,
    w_f,
    a_str,
    a_y,
    dg,
    cdb,
    inv_v,
    base_v,
    in_sem,
    out_sem,
    a2a_send,
    a2a_recv,
    low_send,
    low_recv,
    high_send,
    high_recv,
    far_send,
    far_recv,
    row_send,
    row_recv,
    perm_send,
    perm_recv,
    str_send,
    str_recv,
    ret_send,
    ret_recv,
    keep_sem,
    shared,
    share_send,
    share_recv,
):
    m = lax.axis_index("modes")
    s = lax.axis_index("space")
    has_dn = s > 0
    has_up = s < space_count - 1
    steps_up = jnp.logical_and(has_up, lax.rem(s, RUN) == RUN - 1)
    steps_dn = jnp.logical_and(has_dn, lax.rem(s, RUN) == 0)
    near_up = jnp.logical_and(has_up, jnp.logical_not(steps_up))
    near_dn = jnp.logical_and(has_dn, jnp.logical_not(steps_dn))

    half_of = m // QUAD

    def peer_to(d):
        return lax.rem(half_of + d // QUAD, HALVES) * QUAD + lax.rem(m + d, QUAD)

    def peer_from(d):
        return lax.rem(half_of + d // QUAD, HALVES) * QUAD + lax.rem(m + GROUPS - d, QUAD)

    def block_of(g):
        return jnp.where(g < QUAD, g, GROUPS + QUAD - 1 - g)

    block = block_of(m)
    turned = half_of == 1
    ahead = lax.rem(m, QUAD) < QUAD - 1
    behind = lax.rem(m, QUAD) > 0
    row_up, row_up_to = jnp.where(turned, 1, OWN), jnp.where(turned, OWN + 1, 0)
    row_dn, row_dn_to = jnp.where(turned, OWN, 1), jnp.where(turned, 0, OWN + 1)

    row_dn_to_far = jnp.where(turned, 0, OWN + 1)

    def far_row(b):
        return jnp.where(b == QUAD, QUAD * OWN, QUAD * OWN + 1)

    def mode_rows(g):
        return pl.ds(pl.multiple_of(g * PAD, PAD), PAD)

    barrier = pltpu.get_barrier_semaphore()
    for d in range(1, GROUPS):
        pl.semaphore_signal(barrier, inc=1, device_id=(peer_to(d), s), device_id_type=MESH)

    @pl.when(has_dn)
    def _():
        pl.semaphore_signal(barrier, inc=1, device_id=(m, s - 1), device_id_type=MESH)

    @pl.when(has_up)
    def _():
        pl.semaphore_signal(barrier, inc=1, device_id=(m, s + 1), device_id_type=MESH)

    load_p = pltpu.make_async_copy(p_hbm, p_v.at[0 : LOCAL * 64], in_sem.at[0])
    load_a = pltpu.make_async_copy(a_hbm, a_v.at[:, 1:3, DATA], in_sem.at[1])
    load_t = pltpu.make_async_copy(tri_hbm, tri_v, in_sem.at[2])
    load_c = pltpu.make_async_copy(cf_hbm, cf_v, in_sem.at[3])
    load_s = pltpu.make_async_copy(s_hbm, s_v, in_sem.at[4])
    for load in (load_p, load_a, load_t, load_c, load_s):
        load.start()

    p_v[LOCAL * 64 :, :] = jnp.zeros((64, LANES), F32)
    t[:, 0] = jnp.zeros((LAYERS, PAD, LANES), F32)
    t[:, ROWS + 1] = jnp.zeros((LAYERS, PAD, LANES), F32)
    load_p.wait()

    def stage(row, carry):
        for layer in range(LAYERS):
            for half in range(2):
                start = half * 8 * 64 + layer * ROWS + row
                t[layer, row + 1, half * 8 : half * 8 + 8, :] = p_v[pl.ds(start, 8, stride=64), :]
        return carry

    lax.fori_loop(0, ROWS, stage, 0)
    q[1:3, 1 : OWN + 1, mode_rows(m), :] = t[:, pl.ds(block * OWN + 1, OWN), :, :]

    @pl.when(jnp.logical_not(ahead))
    def _():
        q[1:3, pl.ds(row_dn_to_far, 1), mode_rows(m), :] = t[:, pl.ds(far_row(block), 1), :, :]

    @pl.when(jnp.logical_not(behind))
    def _():
        q[1:3, pl.ds(row_up_to, 1), :, :] = jnp.zeros((LAYERS, 1, WIDE, LANES), F32)

    def send_block(d):
        g = peer_to(d)
        return pltpu.make_async_remote_copy(
            src_ref=t.at[:, pl.ds(block_of(g) * OWN + 1, OWN)],
            dst_ref=q.at[1:3, 1 : OWN + 1, mode_rows(m), :],
            send_sem=a2a_send.at[d],
            recv_sem=a2a_recv.at[d],
            device_id=(g, s),
            device_id_type=MESH,
        )

    def send_far(d):
        g = peer_to(d)
        b = block_of(g)
        to = jnp.where(b == QUAD, 0, OWN + 1)
        return pltpu.make_async_remote_copy(
            src_ref=t.at[:, pl.ds(far_row(b), 1)],
            dst_ref=q.at[1:3, pl.ds(to, 1), mode_rows(m), :],
            send_sem=far_send.at[d],
            recv_sem=far_recv.at[d],
            device_id=(g, s),
            device_id_type=MESH,
        )

    def is_middle(d):
        b = block_of(peer_to(d))
        return jnp.logical_or(b == QUAD - 1, b == QUAD)

    def halves(part):
        first = lax.rem(half_of + part, HALVES) * QUAD * PAD
        return pl.ds(pl.multiple_of(first, QUAD * PAD), QUAD * PAD)

    def row_halo(part, up):
        src, dst = (row_up, row_up_to) if up else (row_dn, row_dn_to)
        return pltpu.make_async_remote_copy(
            src_ref=q.at[1:3, pl.ds(src, 1), halves(part), :],
            dst_ref=q.at[1:3, pl.ds(dst, 1), halves(part), :],
            send_sem=row_send.at[part, 1 if up else 0],
            recv_sem=row_recv.at[part, 1 if up else 0],
            device_id=(m + 1 if up else m - 1, s),
            device_id_type=MESH,
        )

    def rows_out(part, act):
        @pl.when(ahead)
        def _():
            getattr(row_halo(part, True), act)()

        @pl.when(behind)
        def _():
            getattr(row_halo(part, False), act)()

    def rows_in(part):
        @pl.when(behind)
        def _():
            row_halo(part, True).wait_recv()

        @pl.when(ahead)
        def _():
            row_halo(part, False).wait_recv()

        @pl.when(jnp.logical_not(ahead))
        def _():
            for d in range(max(part * QUAD, 1), (part + 1) * QUAD):
                send_far(d).wait_recv()

    def halo(part, up):
        rows = halves(part)
        sems = (high_send, high_recv) if up else (low_send, low_recv)
        return pltpu.make_async_remote_copy(
            src_ref=q.at[2 if up else 1, 1 : OWN + 1, rows, :],
            dst_ref=q.at[0 if up else 3, 1 : OWN + 1, rows, :],
            send_sem=sems[0].at[part],
            recv_sem=sems[1].at[part],
            device_id=(m, s + 1 if up else s - 1),
            device_id_type=MESH,
        )

    def perm_halo(up):
        return pltpu.make_async_remote_copy(
            src_ref=a_v.at[:, 2 if up else 1, DATA],
            dst_ref=a_v.at[:, 0 if up else 3, DATA],
            send_sem=perm_send.at[1 if up else 0],
            recv_sem=perm_recv.at[1 if up else 0],
            device_id=(m, s + 1 if up else s - 1),
            device_id_type=MESH,
        )

    def perm_out(act):
        @pl.when(near_up)
        def _():
            getattr(perm_halo(True), act)()

        @pl.when(near_dn)
        def _():
            getattr(perm_halo(False), act)()

    def perm_in():
        @pl.when(near_dn)
        def _():
            perm_halo(True).wait_recv()

        @pl.when(near_up)
        def _():
            perm_halo(False).wait_recv()

    def share(d, layer):
        return pltpu.make_async_remote_copy(
            src_ref=a_str.at[layer],
            dst_ref=shared.at[block],
            send_sem=share_send.at[d],
            recv_sem=share_recv.at[d],
            device_id=(peer_to(d), s),
            device_id_type=MESH,
        )

    def share_all(act):
        for there, layer in ((steps_dn, 0), (steps_up, 3)):

            @pl.when(there)
            def _(layer=layer):
                for d in range(1, GROUPS):
                    getattr(share(d, layer), act)()

    def share_in():
        for there, layer in ((steps_dn, 0), (steps_up, 3)):

            @pl.when(there)
            def _(layer=layer):
                shared[pl.ds(block, 1)] = a_str[layer : layer + 1]
                for d in range(1, GROUPS):
                    share(d, layer).wait_recv()
                for b in range(GROUPS):
                    for k in range(KA):
                        to = slice(EDGE + b * OWN, EDGE + (b + 1) * OWN)
                        a_v[k, layer, to, :] = shared[b, k * OWN : (k + 1) * OWN, :]

    def strip(up):
        return pltpu.make_async_remote_copy(
            src_ref=a_str.at[2 if up else 1],
            dst_ref=a_str.at[0 if up else 3],
            send_sem=str_send.at[1 if up else 0],
            recv_sem=str_recv.at[1 if up else 0],
            device_id=(m, s + 1 if up else s - 1),
            device_id_type=MESH,
        )

    own_rows_back = pl.ds(pl.multiple_of(block * OWN * PAD, OWN * PAD), OWN * PAD)

    def keep(layer):
        return pltpu.make_async_copy(
            r_out.at[m, layer], ret.at[layer, own_rows_back, :], keep_sem.at[layer]
        )

    def send_back(d, layer):
        g = peer_to(d)
        return pltpu.make_async_remote_copy(
            src_ref=r_out.at[g, layer],
            dst_ref=ret.at[layer, own_rows_back, :],
            send_sem=ret_send.at[layer, d],
            recv_sem=ret_recv.at[layer, d],
            device_id=(g, s),
            device_id_type=MESH,
        )

    def both_ways(make, act):
        @pl.when(has_up)
        def _():
            getattr(make(True), act)()

        @pl.when(has_dn)
        def _():
            getattr(make(False), act)()

    def arrived(make):
        @pl.when(has_dn)
        def _():
            make(True).wait_recv()

        @pl.when(has_up)
        def _():
            make(False).wait_recv()

    neighbours = GROUPS - 1 + has_dn.astype(jnp.int32) + has_up.astype(jnp.int32)
    pl.semaphore_wait(barrier, neighbours)
    for d in range(1, GROUPS):
        send_block(d).start()

        @pl.when(is_middle(d))
        def _(d=d):
            send_far(d).start()


    load_a.wait()
    for layer in range(LAYERS):
        a_v[:, layer + 1, 0:EDGE] = jnp.zeros((KA, EDGE, LANES), F32)
        a_v[:, layer + 1, EDGE + ROWS :] = jnp.zeros((KA, EDGE, LANES), F32)
        for k in range(KA):
            to = slice(k * OWN, (k + 1) * OWN)
            a_str[layer + 1, to, :] = a_v[k, layer + 1, pl.ds(EDGE + block * OWN, OWN), :]
            a_y[0, layer, to, :] = a_v[k, layer + 1, pl.ds(EDGE + block * OWN - 1, OWN), :]
            a_y[1, layer, to, :] = a_v[k, layer + 1, pl.ds(EDGE + block * OWN + 1, OWN), :]
    both_ways(strip, "start")

    @pl.when(jnp.logical_not(has_dn))
    def _():
        q[0] = jnp.zeros(q.shape[1:], F32)
        a_v[:, 0, DATA] = jnp.zeros((KA, ROWS, LANES), F32)
        a_str[0] = jnp.zeros((KA * OWN, LANES), F32)

    @pl.when(jnp.logical_not(has_up))
    def _():
        q[3] = jnp.zeros(q.shape[1:], F32)
        a_v[:, 3, DATA] = jnp.zeros((KA, ROWS, LANES), F32)
        a_str[3] = jnp.zeros((KA * OWN, LANES), F32)

    load_t.wait()
    load_c.wait()
    mode_i = tri_v[0:1, :]
    mode_j = tri_v[1:2, :]
    mode_k = tri_v[2:3, :]
    row_i = mode_i + ((mode_i * 274) >> 12)
    col_jk = mode_j + 113 * ((mode_j * 274) >> 12) + PAD * mode_k
    cf = cf_v[...].reshape(1, ENTRIES)
    cf_hi = cf.astype(BF16).astype(F32)
    cf_lo = cf - cf_hi
    is_row = lax.broadcasted_iota(jnp.int32, (WIDE, ENTRIES), 0) == row_i
    a_hot[0:WIDE, :] = jnp.where(is_row, cf_hi, 0.0).astype(BF16)
    a_hot[WIDE:, :] = jnp.where(is_row, cf_lo, 0.0).astype(BF16)

    def table(c, carry):
        cols = lax.broadcasted_iota(jnp.int32, (2 * WIDE, ENTRIES), 0) + c * (2 * WIDE)
        b_hot = jnp.where(cols == col_jk, 1.0, 0.0).astype(BF16)
        both = lax.dot_general(
            a_hot[...], b_hot, (((1,), (1,)), ((), ())), preferred_element_type=F32
        )
        coupled = both[:WIDE] + both[WIDE:]
        for part in range(2):
            one = coupled[:, part * WIDE : (part + 1) * WIDE]
            hi = one.astype(BF16)
            lo = (one - hi.astype(F32)).astype(BF16)
            for side in range(2):
                at = pl.multiple_of(c * 4 * WIDE + (2 * part + side) * WIDE, WIDE)
                w_mat[0:WIDE, pl.ds(at, WIDE)] = hi
                w_mat[WIDE:, pl.ds(at, WIDE)] = lo
        return carry

    def hand_on(part):
        for d in range(max(part * QUAD, 1), (part + 1) * QUAD):
            send_block(d).wait_recv()
        both_ways(functools.partial(halo, part), "start")
        rows_out(part, "start")

    lax.fori_loop(0, GROUPS // 4, table, 0)
    hand_on(0)
    lax.fori_loop(GROUPS // 4, GROUPS // 2, table, 0)
    arrived(strip)
    lane_ids = lax.broadcasted_iota(jnp.int32, (ROWS, LANES), 1)

    def beside(a):
        return (
            jnp.where(lane_ids > 0, pltpu.roll(a, 1, 1), 0.0),
            jnp.where(lane_ids < LANES - 1, pltpu.roll(a, LANES - 1, 1), 0.0),
        )

    for layer in range(LAYERS):
        a = a_str[layer + 1]
        sides = (a_str[layer], a_str[layer + 2], a_y[0, layer], a_y[1, layer]) + beside(a)
        for f, side in enumerate(sides):
            w_f[f, layer] = a + side
    hand_on(1)
    perm_out("start")
    share_all("start")

    first_layer = lax.rem(s + 1, 2)

    def edge_arrived(part, layer):
        @pl.when(jnp.logical_and(layer == 0, has_dn))
        def _():
            halo(part, True).wait_recv()

        @pl.when(jnp.logical_and(layer == 1, has_up))
        def _():
            halo(part, False).wait_recv()

    def chunk(layer, d, carry):
        g = peer_from(d)
        rows = mode_rows(g)
        lanes = lax.broadcasted_iota(jnp.int32, (PAD, LANES), 1)
        for r in range(OWN):
            p = q[layer + 1, r + 1, rows, :]
            diffs = (
                p - q[layer, r + 1, rows, :],
                p - q[layer + 2, r + 1, rows, :],
                p - q[layer + 1, r, rows, :],
                p - q[layer + 1, r + 2, rows, :],
                p - jnp.where(lanes > 0, pltpu.roll(p, 1, 1), 0.0),
                p - jnp.where(lanes < LANES - 1, pltpu.roll(p, LANES - 1, 1), 0.0),
            )
            for k in range(KA):
                total = None
                for f in range(6):
                    term = w_f[f, layer, k * OWN + r : k * OWN + r + 1, :] * diffs[f]
                    total = term if total is None else total + term
                hi = total.astype(BF16)
                lo = (total - hi.astype(F32)).astype(BF16)
                for part, piece in enumerate((hi, lo)):
                    to = pl.multiple_of((2 * g + part) * WIDE + k * PAD, PAD)
                    m_buf[layer, pl.ds(to, PAD), r * LANES : (r + 1) * LANES] = piece
        return carry

    for part in range(HALVES):
        rows_in(part)
        depth = QUAD * 2 * WIDE
        half_first = lax.rem(half_of + part, HALVES) * depth
        deep = pl.ds(pl.multiple_of(half_first, depth), depth)
        for turn in range(LAYERS):
            layer = lax.rem(first_layer + turn, LAYERS)
            edge_arrived(part, layer)
            lax.fori_loop(part * QUAD, (part + 1) * QUAD, functools.partial(chunk, layer), 0)
            prod = jnp.dot(w_mat[:, deep], m_buf[layer, deep, :], preferred_element_type=F32)
            prod = prod[:WIDE] + prod[WIDE:]
            for r in range(OWN):
                for go in range(GROUPS):
                    to = (go, layer, slice(r * PAD, (r + 1) * PAD))
                    piece = prod[go * PAD : (go + 1) * PAD, r * LANES : (r + 1) * LANES]
                    r_out[to] = piece if part == 0 else r_out[to] + piece
            if part == HALVES - 1:
                for d in range(1, GROUPS):
                    send_back(d, layer).start()
                keep(layer).start()

    own_cols = pl.ds(pl.multiple_of(2 * WIDE * m, 2 * WIDE), WIDE)
    own_rows = w_mat[mode_rows(m), own_cols].astype(F32) + w_mat[
        pl.ds(pl.multiple_of(WIDE + m * PAD, PAD), PAD), own_cols
    ].astype(F32)
    sub = lax.broadcasted_iota(jnp.int32, (PAD, LANES), 0)
    lane = lax.broadcasted_iota(jnp.int32, (PAD, LANES), 1)
    for k in range(KA):
        picked = jnp.where(lane == sub + k * PAD, own_rows, 0.0)
        cdb[k] = jnp.broadcast_to(jnp.sum(picked, axis=1, keepdims=True), (PAD, LANES))

    perm_in()
    share_in()

    def diagonal(k, carry):
        for layer in range(LAYERS):
            a = a_v[k, layer + 1, DATA]
            sides = (
                a_v[k, layer, DATA],
                a_v[k, layer + 2, DATA],
                a_v[k, layer + 1, EDGE - 1 : EDGE - 1 + ROWS],
                a_v[k, layer + 1, EDGE + 1 : EDGE + 1 + ROWS],
            ) + beside(a)
            total = 6.0 * a
            for side in sides:
                total = total + side
            dg[k, layer] = 0.5 * total
        return carry

    lax.fori_loop(0, KA, diagonal, 0)
    load_s.wait()

    def scales(j, carry):
        for layer in range(LAYERS):
            scale = jnp.zeros((ROWS, LANES), F32)
            for k in range(KA):
                scale = scale + cdb[k, pl.ds(j, 1), :] * dg[k, layer]
            at = pl.ds(pl.multiple_of(j * 64 + layer * ROWS, ROWS), ROWS)
            inv = relax_weight / scale
            inv_v[at, :] = inv
            base_v[at, :] = p_v[at, :] + s_v[at, :] * inv
        return carry

    lax.fori_loop(0, LOCAL, scales, 0)

    out_b = pltpu.make_async_copy(base_v, out_b_hbm, out_sem.at[0])
    out_i = pltpu.make_async_copy(inv_v, out_i_hbm, out_sem.at[1])
    out_b.start()
    out_i.start()

    for d in range(1, GROUPS):
        send_block(d).wait_send()
        for layer in range(LAYERS):
            send_back(d, layer).wait_send()

        @pl.when(is_middle(d))
        def _(d=d):
            send_far(d).wait_send()

    for part in range(HALVES):
        both_ways(functools.partial(halo, part), "wait_send")
        rows_out(part, "wait_send")
    perm_out("wait_send")
    share_all("wait_send")
    both_ways(strip, "wait_send")
    out_b.wait()
    out_i.wait()
    for layer in range(LAYERS):
        keep(layer).wait()
        for d in range(1, GROUPS):
            send_back(d, layer).wait_recv()


def finish(ret, base, inv, applied, relaxed):
    for j in range(LOCAL):
        for r8 in range(ROWS // 8):
            rows = slice(r8 * 8, r8 * 8 + 8)
            got = 0.5 * ret[0, pl.ds(r8 * 8 * PAD + j, 8, stride=PAD), :]
            applied[j, 0, rows, :] = got
            relaxed[j, 0, rows, :] = base[j, 0, rows, :] - got * inv[j, 0, rows, :]


def solution(mesh):
    space_count = mesh.shape["space"]
    cells = (LOCAL * LAYERS * ROWS, LANES)

    def on_device(pressure, source, perm_modes, triples, coeffs):
        returned, base, inv = pl.pallas_call(
            functools.partial(kernel, space_count),
            out_shape=[jax.ShapeDtypeStruct((LAYERS, ROWS * PAD, LANES), F32)]
            + [jax.ShapeDtypeStruct(cells, F32)] * 2,
            in_specs=[pl.BlockSpec(memory_space=pltpu.HBM)] * 5,
            out_specs=[pl.BlockSpec(memory_space=pl.ANY)] * 3,
            scratch_shapes=[
                pltpu.VMEM((PAD * LAYERS * ROWS, LANES), F32),
                pltpu.VMEM(cells, F32),
                pltpu.VMEM((KA, LAYERS + 2, ROWS + 2 * EDGE, LANES), F32),
                pltpu.VMEM((3, ENTRIES), jnp.int32),
                pltpu.VMEM((ENTRIES,), F32),
                pltpu.VMEM((LAYERS, ROWS + 2, PAD, LANES), F32),
                pltpu.VMEM((LAYERS + 2, OWN + 2, WIDE, LANES), F32),
                pltpu.VMEM((GROUPS, LAYERS, OWN * PAD, LANES), F32),
                pltpu.VMEM((2 * WIDE, GROUPS * 2 * WIDE), BF16),
                pltpu.VMEM((2 * WIDE, ENTRIES), BF16),
                pltpu.VMEM((LAYERS, GROUPS * 2 * WIDE, OWN * LANES), BF16),
                pltpu.VMEM((6, LAYERS, KA * OWN, LANES), F32),
                pltpu.VMEM((LAYERS + 2, KA * OWN, LANES), F32),
                pltpu.VMEM((2, LAYERS, KA * OWN, LANES), F32),
                pltpu.VMEM((KA, LAYERS, ROWS, LANES), F32),
                pltpu.VMEM((KA, PAD, LANES), F32),
                pltpu.VMEM(cells, F32),
                pltpu.VMEM(cells, F32),
                pltpu.SemaphoreType.DMA((5,)),
                pltpu.SemaphoreType.DMA((2,)),
            ]
            + [pltpu.SemaphoreType.DMA((GROUPS,))] * 2
            + [pltpu.SemaphoreType.DMA((HALVES,))] * 4
            + [pltpu.SemaphoreType.DMA((GROUPS,))] * 2
            + [pltpu.SemaphoreType.DMA((HALVES, 2))] * 2
            + [pltpu.SemaphoreType.DMA((2,))] * 4
            + [pltpu.SemaphoreType.DMA((LAYERS, GROUPS))] * 2
            + [pltpu.SemaphoreType.DMA((LAYERS,))]
            + [pltpu.VMEM((GROUPS, KA * OWN, LANES), F32)]
            + [pltpu.SemaphoreType.DMA((GROUPS,))] * 2,
            compiler_params=pltpu.CompilerParams(
                collective_id=0, has_side_effects=True, vmem_limit_bytes=60 * 1024 * 1024
            ),
        )(
            pressure.reshape(cells),
            source.reshape(cells),
            perm_modes,
            triples,
            coeffs,
        )
        whole = (LOCAL, LAYERS, ROWS, LANES)
        one_layer = pl.BlockSpec((LOCAL, 1, ROWS, LANES), lambda layer: (0, layer, 0, 0))
        return pl.pallas_call(
            finish,
            grid=(LAYERS,),
            out_shape=[jax.ShapeDtypeStruct(whole, F32)] * 2,
            in_specs=[
                pl.BlockSpec((1, ROWS * PAD, LANES), lambda layer: (layer, 0, 0)),
                one_layer,
                one_layer,
            ],
            out_specs=[one_layer] * 2,
            compiler_params=pltpu.CompilerParams(vmem_limit_bytes=60 * 1024 * 1024),
        )(returned, base.reshape(whole), inv.reshape(whole))

    return jax.shard_map(
        on_device,
        mesh=mesh,
        in_specs=(
            P("modes", "space", None, None),
            P("modes", "space", None, None),
            P(None, "space", None, None),
            P(),
            P(),
        ),
        out_specs=(P("modes", "space", None, None), P("modes", "space", None, None)),
        check_vma=False,
    )
```
